32 devices in a mesh: grp: 8 (over y, x, core), blk: 4 (over z).
Axes of the slice: x: 2, y: 2, z: 4, core: 2. Of those that a mesh axis runs over, the one named last changes fastest.
Arguments:
- dual_populace: float32 [19, 64, 64, 128], P(None, 'grp', 'blk'), may hold values from -6 to 6
- forward_motion_vector: float32 [3, 64, 64, 128], P(None, 'grp', 'blk'), may hold values from -0.4 to 0.4
- forward_heat_level: float32 [64, 64, 128], P('grp', 'blk'), may hold values from 0.5 to 1.5
- objective_heat_gradient: float32 [64, 64, 128], P('grp', 'blk'), may hold values from -6 to 6
- liquid_indicator: int32 [64, 64, 128], P('grp', 'blk'), may hold values 0 or 1
- filter_span_group: int32 [64, 64, 128], P('grp', 'blk'), may hold values from 0 to 3
Outputs:
- adjoint_out: float32 [19, 64, 64, 128], P(None, 'grp', 'blk')
- filtered: float32 [64, 64, 128], P('grp', 'blk')
The draws below stay inside these ranges and needn't reach their ends.
All inputs are finite; a program needn't handle non-finite values. No bound on the sum of `liquid_indicator` on one device may be relied on, other than what follows from the above.
Results may differ from the reference program's by a relative error of at most 0.000031.
Values sent between devices are 32-bit elements; how exact they have to be, the bound alone decides.
No kernel may reach another device: no remote copies, remote signals or barrier semaphores. Data moves between devices by JAX's collectives and lax.ppermute only.
A program may use at most 64 MiB of HBM per device.

```python
import jax
import jax.numpy as jnp

POPS = 19
STEPS = 3
SWEEPS = 8
NODES_LEADING = 64
NODES_MIDDLING = 64
NODES_TRAILING = 128


def set_ends(array, rng, smallest, top_value):
    index_at = [jax.random.randint(jax.random.fold_in(rng, axis), (), 0, length) for axis, length in enumerate(array.shape)]
    main_axis = array.shape.index(max(array.shape))
    beside = index_at[:main_axis] + [(index_at[main_axis] + 1) % array.shape[main_axis]] + index_at[main_axis + 1:]
    return array.at[tuple(index_at)].set(smallest).at[tuple(beside)].set(top_value)


def steps_of(key, extent, split, least, high):
    loudness, own = 1.0, jax.random.fold_in(key, 6)
    for dim, parts in split:
        heights = jnp.exp(jax.random.uniform(jax.random.fold_in(own, dim), (parts,), jnp.float32, least / len(split), high / len(split)))
        loudness = loudness * jnp.repeat(heights, extent[dim] // parts).reshape([-1 if axis == dim else 1 for axis in range(len(extent))])
    return loudness


def normal_values(stream_key, extent, spread, reach, cuts=(), kind=jnp.bfloat16):
    result = jax.random.normal(stream_key, extent, jnp.float32) * spread
    if len(cuts) > 0:
        result = steps_of(stream_key, extent, cuts, -0.22, 0.18) * result
    return jnp.clip(result, min=-reach, max=reach).astype(kind)


def setup_inputs(seed: int = 0) -> dict:
    splits = jax.random.split(jax.random.key(seed), 7)
    return {
        "dual_populace": normal_values(splits[0], (POPS, NODES_LEADING, NODES_MIDDLING, NODES_TRAILING), 1.0, 6.0, ((1, 8), (2, 4)), jnp.float32),
        "forward_motion_vector": normal_values(splits[1], (3, NODES_LEADING, NODES_MIDDLING, NODES_TRAILING), 0.1, 0.4, ((1, 8), (2, 4)), jnp.float32),
        "forward_heat_level": jnp.clip(0.5 + 1.0 * jax.random.uniform(splits[2], (NODES_LEADING, NODES_MIDDLING, NODES_TRAILING), jnp.float32) ** steps_of(splits[2], (NODES_LEADING, NODES_MIDDLING, NODES_TRAILING), ((0, 8), (1, 4)), -0.2, 0.2), 0.5, 1.5),
        "objective_heat_gradient": normal_values(splits[3], (NODES_LEADING, NODES_MIDDLING, NODES_TRAILING), 1.0, 6.0, ((0, 8), (1, 4)), jnp.float32),
        "liquid_indicator": set_ends((jax.random.randint(splits[4], (NODES_LEADING, NODES_MIDDLING, NODES_TRAILING), 0, 4) < 3).astype(jnp.int32), jax.random.fold_in(splits[4], 1), 0, 1),
        "filter_span_group": set_ends(jax.random.randint(splits[5], (NODES_LEADING, NODES_MIDDLING, NODES_TRAILING), 0, 4), jax.random.fold_in(splits[5], 1), 0, 3).astype(jnp.int32),
    }


VELOCITIES = ((0, 0, 0), (1, 0, 0), (-1, 0, 0), (0, 1, 0), (0, -1, 0), (0, 0, 1), (0, 0, -1),
              (1, 1, 0), (-1, -1, 0), (1, -1, 0), (-1, 1, 0), (1, 0, 1), (-1, 0, -1), (1, 0, -1),
              (-1, 0, 1), (0, 1, 1), (0, -1, -1), (0, 1, -1), (0, -1, 1))
WEIGHTS = (1.0 / 3.0,) + (1.0 / 18.0,) * 6 + (1.0 / 36.0,) * 12


def collide(pulled, omega, vel_x, vel_y, vel_z, objective_heat_gradient):
    equilib = jnp.zeros_like(omega)
    average = jnp.zeros_like(omega)
    for population in range(19):
        cx, cy, cz = VELOCITIES[population]
        along = cx * vel_x + cy * vel_y + cz * vel_z
        equilib = equilib + WEIGHTS[population] * (1.0 + 3.0 * along) * pulled[population]
        average = average + WEIGHTS[population] * pulled[population]
    posts = [pulled[population] - omega * (pulled[population] - equilib) + WEIGHTS[population] * objective_heat_gradient
             for population in range(19)]
    return jnp.stack(posts), equilib - average


def pull_all(state):
    width_x, width_y, width_z = state.shape[1], state.shape[2], state.shape[3]
    padded = jnp.pad(state, ((0, 0), (1, 1), (1, 1), (1, 1)))
    pieces = []
    for population in range(19):
        cx, cy, cz = VELOCITIES[population]
        pieces.append(padded[population, 1 + cx:1 + cx + width_x, 1 + cy:1 + cy + width_y, 1 + cz:1 + cz + width_z])
    return jnp.stack(pieces)


def reference(dual_populace, forward_motion_vector, forward_heat_level, objective_heat_gradient, liquid_indicator, filter_span_group):
    fluid = liquid_indicator.astype(jnp.float32)
    moving = forward_motion_vector * fluid[None]
    omega = 0.9 + 0.7 * fluid
    state = dual_populace
    gradient_map = jnp.zeros_like(forward_heat_level)
    for number in range(STEPS):
        pulled = pull_all(state)
        state, correction_increment = collide(pulled, omega, moving[0], moving[1], moving[2], objective_heat_gradient)
        gradient_map = gradient_map + forward_heat_level * correction_increment
    radius_sq = 0.25 * jnp.power(4.0, filter_span_group.astype(jnp.float32))
    denom = 1.0 + 6.0 * radius_sq
    smooth = gradient_map
    for number in range(SWEEPS):
        padded = jnp.pad(smooth, 1)
        beside = padded[2:, 1:-1, 1:-1] + padded[:-2, 1:-1, 1:-1]
        beside = beside + padded[1:-1, 2:, 1:-1] + padded[1:-1, :-2, 1:-1]
        beside = beside + padded[1:-1, 1:-1, 2:] + padded[1:-1, 1:-1, :-2]
        smooth = (gradient_map + radius_sq * beside) / denom
    return state, smooth
```

```python
import functools

import jax
import jax.numpy as jnp
from jax import lax
from jax.experimental import pallas as pl
from jax.experimental.pallas import tpu as pltpu
from jax.sharding import PartitionSpec as P

SWEEPS = 8
REACH = 8

VELOCITIES = (
    (0, 0, 0),
    (1, 0, 0),
    (-1, 0, 0),
    (0, 1, 0),
    (0, -1, 0),
    (0, 0, 1),
    (0, 0, -1),
    (1, 1, 0),
    (-1, -1, 0),
    (1, -1, 0),
    (-1, 1, 0),
    (1, 0, 1),
    (-1, 0, -1),
    (1, 0, -1),
    (-1, 0, 1),
    (0, 1, 1),
    (0, -1, -1),
    (0, 1, -1),
    (0, -1, 1),
)
POPS = 19
SHARE = 1.0 / 36.0
MULTIPLE = (12.0,) + (2.0,) * 6 + (1.0,) * 12
RIGHT = tuple(i for i in range(POPS) if VELOCITIES[i][0] == 1)
LEFT = tuple(i for i in range(POPS) if VELOCITIES[i][0] == -1)
LEVEL = tuple(i for i in range(POPS) if VELOCITIES[i][0] == 0)
PAD = 8
FIRST = 5
EDGES = 19


def rim_entries(sign):
    entries = [(0, i, 1) for i in range(POPS)]
    entries += [(0, i, 2) for i in range(POPS) if VELOCITIES[i][1] != -sign]
    entries += [(0, i, 3) for i in range(POPS) if VELOCITIES[i][1] == sign]
    for distance in (1, 2):
        entries += [(1, i, distance) for i in range(3)]
        entries += [(2, 0, distance), (3, 0, distance)]
    return entries


def lane_pull(v, cz):
    if cz == 0:
        return v
    lanes = v.shape[-1]
    lane = lax.broadcasted_iota(jnp.int32, v.shape, 1)
    if cz == 1:
        return jnp.where(lane != lanes - 1, pltpu.roll(v, lanes - 1, 1), 0.0)
    return jnp.where(lane != 0, pltpu.roll(v, 1, 1), 0.0)


def total(terms):
    terms = [t for t in terms if t is not None]
    return functools.reduce(lambda a, b: a + b, terms) if terms else None


def scaled(v, factor):
    return None if v is None else factor * v


def negated(v):
    return None if v is None else -v


def moments(p):
    s, d = {}, {}
    for i in range(1, POPS, 2):
        a, b = p[i], p[i + 1]
        s[i] = total([a, b])
        d[i] = a - b if a is not None and b is not None else (a if b is None else negated(b))
    average = total(
        [scaled(p[0], 12.0), scaled(total([s[1], s[3], s[5]]), 2.0)] + [s[i] for i in (7, 9, 11, 13, 15, 17)]
    )
    along_x = total([scaled(d[1], 2.0), d[7], d[9], d[11], d[13]])
    along_y = total([scaled(d[3], 2.0), d[7], negated(d[9]), d[15], d[17]])
    along_z = total([scaled(d[5], 2.0), d[11], negated(d[13]), d[15], negated(d[17])])
    return average, (along_x, along_y, along_z)


def relaxed(p, u):
    average, along = moments(p)
    shift = total([u[k] * along[k] for k in range(3) if along[k] is not None])
    return shift, SHARE * average + shift


def pulled_from(read, pops):
    p = [None] * POPS
    for i in pops:
        p[i] = lane_pull(read(i), VELOCITIES[i][2])
    return p


def posts_of(p, keep, equilib, rate, source, pops):
    base = rate * equilib
    terms = {m: base + (source if m == 1.0 else m * source) for m in (12.0, 2.0, 1.0)}
    return {i: keep * p[i] + terms[MULTIPLE[i]] for i in pops}


def extend(x_size, y_size, dual, vel, grad, fluid, above, below, state, coef):
    pitch = y_size + 2 * PAD
    planes = x_size + 2
    lanes = dual.shape[-1]
    flat = state.reshape(state.shape[0] * pitch, lanes)

    def copy_own(i, _):
        for x in range(x_size):
            state[i * planes + x + 1, pl.ds(PAD, y_size), :] = dual[i * x_size + x]
        return 0

    lax.fori_loop(0, POPS, copy_own, 0)
    rows = {}
    for sign, ref in ((1, above), (-1, below)):
        for k, (kind, i, distance) in enumerate(rim_entries(sign)):
            at = PAD + (y_size - 1 + distance if sign == 1 else -distance)
            value = ref[pl.ds(k * x_size, x_size), :]
            if kind == 0:
                flat[pl.ds((i * planes + 1) * pitch + at, x_size, stride=pitch), :] = value
            else:
                rows[(kind, i, at)] = value
    coef_flat = coef.reshape(coef.shape[0] * pitch, lanes)

    def coefficients(there, ux, uy, uz, g):
        inside = there > 0.5
        wet = jnp.where(inside, there - 1.0, 0.0)
        keep = jnp.where(inside, 0.1 - 0.7 * wet, 0.0)
        rate = jnp.where(inside, 0.9 + 0.7 * wet, 0.0)
        scale = (3.0 * SHARE) * wet
        return keep, rate, scale * ux, scale * uy, scale * uz, SHARE * g

    def own_coefficients(x, _):
        there = fluid[x].astype(jnp.float32) + 1.0
        values = coefficients(there, vel[x], vel[x_size + x], vel[2 * x_size + x], grad[x])
        for n, value in enumerate(values):
            coef[n * x_size + x, pl.ds(PAD, y_size), :] = value
        return 0

    lax.fori_loop(0, x_size, own_coefficients, 0)
    for at in sorted({key[2] for key in rows}):
        values = coefficients(rows[(2, 0, at)], *(rows[(1, n, at)] for n in range(3)), rows[(3, 0, at)])
        for n, value in enumerate(values):
            coef_flat[pl.ds(n * x_size * pitch + at, x_size, stride=pitch), :] = value


def rim_kernel(x_size, y_size, dual, vel, grad, fluid, low, high):
    lanes = dual.shape[-1]
    flat = [ref.reshape(ref.shape[0] * y_size, lanes) for ref in (dual, vel, fluid, grad)]
    for sign, out in ((1, low), (-1, high)):
        for k, (kind, i, distance) in enumerate(rim_entries(sign)):
            row = distance - 1 if sign == 1 else y_size - distance
            value = flat[kind][pl.ds(i * x_size * y_size + row, x_size, stride=y_size), :]
            if kind == 2:
                value = value.astype(jnp.float32) + 1.0
            out[pl.ds(k * x_size, x_size), :] = value


def edge_kernel(x_size, y_size, dual, vel, grad, fluid, above, below, to_left, to_right, state, coef, near, far):
    extend(x_size, y_size, dual, vel, grad, fluid, above, below, state, coef)
    planes = x_size + 2
    window = y_size + 8
    groups = window // 8
    for out, plane, inward, pops in ((to_left, 0, 1, RIGHT), (to_right, x_size - 1, -1, LEFT)):
        known = pops + LEVEL

        def coefs(x, at):
            return [coef[n * x_size + x, pl.ds(at, 8), :] for n in range(6)]

        def read_state(x, at):
            def read(i):
                cx, cy, _ = VELOCITIES[i]
                return state[i * planes + x + 1 + cx, pl.ds(at + cy, 8), :]

            return read

        for j in range(groups):
            at = FIRST + 8 * j
            keep, rate, *u, source = coefs(plane, at)
            for n, i in enumerate(pops):
                out[pl.ds(n * window + 8 * j, 8), :] = state[i * planes + plane + 1, pl.ds(at, 8), :]
            for n, value in enumerate((rate, *u)):
                out[pl.ds((15 + n) * window + 8 * j, 8), :] = value
            p = pulled_from(read_state(plane, at), known)
            _, equilib = relaxed(p, u)
            posts = posts_of(p, keep, equilib, rate, source, known)
            for n, i in enumerate(pops):
                out[pl.ds((5 + n) * window + 8 * j, 8), :] = posts[i]
            for n, i in enumerate(LEVEL):
                near[n, pl.ds(at, 8), :] = posts[i]
            keep, rate, *u, source = coefs(plane + inward, at)
            p = pulled_from(read_state(plane + inward, at), range(POPS))
            _, equilib = relaxed(p, u)
            posts = posts_of(p, keep, equilib, rate, source, pops)
            for n, i in enumerate(pops):
                far[n, pl.ds(at, 8), :] = posts[i]
        for j in range(groups):
            at = FIRST + 8 * j
            keep, rate, *u, source = coefs(plane, at)

            def read(i):
                ref, n = (far, pops.index(i)) if i in pops else (near, LEVEL.index(i))
                return ref[n, pl.ds(at + VELOCITIES[i][1], 8), :]

            p = pulled_from(read, known)
            _, equilib = relaxed(p, u)
            posts = posts_of(p, keep, equilib, rate, source, pops)
            for n, i in enumerate(pops):
                out[pl.ds((10 + n) * window + 8 * j, 8), :] = posts[i]


def steps_kernel(
    x_size, y_size, dual, vel, grad, fluid, above, below, heat, span, from_right, from_left,
    adjoint, sens, state, later, coef, shifts, extra,
):
    extend(x_size, y_size, dual, vel, grad, fluid, above, below, state, coef)
    planes = x_size + 2
    window = y_size + 8
    groups = window // 8
    sides = ((from_right, x_size - 1, x_size + 1, RIGHT, LEFT), (from_left, 0, 0, LEFT, RIGHT))

    for ref, _, halo, pops, _ in sides:
        for n, i in enumerate(pops):
            for j in range(groups):
                state[i * planes + halo, pl.ds(FIRST + 8 * j, 8), :] = ref[pl.ds(n * window + 8 * j, 8), :]

    def read_from(source, x, at):
        def read(i):
            cx, cy, _ = VELOCITIES[i]
            return source[i * planes + x + 1 + cx, pl.ds(at + cy, 8), :]

        return read

    def step(number, source, target):
        def plane(x, _):
            for j in range(groups):
                at = FIRST + 8 * j
                keep, rate, *u, drive = [coef[n * x_size + x, pl.ds(at, 8), :] for n in range(6)]
                p = pulled_from(read_from(source, x, at), range(POPS))
                shift, equilib = relaxed(p, u)
                shifts[(number - 1) * x_size + x, pl.ds(at, 8), :] = shift
                posts = posts_of(p, keep, equilib, rate, drive, range(POPS))
                for i in range(POPS):
                    target[i * planes + x + 1, pl.ds(at, 8), :] = posts[i]
            return 0

        lax.fori_loop(0, x_size, plane, 0)
        for side, (ref, edge, halo, pops, back) in enumerate(sides):
            for j in range(groups):
                at = FIRST + 8 * j
                rate, *u = [ref[pl.ds((15 + n) * window + 8 * j, 8), :] for n in range(4)]

                def read(i):
                    cy = VELOCITIES[i][1]
                    if i in back:
                        return source[i * planes + edge + 1, pl.ds(at + cy, 8), :]
                    return extra[side, pl.ds(at + cy, 8), :]

                p = pulled_from(read, back if number == 1 else back + LEVEL)
                added = rate * relaxed(p, u)[1]
                if number == 1:
                    extra[side, pl.ds(at, 8), :] = added
                for n, i in enumerate(pops):
                    target[i * planes + halo, pl.ds(at, 8), :] = (
                        ref[pl.ds((5 * number + n) * window + 8 * j, 8), :] + added
                    )

    step(1, state, later)
    step(2, later, state)

    def last(x, _):
        for j in range(y_size // 8):
            at = PAD + 8 * j
            keep, rate, *u, drive = [coef[n * x_size + x, pl.ds(at, 8), :] for n in range(6)]
            p = pulled_from(read_from(state, x, at), range(POPS))
            shift, equilib = relaxed(p, u)
            posts = posts_of(p, keep, equilib, rate, drive, range(POPS))
            for i in range(POPS):
                adjoint[i * x_size + x, pl.ds(8 * j, 8), :] = posts[i]
            shift = shifts[x, pl.ds(at, 8), :] + shifts[x_size + x, pl.ds(at, 8), :] + shift
            sens[x, pl.ds(8 * j, 8), :] = heat[x, pl.ds(8 * j, 8), :] * shift
        sens[x_size + x] = span[x].astype(jnp.float32) + 1.0
        return 0

    lax.fori_loop(0, x_size, last, 0)


def band_kernel(x_size, y_size, own, left, right, low, high):
    for kind in range(2):
        for n, ref in enumerate((left, own, right)):
            for x in range(x_size):
                k = kind * 3 * x_size + n * x_size + x
                low[k] = ref[kind * x_size + x, pl.ds(0, REACH), :]
                high[k] = ref[kind * x_size + x, pl.ds(y_size - REACH, REACH), :]


def filter_kernel(x_size, y_size, own, left, right, above, below, filtered, first, second, given, beta):
    wide = 3 * x_size
    rows = y_size + 2 * REACH

    def prepare(n, ref):
        def plane(x, _):
            k = n * x_size + x
            parts = (
                (0, REACH, below[k], below[wide + k]),
                (REACH, y_size, ref[x], ref[x_size + x]),
                (REACH + y_size, REACH, above[k], above[wide + k]),
            )
            for start, count, s, there in parts:
                r2 = jnp.where(there < 1.5, 0.25, jnp.where(there < 2.5, 1.0, jnp.where(there < 3.5, 4.0, 16.0)))
                inverse = 1.0 / (1.0 + 6.0 * r2)
                first[k, pl.ds(PAD + start, count), :] = s
                given[k, pl.ds(start, count), :] = s * inverse
                beta[k, pl.ds(start, count), :] = jnp.where(there > 0.5, r2 * inverse, 0.0)
            return 0

        lax.fori_loop(0, x_size, plane, 0)

    for n, ref in enumerate((left, own, right)):
        prepare(n, ref)
    source, target = first, second
    for number in range(1, SWEEPS + 1):
        final = number == SWEEPS
        margin = SWEEPS - number

        def plane(x, _, source=source, target=target, final=final):
            for j in range(1, 1 + y_size // 8) if final else range(rows // 8):
                at = PAD + 8 * j
                middle = source[x, pl.ds(at, 8), :]
                beside = source[x + 1, pl.ds(at, 8), :] + source[x - 1, pl.ds(at, 8), :]
                beside = beside + source[x, pl.ds(at + 1, 8), :] + source[x, pl.ds(at - 1, 8), :]
                beside = beside + lane_pull(middle, 1) + lane_pull(middle, -1)
                value = given[x, pl.ds(8 * j, 8), :] + beta[x, pl.ds(8 * j, 8), :] * beside
                if final:
                    filtered[x - x_size, pl.ds(8 * j - REACH, 8), :] = value
                else:
                    target[x, pl.ds(at, 8), :] = value
            return 0

        lax.fori_loop(x_size - margin, 2 * x_size + margin, plane, 0)
        source, target = target, source


def call(kernel, outs, scratch, args, name):
    return pl.pallas_call(
        kernel,
        out_shape=[jax.ShapeDtypeStruct(shape, jnp.float32) for shape in outs],
        in_specs=[pl.BlockSpec(memory_space=pltpu.VMEM)] * len(args),
        out_specs=[pl.BlockSpec(memory_space=pltpu.VMEM)] * len(outs),
        scratch_shapes=[pltpu.VMEM(shape, jnp.float32) for shape in scratch],
        compiler_params=pltpu.CompilerParams(vmem_limit_bytes=32 * 1024 * 1024),
        name=name,
    )(*args)


def both_ways(axis, to_previous, to_next):
    size = lax.axis_size(axis)
    on = [(i, i + 1) for i in range(size - 1)]
    back = [(i + 1, i) for i in range(size - 1)]
    return lax.ppermute(to_previous, axis, back), lax.ppermute(to_next, axis, on)


def on_device(dual_populace, forward_motion_vector, forward_heat_level, objective_heat_gradient, liquid_indicator,
              filter_span_group):
    _, x_size, y_size, lanes = dual_populace.shape
    planes, pitch, window = x_size + 2, y_size + 2 * PAD, y_size + 8
    dual = dual_populace.reshape(POPS * x_size, y_size, lanes)
    vel = forward_motion_vector.reshape(3 * x_size, y_size, lanes)
    fields = (dual, vel, objective_heat_gradient, liquid_indicator)
    rim = (len(rim_entries(1)) * x_size, lanes)
    edge = (EDGES * window, lanes)
    state = (POPS * planes, pitch, lanes)
    coef = (6 * x_size, pitch, lanes)

    low, high = call(
        functools.partial(rim_kernel, x_size, y_size), [rim, rim], [], fields, "rim_rows"
    )
    above, below = both_ways("blk", low, high)
    to_left, to_right = call(
        functools.partial(edge_kernel, x_size, y_size),
        [edge, edge],
        [state, coef, (len(LEVEL), pitch, lanes), (len(RIGHT), pitch, lanes)],
        (*fields, above, below),
        "edge_planes",
    )
    from_right, from_left = both_ways("grp", to_left, to_right)
    adjoint, sens = call(
        functools.partial(steps_kernel, x_size, y_size),
        [(POPS * x_size, y_size, lanes), (2 * x_size, y_size, lanes)],
        [state, state, coef, (2 * x_size, pitch, lanes), (2, pitch, lanes)],
        (*fields, above, below, forward_heat_level, filter_span_group, from_right, from_left),
        "three_steps",
    )
    right, left = both_ways("grp", sens, sens)
    band = (6 * x_size, REACH, lanes)
    low, high = call(
        functools.partial(band_kernel, x_size, y_size), [band, band], [], (sens, left, right), "band_rows"
    )
    above, below = both_ways("blk", low, high)
    wide = 3 * x_size
    rows = y_size + 2 * REACH
    (filtered,) = call(
        functools.partial(filter_kernel, x_size, y_size),
        [(x_size, y_size, lanes)],
        [(wide, rows + 2 * PAD, lanes)] * 2 + [(wide, rows, lanes)] * 2,
        (sens, left, right, above, below),
        "eight_sweeps",
    )
    return adjoint.reshape(dual_populace.shape), filtered


def solution(mesh):
    in_specs = (
        P(None, "grp", "blk", None),
        P(None, "grp", "blk", None),
        P("grp", "blk", None),
        P("grp", "blk", None),
        P("grp", "blk", None),
        P("grp", "blk", None),
    )
    out_specs = (P(None, "grp", "blk", None), P("grp", "blk", None))
    return jax.shard_map(
        on_device, mesh=mesh, in_specs=in_specs, out_specs=out_specs, check_vma=False
    )
```

```python
import functools

import jax
import jax.numpy as jnp
from jax import lax
from jax.experimental import pallas as pl
from jax.experimental.pallas import tpu as pltpu
from jax.sharding import PartitionSpec as P

SWEEPS = 8
REACH = 8

VELOCITIES = (
    (0, 0, 0),
    (1, 0, 0),
    (-1, 0, 0),
    (0, 1, 0),
    (0, -1, 0),
    (0, 0, 1),
    (0, 0, -1),
    (1, 1, 0),
    (-1, -1, 0),
    (1, -1, 0),
    (-1, 1, 0),
    (1, 0, 1),
    (-1, 0, -1),
    (1, 0, -1),
    (-1, 0, 1),
    (0, 1, 1),
    (0, -1, -1),
    (0, 1, -1),
    (0, -1, 1),
)
POPS = 19
SHARE = 1.0 / 36.0
MULTIPLE = (12.0,) + (2.0,) * 6 + (1.0,) * 12
RIGHT = tuple(i for i in range(POPS) if VELOCITIES[i][0] == 1)
LEFT = tuple(i for i in range(POPS) if VELOCITIES[i][0] == -1)
LEVEL = tuple(i for i in range(POPS) if VELOCITIES[i][0] == 0)
PAD = 8
FIRST = 5
EDGES = 19


def rim_entries(sign):
    entries = [(0, i, 1) for i in range(POPS)]
    entries += [(0, i, 2) for i in range(POPS) if VELOCITIES[i][1] != -sign]
    entries += [(0, i, 3) for i in range(POPS) if VELOCITIES[i][1] == sign]
    for distance in (1, 2):
        entries += [(1, i, distance) for i in range(3)]
        entries += [(2, 0, distance), (3, 0, distance)]
    return entries


def lane_pull(v, cz):
    if cz == 0:
        return v
    lanes = v.shape[-1]
    lane = lax.broadcasted_iota(jnp.int32, v.shape, 1)
    if cz == 1:
        return jnp.where(lane != lanes - 1, pltpu.roll(v, lanes - 1, 1), 0.0)
    return jnp.where(lane != 0, pltpu.roll(v, 1, 1), 0.0)


def total(terms):
    terms = [t for t in terms if t is not None]
    return functools.reduce(lambda a, b: a + b, terms) if terms else None


def scaled(v, factor):
    return None if v is None else factor * v


def negated(v):
    return None if v is None else -v


def moments(p):
    s, d = {}, {}
    for i in range(1, POPS, 2):
        a, b = p[i], p[i + 1]
        s[i] = total([a, b])
        d[i] = a - b if a is not None and b is not None else (a if b is None else negated(b))
    average = total(
        [scaled(p[0], 12.0), scaled(total([s[1], s[3], s[5]]), 2.0)] + [s[i] for i in (7, 9, 11, 13, 15, 17)]
    )
    along_x = total([scaled(d[1], 2.0), d[7], d[9], d[11], d[13]])
    along_y = total([scaled(d[3], 2.0), d[7], negated(d[9]), d[15], d[17]])
    along_z = total([scaled(d[5], 2.0), d[11], negated(d[13]), d[15], negated(d[17])])
    return average, (along_x, along_y, along_z)


def relaxed(p, u):
    average, along = moments(p)
    shift = total([u[k] * along[k] for k in range(3) if along[k] is not None])
    return shift, SHARE * average + shift


def pulled_from(read, pops):
    p = [None] * POPS
    for i in pops:
        p[i] = lane_pull(read(i), VELOCITIES[i][2])
    return p


def posts_of(p, keep, equilib, rate, source, pops):
    base = rate * equilib
    terms = {m: base + (source if m == 1.0 else m * source) for m in (12.0, 2.0, 1.0)}
    return {i: keep * p[i] + terms[MULTIPLE[i]] for i in pops}


def extend(x_size, y_size, dual, vel, grad, fluid, above, below, state, coef):
    pitch = y_size + 2 * PAD
    planes = x_size + 2
    lanes = dual.shape[-1]
    flat = state.reshape(state.shape[0] * pitch, lanes)

    def copy_own(i, _):
        for x in range(x_size):
            state[i * planes + x + 1, pl.ds(PAD, y_size), :] = dual[i * x_size + x]
        return 0

    lax.fori_loop(0, POPS, copy_own, 0)
    rows = {}
    for sign, ref in ((1, above), (-1, below)):
        for k, (kind, i, distance) in enumerate(rim_entries(sign)):
            at = PAD + (y_size - 1 + distance if sign == 1 else -distance)
            value = ref[pl.ds(k * x_size, x_size), :]
            if kind == 0:
                flat[pl.ds((i * planes + 1) * pitch + at, x_size, stride=pitch), :] = value
            else:
                rows[(kind, i, at)] = value
    coef_flat = coef.reshape(coef.shape[0] * pitch, lanes)

    def coefficients(there, ux, uy, uz, g):
        inside = there > 0.5
        wet = jnp.where(inside, there - 1.0, 0.0)
        keep = jnp.where(inside, 0.1 - 0.7 * wet, 0.0)
        rate = jnp.where(inside, 0.9 + 0.7 * wet, 0.0)
        scale = (3.0 * SHARE) * wet
        return keep, rate, scale * ux, scale * uy, scale * uz, SHARE * g

    def own_coefficients(x, _):
        there = fluid[x].astype(jnp.float32) + 1.0
        values = coefficients(there, vel[x], vel[x_size + x], vel[2 * x_size + x], grad[x])
        for n, value in enumerate(values):
            coef[n * x_size + x, pl.ds(PAD, y_size), :] = value
        return 0

    lax.fori_loop(0, x_size, own_coefficients, 0)
    for at in sorted({key[2] for key in rows}):
        values = coefficients(rows[(2, 0, at)], *(rows[(1, n, at)] for n in range(3)), rows[(3, 0, at)])
        for n, value in enumerate(values):
            coef_flat[pl.ds(n * x_size * pitch + at, x_size, stride=pitch), :] = value


def rim_kernel(x_size, y_size, dual, vel, grad, fluid, low, high):
    lanes = dual.shape[-1]
    flat = [ref.reshape(ref.shape[0] * y_size, lanes) for ref in (dual, vel, fluid, grad)]
    for sign, out in ((1, low), (-1, high)):
        for k, (kind, i, distance) in enumerate(rim_entries(sign)):
            row = distance - 1 if sign == 1 else y_size - distance
            value = flat[kind][pl.ds(i * x_size * y_size + row, x_size, stride=y_size), :]
            if kind == 2:
                value = value.astype(jnp.float32) + 1.0
            out[pl.ds(k * x_size, x_size), :] = value


def edge_kernel(x_size, y_size, dual, vel, grad, fluid, above, below, to_left, to_right, state, coef, near, far):
    extend(x_size, y_size, dual, vel, grad, fluid, above, below, state, coef)
    planes = x_size + 2
    window = y_size + 8
    groups = window // 8
    for out, plane, inward, pops in ((to_left, 0, 1, RIGHT), (to_right, x_size - 1, -1, LEFT)):
        known = pops + LEVEL

        def coefs(x, at):
            return [coef[n * x_size + x, pl.ds(at, 8), :] for n in range(6)]

        def read_state(x, at):
            def read(i):
                cx, cy, _ = VELOCITIES[i]
                return state[i * planes + x + 1 + cx, pl.ds(at + cy, 8), :]

            return read

        for j in range(groups):
            at = FIRST + 8 * j
            keep, rate, *u, source = coefs(plane, at)
            for n, i in enumerate(pops):
                out[pl.ds(n * window + 8 * j, 8), :] = state[i * planes + plane + 1, pl.ds(at, 8), :]
            for n, value in enumerate((rate, *u)):
                out[pl.ds((15 + n) * window + 8 * j, 8), :] = value
            p = pulled_from(read_state(plane, at), known)
            _, equilib = relaxed(p, u)
            posts = posts_of(p, keep, equilib, rate, source, known)
            for n, i in enumerate(pops):
                out[pl.ds((5 + n) * window + 8 * j, 8), :] = posts[i]
            for n, i in enumerate(LEVEL):
                near[n, pl.ds(at, 8), :] = posts[i]
            keep, rate, *u, source = coefs(plane + inward, at)
            p = pulled_from(read_state(plane + inward, at), range(POPS))
            _, equilib = relaxed(p, u)
            posts = posts_of(p, keep, equilib, rate, source, pops)
            for n, i in enumerate(pops):
                far[n, pl.ds(at, 8), :] = posts[i]
        for j in range(groups):
            at = FIRST + 8 * j
            keep, rate, *u, source = coefs(plane, at)

            def read(i):
                ref, n = (far, pops.index(i)) if i in pops else (near, LEVEL.index(i))
                return ref[n, pl.ds(at + VELOCITIES[i][1], 8), :]

            p = pulled_from(read, known)
            _, equilib = relaxed(p, u)
            posts = posts_of(p, keep, equilib, rate, source, pops)
            for n, i in enumerate(pops):
                out[pl.ds((10 + n) * window + 8 * j, 8), :] = posts[i]


def steps_kernel(
    x_size, y_size, dual, vel, grad, fluid, above, below, heat, span, from_right, from_left,
    adjoint, sens, state, later, coef, shifts, extra,
):
    extend(x_size, y_size, dual, vel, grad, fluid, above, below, state, coef)
    planes = x_size + 2
    window = y_size + 8
    groups = window // 8
    sides = ((from_right, x_size - 1, x_size + 1, RIGHT, LEFT), (from_left, 0, 0, LEFT, RIGHT))

    for ref, _, halo, pops, _ in sides:
        for n, i in enumerate(pops):
            for j in range(groups):
                state[i * planes + halo, pl.ds(FIRST + 8 * j, 8), :] = ref[pl.ds(n * window + 8 * j, 8), :]

    def read_from(source, x, at):
        def read(i):
            cx, cy, _ = VELOCITIES[i]
            return source[i * planes + x + 1 + cx, pl.ds(at + cy, 8), :]

        return read

    def step(number, source, target):
        def plane(x, _):
            for j in range(groups):
                at = FIRST + 8 * j
                keep, rate, *u, drive = [coef[n * x_size + x, pl.ds(at, 8), :] for n in range(6)]
                p = pulled_from(read_from(source, x, at), range(POPS))
                shift, equilib = relaxed(p, u)
                shifts[(number - 1) * x_size + x, pl.ds(at, 8), :] = shift
                posts = posts_of(p, keep, equilib, rate, drive, range(POPS))
                for i in range(POPS):
                    target[i * planes + x + 1, pl.ds(at, 8), :] = posts[i]
            return 0

        lax.fori_loop(0, x_size, plane, 0, unroll=True)
        for side, (ref, edge, halo, pops, back) in enumerate(sides):
            for j in range(groups):
                at = FIRST + 8 * j
                rate, *u = [ref[pl.ds((15 + n) * window + 8 * j, 8), :] for n in range(4)]

                def read(i):
                    cy = VELOCITIES[i][1]
                    if i in back:
                        return source[i * planes + edge + 1, pl.ds(at + cy, 8), :]
                    return extra[side, pl.ds(at + cy, 8), :]

                p = pulled_from(read, back if number == 1 else back + LEVEL)
                added = rate * relaxed(p, u)[1]
                if number == 1:
                    extra[side, pl.ds(at, 8), :] = added
                for n, i in enumerate(pops):
                    target[i * planes + halo, pl.ds(at, 8), :] = (
                        ref[pl.ds((5 * number + n) * window + 8 * j, 8), :] + added
                    )

    step(1, state, later)
    step(2, later, state)

    def last(x, _):
        for j in range(y_size // 8):
            at = PAD + 8 * j
            keep, rate, *u, drive = [coef[n * x_size + x, pl.ds(at, 8), :] for n in range(6)]
            p = pulled_from(read_from(state, x, at), range(POPS))
            shift, equilib = relaxed(p, u)
            posts = posts_of(p, keep, equilib, rate, drive, range(POPS))
            for i in range(POPS):
                adjoint[i * x_size + x, pl.ds(8 * j, 8), :] = posts[i]
            shift = shifts[x, pl.ds(at, 8), :] + shifts[x_size + x, pl.ds(at, 8), :] + shift
            sens[x, pl.ds(8 * j, 8), :] = heat[x, pl.ds(8 * j, 8), :] * shift
        sens[x_size + x] = span[x].astype(jnp.float32) + 1.0
        return 0

    lax.fori_loop(0, x_size, last, 0, unroll=True)


def band_kernel(x_size, y_size, own, left, right, low, high):
    for kind in range(2):
        for n, ref in enumerate((left, own, right)):
            for x in range(x_size):
                k = kind * 3 * x_size + n * x_size + x
                low[k] = ref[kind * x_size + x, pl.ds(0, REACH), :]
                high[k] = ref[kind * x_size + x, pl.ds(y_size - REACH, REACH), :]


def filter_kernel(x_size, y_size, own, left, right, above, below, filtered, first, second, given, beta):
    wide = 3 * x_size
    rows = y_size + 2 * REACH

    def prepare(n, ref):
        def plane(x, _):
            k = n * x_size + x
            parts = (
                (0, REACH, below[k], below[wide + k]),
                (REACH, y_size, ref[x], ref[x_size + x]),
                (REACH + y_size, REACH, above[k], above[wide + k]),
            )
            for start, count, s, there in parts:
                r2 = jnp.where(there < 1.5, 0.25, jnp.where(there < 2.5, 1.0, jnp.where(there < 3.5, 4.0, 16.0)))
                inverse = 1.0 / (1.0 + 6.0 * r2)
                first[k, pl.ds(PAD + start, count), :] = s
                given[k, pl.ds(start, count), :] = s * inverse
                beta[k, pl.ds(start, count), :] = jnp.where(there > 0.5, r2 * inverse, 0.0)
            return 0

        lax.fori_loop(0, x_size, plane, 0, unroll=True)

    for n, ref in enumerate((left, own, right)):
        prepare(n, ref)
    source, target = first, second
    for number in range(1, SWEEPS + 1):
        final = number == SWEEPS
        margin = SWEEPS - number

        for j in range(1, 1 + y_size // 8) if final else range(rows // 8):
            at = PAD + 8 * j
            begin, end = x_size - margin, 2 * x_size + margin
            column = {x: source[x, pl.ds(at, 8), :] for x in range(begin - 1, end + 1)}
            for x in range(begin, end):
                beside = column[x + 1] + column[x - 1]
                beside = beside + source[x, pl.ds(at + 1, 8), :] + source[x, pl.ds(at - 1, 8), :]
                beside = beside + lane_pull(column[x], 1) + lane_pull(column[x], -1)
                value = given[x, pl.ds(8 * j, 8), :] + beta[x, pl.ds(8 * j, 8), :] * beside
                if final:
                    filtered[x - x_size, pl.ds(8 * j - REACH, 8), :] = value
                else:
                    target[x, pl.ds(at, 8), :] = value
        source, target = target, source


def call(kernel, outs, scratch, args, name):
    return pl.pallas_call(
        kernel,
        out_shape=[jax.ShapeDtypeStruct(shape, jnp.float32) for shape in outs],
        in_specs=[pl.BlockSpec(memory_space=pltpu.VMEM)] * len(args),
        out_specs=[pl.BlockSpec(memory_space=pltpu.VMEM)] * len(outs),
        scratch_shapes=[pltpu.VMEM(shape, jnp.float32) for shape in scratch],
        compiler_params=pltpu.CompilerParams(vmem_limit_bytes=32 * 1024 * 1024),
        name=name,
    )(*args)


def both_ways(axis, to_previous, to_next):
    size = lax.axis_size(axis)
    on = [(i, i + 1) for i in range(size - 1)]
    back = [(i + 1, i) for i in range(size - 1)]
    return lax.ppermute(to_previous, axis, back), lax.ppermute(to_next, axis, on)


def on_device(dual_populace, forward_motion_vector, forward_heat_level, objective_heat_gradient, liquid_indicator,
              filter_span_group):
    _, x_size, y_size, lanes = dual_populace.shape
    planes, pitch, window = x_size + 2, y_size + 2 * PAD, y_size + 8
    dual = dual_populace.reshape(POPS * x_size, y_size, lanes)
    vel = forward_motion_vector.reshape(3 * x_size, y_size, lanes)
    fields = (dual, vel, objective_heat_gradient, liquid_indicator)
    rim = (len(rim_entries(1)) * x_size, lanes)
    edge = (EDGES * window, lanes)
    state = (POPS * planes, pitch, lanes)
    coef = (6 * x_size, pitch, lanes)

    low, high = call(
        functools.partial(rim_kernel, x_size, y_size), [rim, rim], [], fields, "rim_rows"
    )
    above, below = both_ways("blk", low, high)
    to_left, to_right = call(
        functools.partial(edge_kernel, x_size, y_size),
        [edge, edge],
        [state, coef, (len(LEVEL), pitch, lanes), (len(RIGHT), pitch, lanes)],
        (*fields, above, below),
        "edge_planes",
    )
    from_right, from_left = both_ways("grp", to_left, to_right)
    adjoint, sens = call(
        functools.partial(steps_kernel, x_size, y_size),
        [(POPS * x_size, y_size, lanes), (2 * x_size, y_size, lanes)],
        [state, state, coef, (2 * x_size, pitch, lanes), (2, pitch, lanes)],
        (*fields, above, below, forward_heat_level, filter_span_group, from_right, from_left),
        "three_steps",
    )
    right, left = both_ways("grp", sens, sens)
    band = (6 * x_size, REACH, lanes)
    low, high = call(
        functools.partial(band_kernel, x_size, y_size), [band, band], [], (sens, left, right), "band_rows"
    )
    above, below = both_ways("blk", low, high)
    wide = 3 * x_size
    rows = y_size + 2 * REACH
    (filtered,) = call(
        functools.partial(filter_kernel, x_size, y_size),
        [(x_size, y_size, lanes)],
        [(wide, rows + 2 * PAD, lanes)] * 2 + [(wide, rows, lanes)] * 2,
        (sens, left, right, above, below),
        "eight_sweeps",
    )
    return adjoint.reshape(dual_populace.shape), filtered


def solution(mesh):
    in_specs = (
        P(None, "grp", "blk", None),
        P(None, "grp", "blk", None),
        P("grp", "blk", None),
        P("grp", "blk", None),
        P("grp", "blk", None),
        P("grp", "blk", None),
    )
    out_specs = (P(None, "grp", "blk", None), P("grp", "blk", None))
    return jax.shard_map(
        on_device, mesh=mesh, in_specs=in_specs, out_specs=out_specs, check_vma=False
    )
```

```python
import functools

import jax
import jax.numpy as jnp
from jax import lax
from jax.experimental import pallas as pl
from jax.experimental.pallas import tpu as pltpu
from jax.sharding import PartitionSpec as P

SWEEPS = 8
REACH = 8

VELOCITIES = (
    (0, 0, 0),
    (1, 0, 0),
    (-1, 0, 0),
    (0, 1, 0),
    (0, -1, 0),
    (0, 0, 1),
    (0, 0, -1),
    (1, 1, 0),
    (-1, -1, 0),
    (1, -1, 0),
    (-1, 1, 0),
    (1, 0, 1),
    (-1, 0, -1),
    (1, 0, -1),
    (-1, 0, 1),
    (0, 1, 1),
    (0, -1, -1),
    (0, 1, -1),
    (0, -1, 1),
)
POPS = 19
SHARE = 1.0 / 36.0
MULTIPLE = (12.0,) + (2.0,) * 6 + (1.0,) * 12
RIGHT = tuple(i for i in range(POPS) if VELOCITIES[i][0] == 1)
LEFT = tuple(i for i in range(POPS) if VELOCITIES[i][0] == -1)
LEVEL = tuple(i for i in range(POPS) if VELOCITIES[i][0] == 0)
PAD = 8
FIRST = 5
EDGES = 19


def rim_entries():
    entries = [(0, i, 1) for i in range(POPS)]
    entries += [(0, i, 2) for i in range(POPS) if VELOCITIES[i][1] != -1]
    entries += [(0, i, 3) for i in range(POPS) if VELOCITIES[i][1] == 1]
    for distance in (1, 2):
        entries += [(1, i, distance) for i in range(3)]
        entries += [(2, 0, distance), (3, 0, distance)]
    return entries


def mirrored(i, axis):
    velocity = list(VELOCITIES[i])
    velocity[axis] = -velocity[axis]
    return VELOCITIES.index(tuple(velocity))


def pick(condition, a, b):
    return a if a == b else jnp.where(condition, a, b)


def toward_next(axis):
    even = lax.axis_index(axis) % 2 == 0
    return even, jnp.logical_not(even)


def lane_pull(v, cz):
    if cz == 0:
        return v
    lanes = v.shape[-1]
    lane = lax.broadcasted_iota(jnp.int32, v.shape, 1)
    if cz == 1:
        return jnp.where(lane != lanes - 1, pltpu.roll(v, lanes - 1, 1), 0.0)
    return jnp.where(lane != 0, pltpu.roll(v, 1, 1), 0.0)


def total(terms):
    terms = [t for t in terms if t is not None]
    return functools.reduce(lambda a, b: a + b, terms) if terms else None


def scaled(v, factor):
    return None if v is None else factor * v


def negated(v):
    return None if v is None else -v


def moments(p):
    s, d = {}, {}
    for i in range(1, POPS, 2):
        a, b = p[i], p[i + 1]
        s[i] = total([a, b])
        d[i] = a - b if a is not None and b is not None else (a if b is None else negated(b))
    average = total(
        [scaled(p[0], 12.0), scaled(total([s[1], s[3], s[5]]), 2.0)] + [s[i] for i in (7, 9, 11, 13, 15, 17)]
    )
    along_x = total([scaled(d[1], 2.0), d[7], d[9], d[11], d[13]])
    along_y = total([scaled(d[3], 2.0), d[7], negated(d[9]), d[15], d[17]])
    along_z = total([scaled(d[5], 2.0), d[11], negated(d[13]), d[15], negated(d[17])])
    return average, (along_x, along_y, along_z)


def relaxed(p, u):
    average, along = moments(p)
    shift = total([u[k] * along[k] for k in range(3) if along[k] is not None])
    return shift, SHARE * average + shift


def pulled_from(read, pops):
    p = [None] * POPS
    for i in pops:
        p[i] = lane_pull(read(i), VELOCITIES[i][2])
    return p


def posts_of(p, keep, equilib, rate, source, pops):
    base = rate * equilib
    terms = {m: base + (source if m == 1.0 else m * source) for m in (12.0, 2.0, 1.0)}
    return {i: keep * p[i] + terms[MULTIPLE[i]] for i in pops}


def extend(x_size, y_size, dual, vel, grad, fluid, messages, state, coef):
    pitch = y_size + 2 * PAD
    planes = x_size + 2
    lanes = dual.shape[-1]
    flat = state.reshape(state.shape[0] * pitch, lanes)

    def copy_own(i, _):
        for x in range(x_size):
            state[i * planes + x + 1, pl.ds(PAD, y_size), :] = dual[i * x_size + x]
        return 0

    lax.fori_loop(0, POPS, copy_own, 0)
    rows = []
    for after, ref in zip(toward_next("blk"), messages):
        places = {d: jnp.where(after, PAD + y_size - 1 + d, PAD - d) for d in (1, 2, 3)}
        side = {}
        for k, (kind, i, distance) in enumerate(rim_entries()):
            value = ref[pl.ds(k * x_size, x_size), :]
            if kind == 0:
                pop = pick(after, i, mirrored(i, 1))
                at = (pop * planes + 1) * pitch + places[distance]
                flat[pl.ds(at, x_size, stride=pitch), :] = value
            else:
                side[(kind, i, distance)] = value
        rows += [(places[d], [side[key, n, d] for key, n in ((2, 0), (1, 0), (1, 1), (1, 2), (3, 0))]) for d in (1, 2)]
    coef_flat = coef.reshape(coef.shape[0] * pitch, lanes)

    def coefficients(there, ux, uy, uz, g):
        inside = there > 0.5
        wet = jnp.where(inside, there - 1.0, 0.0)
        keep = jnp.where(inside, 0.1 - 0.7 * wet, 0.0)
        rate = jnp.where(inside, 0.9 + 0.7 * wet, 0.0)
        scale = (3.0 * SHARE) * wet
        return keep, rate, scale * ux, scale * uy, scale * uz, SHARE * g

    def own_coefficients(x, _):
        there = fluid[x].astype(jnp.float32) + 1.0
        values = coefficients(there, vel[x], vel[x_size + x], vel[2 * x_size + x], grad[x])
        for n, value in enumerate(values):
            coef[n * x_size + x, pl.ds(PAD, y_size), :] = value
        return 0

    lax.fori_loop(0, x_size, own_coefficients, 0)
    for at, values in rows:
        for n, value in enumerate(coefficients(*values)):
            coef_flat[pl.ds(n * x_size * pitch + at, x_size, stride=pitch), :] = value


def rim_kernel(x_size, y_size, dual, vel, grad, fluid, *messages):
    lanes = dual.shape[-1]
    flat = [ref.reshape(ref.shape[0] * y_size, lanes) for ref in (dual, vel, fluid, grad)]
    for after, out in zip(toward_next("blk"), messages):
        for k, (kind, i, distance) in enumerate(rim_entries()):
            row = jnp.where(after, y_size - distance, distance - 1)
            field = pick(after, mirrored(i, 1), i) if kind == 0 else i
            value = flat[kind][pl.ds(field * x_size * y_size + row, x_size, stride=y_size), :]
            if kind == 2:
                value = value.astype(jnp.float32) + 1.0
            out[pl.ds(k * x_size, x_size), :] = value


def edge_kernel(x_size, y_size, dual, vel, grad, fluid, rim_a, rim_b, edge_a, edge_b, state, coef, near, far):
    extend(x_size, y_size, dual, vel, grad, fluid, (rim_a, rim_b), state, coef)
    planes = x_size + 2
    window = y_size + 8
    groups = window // 8
    known = RIGHT + LEVEL
    for after, out in zip(toward_next("grp"), (edge_a, edge_b)):
        inward = jnp.where(after, -1, 1)
        plane = jnp.where(after, x_size - 1, 0)
        turn = jnp.where(after, -1.0, 1.0)

        def coefs(x, at):
            return [coef[n * x_size + x, pl.ds(at, 8), :] for n in range(6)]

        def read_state(x, at):
            def read(i):
                cx, cy, _ = VELOCITIES[i]
                pop = pick(after, mirrored(i, 0), i)
                return state[pop * planes + x + 1 + cx * inward, pl.ds(at + cy, 8), :]

            return read

        for j in range(groups):
            at = FIRST + 8 * j
            keep, rate, *u, source = coefs(plane, at)
            for n, i in enumerate(RIGHT):
                pop = pick(after, mirrored(i, 0), i)
                out[pl.ds(n * window + 8 * j, 8), :] = state[pop * planes + plane + 1, pl.ds(at, 8), :]
            for n, value in enumerate((rate, *u)):
                out[pl.ds((15 + n) * window + 8 * j, 8), :] = value
            u[0] = turn * u[0]
            p = pulled_from(read_state(plane, at), known)
            _, equilib = relaxed(p, u)
            posts = posts_of(p, keep, equilib, rate, source, known)
            for n, i in enumerate(RIGHT):
                out[pl.ds((5 + n) * window + 8 * j, 8), :] = posts[i]
            for n, i in enumerate(LEVEL):
                near[n, pl.ds(at, 8), :] = posts[i]
            keep, rate, *u, source = coefs(plane + inward, at)
            u[0] = turn * u[0]
            p = pulled_from(read_state(plane + inward, at), range(POPS))
            _, equilib = relaxed(p, u)
            posts = posts_of(p, keep, equilib, rate, source, RIGHT)
            for n, i in enumerate(RIGHT):
                far[n, pl.ds(at, 8), :] = posts[i]
        for j in range(groups):
            at = FIRST + 8 * j
            keep, rate, *u, source = coefs(plane, at)
            u[0] = turn * u[0]

            def read(i):
                ref, n = (far, RIGHT.index(i)) if i in RIGHT else (near, LEVEL.index(i))
                return ref[n, pl.ds(at + VELOCITIES[i][1], 8), :]

            p = pulled_from(read, known)
            _, equilib = relaxed(p, u)
            posts = posts_of(p, keep, equilib, rate, source, RIGHT)
            for n, i in enumerate(RIGHT):
                out[pl.ds((10 + n) * window + 8 * j, 8), :] = posts[i]


def steps_kernel(
    x_size, y_size, dual, vel, grad, fluid, rim_a, rim_b, heat, span, edge_a, edge_b,
    adjoint, sens, state, later, coef, shifts, extra,
):
    extend(x_size, y_size, dual, vel, grad, fluid, (rim_a, rim_b), state, coef)
    planes = x_size + 2
    window = y_size + 8
    groups = window // 8
    sides = tuple(zip(toward_next("grp"), (edge_a, edge_b)))

    for after, ref in sides:
        halo = jnp.where(after, x_size + 1, 0)
        for n, i in enumerate(RIGHT):
            pop = pick(after, i, mirrored(i, 0))
            for j in range(groups):
                state[pop * planes + halo, pl.ds(FIRST + 8 * j, 8), :] = ref[pl.ds(n * window + 8 * j, 8), :]

    def read_from(source, x, at):
        def read(i):
            cx, cy, _ = VELOCITIES[i]
            return source[i * planes + x + 1 + cx, pl.ds(at + cy, 8), :]

        return read

    def step(number, source, target):
        def plane(x, _):
            for j in range(groups):
                at = FIRST + 8 * j
                keep, rate, *u, drive = [coef[n * x_size + x, pl.ds(at, 8), :] for n in range(6)]
                p = pulled_from(read_from(source, x, at), range(POPS))
                shift, equilib = relaxed(p, u)
                shifts[(number - 1) * x_size + x, pl.ds(at, 8), :] = shift
                posts = posts_of(p, keep, equilib, rate, drive, range(POPS))
                for i in range(POPS):
                    target[i * planes + x + 1, pl.ds(at, 8), :] = posts[i]
            return 0

        lax.fori_loop(0, x_size, plane, 0, unroll=True)
        for side, (after, ref) in enumerate(sides):
            halo = jnp.where(after, x_size + 1, 0)
            edge = jnp.where(after, x_size, 1)
            turn = jnp.where(after, 1.0, -1.0)
            for j in range(groups):
                at = FIRST + 8 * j
                rate, *u = [ref[pl.ds((15 + n) * window + 8 * j, 8), :] for n in range(4)]
                u[0] = turn * u[0]

                def read(i):
                    cy = VELOCITIES[i][1]
                    if i in LEFT:
                        return source[pick(after, i, mirrored(i, 0)) * planes + edge, pl.ds(at + cy, 8), :]
                    return extra[side, pl.ds(at + cy, 8), :]

                p = pulled_from(read, LEFT if number == 1 else LEFT + LEVEL)
                added = rate * relaxed(p, u)[1]
                if number == 1:
                    extra[side, pl.ds(at, 8), :] = added
                for n, i in enumerate(RIGHT):
                    target[pick(after, i, mirrored(i, 0)) * planes + halo, pl.ds(at, 8), :] = (
                        ref[pl.ds((5 * number + n) * window + 8 * j, 8), :] + added
                    )

    step(1, state, later)
    step(2, later, state)

    def last(x, _):
        for j in range(y_size // 8):
            at = PAD + 8 * j
            keep, rate, *u, drive = [coef[n * x_size + x, pl.ds(at, 8), :] for n in range(6)]
            p = pulled_from(read_from(state, x, at), range(POPS))
            shift, equilib = relaxed(p, u)
            posts = posts_of(p, keep, equilib, rate, drive, range(POPS))
            for i in range(POPS):
                adjoint[i * x_size + x, pl.ds(8 * j, 8), :] = posts[i]
            shift = shifts[x, pl.ds(at, 8), :] + shifts[x_size + x, pl.ds(at, 8), :] + shift
            sens[x, pl.ds(8 * j, 8), :] = heat[x, pl.ds(8 * j, 8), :] * shift
        sens[x_size + x] = span[x].astype(jnp.float32) + 1.0
        return 0

    lax.fori_loop(0, x_size, last, 0, unroll=True)


def band_kernel(x_size, y_size, own, beside_a, beside_b, band_a, band_b):
    bases = [x_size] + [jnp.where(after, 2 * x_size, 0) for after in toward_next("grp")]
    for after, out in zip(toward_next("blk"), (band_a, band_b)):
        start = pl.multiple_of(jnp.where(after, y_size - REACH, 0), 8)
        for kind in range(2):
            for base, ref in zip(bases, (own, beside_a, beside_b)):
                for x in range(x_size):
                    out[kind * 3 * x_size + base + x] = ref[kind * x_size + x, pl.ds(start, REACH), :]


def filter_kernel(x_size, y_size, own, beside_a, beside_b, band_a, band_b, filtered, first, second, given, beta):
    wide = 3 * x_size
    rows = y_size + 2 * REACH

    def prepare(k, start, count, s, there):
        r2 = jnp.where(there < 1.5, 0.25, jnp.where(there < 2.5, 1.0, jnp.where(there < 3.5, 4.0, 16.0)))
        inverse = 1.0 / (1.0 + 6.0 * r2)
        first[k, pl.ds(pl.multiple_of(PAD + start, 8), count), :] = s
        given[k, pl.ds(start, count), :] = s * inverse
        beta[k, pl.ds(start, count), :] = jnp.where(there > 0.5, r2 * inverse, 0.0)

    bases = [x_size] + [jnp.where(after, 2 * x_size, 0) for after in toward_next("grp")]
    for base, ref in zip(bases, (own, beside_a, beside_b)):
        for x in range(x_size):
            prepare(base + x, REACH, y_size, ref[x], ref[x_size + x])
    for after, ref in zip(toward_next("blk"), (band_a, band_b)):
        start = pl.multiple_of(jnp.where(after, REACH + y_size, 0), 8)
        for k in range(wide):
            prepare(k, start, REACH, ref[k], ref[wide + k])
    source, target = first, second
    for number in range(1, SWEEPS + 1):
        final = number == SWEEPS
        margin = SWEEPS - number

        for j in range(1, 1 + y_size // 8) if final else range(rows // 8):
            at = PAD + 8 * j
            begin, end = x_size - margin, 2 * x_size + margin
            column = {x: source[x, pl.ds(at, 8), :] for x in range(begin - 1, end + 1)}
            for x in range(begin, end):
                beside = column[x + 1] + column[x - 1]
                beside = beside + source[x, pl.ds(at + 1, 8), :] + source[x, pl.ds(at - 1, 8), :]
                beside = beside + lane_pull(column[x], 1) + lane_pull(column[x], -1)
                value = given[x, pl.ds(8 * j, 8), :] + beta[x, pl.ds(8 * j, 8), :] * beside
                if final:
                    filtered[x - x_size, pl.ds(8 * j - REACH, 8), :] = value
                else:
                    target[x, pl.ds(at, 8), :] = value
        source, target = target, source


def call(kernel, outs, scratch, args, name):
    return pl.pallas_call(
        kernel,
        out_shape=[jax.ShapeDtypeStruct(shape, jnp.float32) for shape in outs],
        in_specs=[pl.BlockSpec(memory_space=pltpu.VMEM)] * len(args),
        out_specs=[pl.BlockSpec(memory_space=pltpu.VMEM)] * len(outs),
        scratch_shapes=[pltpu.VMEM(shape, jnp.float32) for shape in scratch],
        compiler_params=pltpu.CompilerParams(vmem_limit_bytes=32 * 1024 * 1024),
        name=name,
    )(*args)


def swapped(axis, message_a, message_b):
    size = lax.axis_size(axis)
    received = []
    for begin, message in ((0, message_a), (1, message_b)):
        pairs = [(i, i + 1) for i in range(begin, size - 1, 2)]
        received.append(lax.ppermute(message, axis, pairs + [(j, i) for i, j in pairs]))
    return received


def on_device(dual_populace, forward_motion_vector, forward_heat_level, objective_heat_gradient, liquid_indicator,
              filter_span_group):
    _, x_size, y_size, lanes = dual_populace.shape
    planes, pitch, window = x_size + 2, y_size + 2 * PAD, y_size + 8
    dual = dual_populace.reshape(POPS * x_size, y_size, lanes)
    vel = forward_motion_vector.reshape(3 * x_size, y_size, lanes)
    fields = (dual, vel, objective_heat_gradient, liquid_indicator)
    rim = (len(rim_entries()) * x_size, lanes)
    edge = (EDGES * window, lanes)
    state = (POPS * planes, pitch, lanes)
    coef = (6 * x_size, pitch, lanes)

    rims = call(functools.partial(rim_kernel, x_size, y_size), [rim, rim], [], fields, "rim_rows")
    rims = swapped("blk", *rims)
    edges = call(
        functools.partial(edge_kernel, x_size, y_size),
        [edge, edge],
        [state, coef, (len(LEVEL), pitch, lanes), (len(RIGHT), pitch, lanes)],
        (*fields, *rims),
        "edge_planes",
    )
    edges = swapped("grp", *edges)
    adjoint, sens = call(
        functools.partial(steps_kernel, x_size, y_size),
        [(POPS * x_size, y_size, lanes), (2 * x_size, y_size, lanes)],
        [state, state, coef, (2 * x_size, pitch, lanes), (2, pitch, lanes)],
        (*fields, *rims, forward_heat_level, filter_span_group, *edges),
        "three_steps",
    )
    beside = swapped("grp", sens, sens)
    band = (6 * x_size, REACH, lanes)
    bands = call(functools.partial(band_kernel, x_size, y_size), [band, band], [], (sens, *beside), "band_rows")
    bands = swapped("blk", *bands)
    wide = 3 * x_size
    rows = y_size + 2 * REACH
    (filtered,) = call(
        functools.partial(filter_kernel, x_size, y_size),
        [(x_size, y_size, lanes)],
        [(wide, rows + 2 * PAD, lanes)] * 2 + [(wide, rows, lanes)] * 2,
        (sens, *beside, *bands),
        "eight_sweeps",
    )
    return adjoint.reshape(dual_populace.shape), filtered


def solution(mesh):
    in_specs = (
        P(None, "grp", "blk", None),
        P(None, "grp", "blk", None),
        P("grp", "blk", None),
        P("grp", "blk", None),
        P("grp", "blk", None),
        P("grp", "blk", None),
    )
    out_specs = (P(None, "grp", "blk", None), P("grp", "blk", None))
    return jax.shard_map(
        on_device, mesh=mesh, in_specs=in_specs, out_specs=out_specs, check_vma=False
    )
```

```python
import functools

import jax
import jax.numpy as jnp
from jax import lax
from jax.experimental import pallas as pl
from jax.experimental.pallas import tpu as pltpu
from jax.sharding import PartitionSpec as P

SWEEPS = 8
REACH = 8

VELOCITIES = (
    (0, 0, 0),
    (1, 0, 0),
    (-1, 0, 0),
    (0, 1, 0),
    (0, -1, 0),
    (0, 0, 1),
    (0, 0, -1),
    (1, 1, 0),
    (-1, -1, 0),
    (1, -1, 0),
    (-1, 1, 0),
    (1, 0, 1),
    (-1, 0, -1),
    (1, 0, -1),
    (-1, 0, 1),
    (0, 1, 1),
    (0, -1, -1),
    (0, 1, -1),
    (0, -1, 1),
)
POPS = 19
SHARE = 1.0 / 36.0
MULTIPLE = (12.0,) + (2.0,) * 6 + (1.0,) * 12
RIGHT = tuple(i for i in range(POPS) if VELOCITIES[i][0] == 1)
LEFT = tuple(i for i in range(POPS) if VELOCITIES[i][0] == -1)
LEVEL = tuple(i for i in range(POPS) if VELOCITIES[i][0] == 0)
PAD = 8
FIRST = 5
EDGES = 19


def rim_entries():
    entries = [(0, i, 1) for i in range(POPS)]
    entries += [(0, i, 2) for i in range(POPS) if VELOCITIES[i][1] != -1]
    entries += [(0, i, 3) for i in range(POPS) if VELOCITIES[i][1] == 1]
    for distance in (1, 2):
        entries += [(1, i, distance) for i in range(3)]
        entries += [(2, 0, distance), (3, 0, distance)]
    return entries


def mirrored(i, axis):
    velocity = list(VELOCITIES[i])
    velocity[axis] = -velocity[axis]
    return VELOCITIES.index(tuple(velocity))


def pick(condition, a, b):
    return a if a == b else jnp.where(condition, a, b)


def toward_next(axis):
    even = lax.axis_index(axis) % 2 == 0
    return even, jnp.logical_not(even)


def lane_pull(v, cz):
    if cz == 0:
        return v
    lanes = v.shape[-1]
    lane = lax.broadcasted_iota(jnp.int32, v.shape, 1)
    if cz == 1:
        return jnp.where(lane != lanes - 1, pltpu.roll(v, lanes - 1, 1), 0.0)
    return jnp.where(lane != 0, pltpu.roll(v, 1, 1), 0.0)


def total(terms):
    terms = [t for t in terms if t is not None]
    return functools.reduce(lambda a, b: a + b, terms) if terms else None


def scaled(v, factor):
    return None if v is None else factor * v


def negated(v):
    return None if v is None else -v


def moments(p):
    s, d = {}, {}
    for i in range(1, POPS, 2):
        a, b = p[i], p[i + 1]
        s[i] = total([a, b])
        d[i] = a - b if a is not None and b is not None else (a if b is None else negated(b))
    average = total(
        [scaled(p[0], 12.0), scaled(total([s[1], s[3], s[5]]), 2.0)] + [s[i] for i in (7, 9, 11, 13, 15, 17)]
    )
    along_x = total([scaled(d[1], 2.0), d[7], d[9], d[11], d[13]])
    along_y = total([scaled(d[3], 2.0), d[7], negated(d[9]), d[15], d[17]])
    along_z = total([scaled(d[5], 2.0), d[11], negated(d[13]), d[15], negated(d[17])])
    return average, (along_x, along_y, along_z)


def relaxed(p, u):
    average, along = moments(p)
    shift = total([u[k] * along[k] for k in range(3) if along[k] is not None])
    return shift, SHARE * average + shift


def pulled_from(read, pops):
    p = [None] * POPS
    for i in pops:
        p[i] = lane_pull(read(i), VELOCITIES[i][2])
    return p


def posts_of(p, keep, equilib, rate, source, pops):
    base = rate * equilib
    terms = {m: base + (source if m == 1.0 else m * source) for m in (12.0, 2.0, 1.0)}
    return {i: keep * p[i] + terms[MULTIPLE[i]] for i in pops}


def coefficients(there, ux, uy, uz, g):
    inside = there > 0.5
    wet = jnp.where(inside, there - 1.0, 0.0)
    keep = jnp.where(inside, 0.1 - 0.7 * wet, 0.0)
    rate = jnp.where(inside, 0.9 + 0.7 * wet, 0.0)
    scale = (3.0 * SHARE) * wet
    return keep, rate, scale * ux, scale * uy, scale * uz, SHARE * g


def extend_own(x_size, y_size, dual, vel, grad, fluid, state, coef):
    planes = x_size + 2

    def copy_own(i, _):
        for x in range(x_size):
            state[i * planes + x + 1, pl.ds(PAD, y_size), :] = dual[i * x_size + x]
        return 0

    lax.fori_loop(0, POPS, copy_own, 0)

    def own_coefficients(x, _):
        there = fluid[x].astype(jnp.float32) + 1.0
        values = coefficients(there, vel[x], vel[x_size + x], vel[2 * x_size + x], grad[x])
        for n, value in enumerate(values):
            coef[n * x_size + x, pl.ds(PAD, y_size), :] = value
        return 0

    lax.fori_loop(0, x_size, own_coefficients, 0)


def extend_rims(x_size, y_size, messages, state, coef):
    pitch = y_size + 2 * PAD
    planes = x_size + 2
    lanes = state.shape[-1]
    flat = state.reshape(state.shape[0] * pitch, lanes)
    coef_flat = coef.reshape(coef.shape[0] * pitch, lanes)
    for after, ref in zip(toward_next("blk"), messages):
        places = {d: jnp.where(after, PAD + y_size - 1 + d, PAD - d) for d in (1, 2, 3)}
        side = {}
        for k, (kind, i, distance) in enumerate(rim_entries()):
            value = ref[pl.ds(k * x_size, x_size), :]
            if kind == 0:
                pop = pick(after, i, mirrored(i, 1))
                at = (pop * planes + 1) * pitch + places[distance]
                flat[pl.ds(at, x_size, stride=pitch), :] = value
            else:
                side[(kind, i, distance)] = value
        for d in (1, 2):
            values = [side[key, n, d] for key, n in ((2, 0), (1, 0), (1, 1), (1, 2), (3, 0))]
            for n, value in enumerate(coefficients(*values)):
                coef_flat[pl.ds(n * x_size * pitch + places[d], x_size, stride=pitch), :] = value


def rim_kernel(x_size, y_size, *refs):
    sources, messages, held, arrived = refs[:4], refs[4:6], refs[6:10], refs[10]
    copies = [pltpu.make_async_copy(a, b, arrived.at[n]) for n, (a, b) in enumerate(zip(sources, held))]
    for copy in copies:
        copy.start()
    for copy in copies:
        copy.wait()
    dual, vel, grad, fluid = held
    lanes = dual.shape[-1]
    flat = [ref.reshape(ref.shape[0] * y_size, lanes) for ref in (dual, vel, fluid, grad)]
    for after, out in zip(toward_next("blk"), messages):
        for k, (kind, i, distance) in enumerate(rim_entries()):
            row = jnp.where(after, y_size - distance, distance - 1)
            field = pick(after, mirrored(i, 1), i) if kind == 0 else i
            value = flat[kind][pl.ds(field * x_size * y_size + row, x_size, stride=y_size), :]
            if kind == 2:
                value = value.astype(jnp.float32) + 1.0
            out[pl.ds(k * x_size, x_size), :] = value


def edge_steps(x_size, after, state, coef, near, far, raw, first, second, put):
    known = RIGHT + LEVEL
    planes = x_size + 2
    inward = jnp.where(after, -1, 1)
    plane = jnp.where(after, x_size - 1, 0)
    turn = jnp.where(after, -1.0, 1.0)

    def coefs(x, at):
        return [coef[n * x_size + x, pl.ds(at, 8), :] for n in range(6)]

    def read_state(x, at):
        def read(i):
            cx, cy, _ = VELOCITIES[i]
            pop = pick(after, mirrored(i, 0), i)
            return state[pop * planes + x + 1 + cx * inward, pl.ds(at + cy, 8), :]

        return read

    for at in raw:
        for n, i in enumerate(RIGHT):
            pop = pick(after, mirrored(i, 0), i)
            put(0, n, at, state[pop * planes + plane + 1, pl.ds(at, 8), :])
    for at in first:
        keep, rate, *u, source = coefs(plane, at)
        for n, value in enumerate((rate, *u)):
            put(3, n, at, value)
        u[0] = turn * u[0]
        p = pulled_from(read_state(plane, at), known)
        _, equilib = relaxed(p, u)
        posts = posts_of(p, keep, equilib, rate, source, known)
        for n, i in enumerate(RIGHT):
            put(1, n, at, posts[i])
        for n, i in enumerate(LEVEL):
            near[n, pl.ds(at, 8), :] = posts[i]
        keep, rate, *u, source = coefs(plane + inward, at)
        u[0] = turn * u[0]
        p = pulled_from(read_state(plane + inward, at), range(POPS))
        _, equilib = relaxed(p, u)
        posts = posts_of(p, keep, equilib, rate, source, RIGHT)
        for n, i in enumerate(RIGHT):
            far[n, pl.ds(at, 8), :] = posts[i]
    for at in second:
        keep, rate, *u, source = coefs(plane, at)
        u[0] = turn * u[0]

        def read(i):
            ref, n = (far, RIGHT.index(i)) if i in RIGHT else (near, LEVEL.index(i))
            return ref[n, pl.ds(at + VELOCITIES[i][1], 8), :]

        p = pulled_from(read, known)
        _, equilib = relaxed(p, u)
        posts = posts_of(p, keep, equilib, rate, source, RIGHT)
        for n, i in enumerate(RIGHT):
            put(2, n, at, posts[i])


EARLY = (0, 5, 10, 15)


def early_kernel(x_size, y_size, dual, vel, grad, fluid, span, early_a, early_b, state, coef, near, far):
    extend_own(x_size, y_size, dual, vel, grad, fluid, state, coef)
    rows = range(PAD, PAD + y_size, 8)
    for after, out in zip(toward_next("grp"), (early_a, early_b)):

        def put(kind, n, at, value, out=out):
            out[pl.ds((EARLY[kind] + n) * y_size + at - PAD, 8), :] = value

        edge_steps(x_size, after, state, coef, near, far, rows, rows, rows, put)
        for x in range(x_size):
            out[pl.ds((EDGES + x) * y_size, y_size), :] = span[x].astype(jnp.float32) + 1.0


def late_pieces(y_size):
    pieces, offset = {}, 0
    for end in (0, 1):
        for kind, count, reach in ((0, 5, 3), (1, 5, 2), (2, 5, 1), (3, 4, 2)):
            rows = 2 if kind == 3 else 3
            begin = PAD + y_size + reach - rows if end else PAD - reach
            pieces[kind, end] = (begin, rows, offset)
            offset += count * rows
    return pieces, -(-offset // 8) * 8


def late_kernel(x_size, y_size, dual, vel, grad, fluid, rim_a, rim_b, late_a, late_b, state, coef, near, far):
    extend_own(x_size, y_size, dual, vel, grad, fluid, state, coef)
    extend_rims(x_size, y_size, (rim_a, rim_b), state, coef)
    pieces, _ = late_pieces(y_size)
    starts = [(PAD - reach, PAD + y_size + reach - 8) for reach in (3, 2, 1)]
    for after, out in zip(toward_next("grp"), (late_a, late_b)):

        def put(kind, n, at, value, out=out):
            begin, rows, offset = pieces[kind, 1 if at > PAD else 0]
            out[pl.ds(offset + n * rows, rows), :] = value[begin - at : begin - at + rows]

        edge_steps(x_size, after, state, coef, near, far, *starts, put)


def steps_kernel(
    x_size, y_size, dual, vel, grad, fluid, rim_a, rim_b, heat, early_a, early_b, late_a, late_b,
    adjoint, sens, state, later, coef, shifts, extra, halos,
):
    extend_own(x_size, y_size, dual, vel, grad, fluid, state, coef)
    extend_rims(x_size, y_size, (rim_a, rim_b), state, coef)
    planes = x_size + 2
    window = y_size + 8
    groups = window // 8
    afters = toward_next("grp")
    pieces, _ = late_pieces(y_size)

    for side, (after, early, late) in enumerate(zip(afters, (early_a, early_b), (late_a, late_b))):
        halo = jnp.where(after, x_size + 1, 0)
        for kind, count in enumerate((5, 5, 5, 4)):
            for n in range(count):
                if kind == 0:
                    ref, plane = state, pick(after, RIGHT[n], mirrored(RIGHT[n], 0)) * planes + halo
                else:
                    ref, plane = halos, side * 14 + EARLY[kind] - 5 + n
                ref[plane, pl.ds(PAD, y_size), :] = early[pl.ds((EARLY[kind] + n) * y_size, y_size), :]
                for end in (0, 1):
                    begin, rows, offset = pieces[kind, end]
                    ref[plane, pl.ds(begin, rows), :] = late[pl.ds(offset + n * rows, rows), :]

    def read_from(source, x, at):
        def read(i):
            cx, cy, _ = VELOCITIES[i]
            return source[i * planes + x + 1 + cx, pl.ds(at + cy, 8), :]

        return read

    def step(number, source, target):
        def plane(x, _):
            for j in range(groups):
                at = FIRST + 8 * j
                keep, rate, *u, drive = [coef[n * x_size + x, pl.ds(at, 8), :] for n in range(6)]
                p = pulled_from(read_from(source, x, at), range(POPS))
                shift, equilib = relaxed(p, u)
                shifts[(number - 1) * x_size + x, pl.ds(at, 8), :] = shift
                posts = posts_of(p, keep, equilib, rate, drive, range(POPS))
                for i in range(POPS):
                    target[i * planes + x + 1, pl.ds(at, 8), :] = posts[i]
            return 0

        lax.fori_loop(0, x_size, plane, 0, unroll=True)
        for side, after in enumerate(afters):
            halo = jnp.where(after, x_size + 1, 0)
            edge = jnp.where(after, x_size, 1)
            turn = jnp.where(after, 1.0, -1.0)
            for j in range(groups):
                at = FIRST + 8 * j
                rate, *u = [halos[side * 14 + 10 + n, pl.ds(at, 8), :] for n in range(4)]
                u[0] = turn * u[0]

                def read(i):
                    cy = VELOCITIES[i][1]
                    if i in LEFT:
                        return source[pick(after, i, mirrored(i, 0)) * planes + edge, pl.ds(at + cy, 8), :]
                    return extra[side, pl.ds(at + cy, 8), :]

                p = pulled_from(read, LEFT if number == 1 else LEFT + LEVEL)
                added = rate * relaxed(p, u)[1]
                if number == 1:
                    extra[side, pl.ds(at, 8), :] = added
                for n, i in enumerate(RIGHT):
                    target[pick(after, i, mirrored(i, 0)) * planes + halo, pl.ds(at, 8), :] = (
                        halos[side * 14 + 5 * number - 5 + n, pl.ds(at, 8), :] + added
                    )

    step(1, state, later)
    step(2, later, state)

    def last(x, _):
        for j in range(y_size // 8):
            at = PAD + 8 * j
            keep, rate, *u, drive = [coef[n * x_size + x, pl.ds(at, 8), :] for n in range(6)]
            p = pulled_from(read_from(state, x, at), range(POPS))
            shift, equilib = relaxed(p, u)
            posts = posts_of(p, keep, equilib, rate, drive, range(POPS))
            for i in range(POPS):
                adjoint[i * x_size + x, pl.ds(8 * j, 8), :] = posts[i]
            shift = shifts[x, pl.ds(at, 8), :] + shifts[x_size + x, pl.ds(at, 8), :] + shift
            sens[x, pl.ds(8 * j, 8), :] = heat[x, pl.ds(8 * j, 8), :] * shift
        return 0

    lax.fori_loop(0, x_size, last, 0, unroll=True)


def diamond(x_size, reach):
    pieces, offset = [], 0
    for slot in range(3):
        for k in range(x_size if slot == 0 else min(x_size, reach - 1)):
            rows = reach if slot == 0 else reach - 1 - k
            pieces.append((slot, k, rows, offset))
            offset += rows
    return pieces, -(-offset // 8) * 8


def slot_plane(x_size, slot, k):
    if slot == 0:
        return x_size + k, k
    after = toward_next("grp")[slot - 1]
    return jnp.where(after, 2 * x_size + k, x_size - 1 - k), jnp.where(after, k, x_size - 1 - k)


def band_kernel(x_size, y_size, reach, own, beside_a, beside_b, band_a, band_b):
    pieces, _ = diamond(x_size, reach)
    skip = EDGES if beside_a.shape[0] > x_size else 0
    for after, out in zip(toward_next("blk"), (band_a, band_b)):
        for slot, k, rows, offset in pieces:
            _, plane = slot_plane(x_size, slot, k)
            start = jnp.where(after, y_size - rows, 0)
            if slot == 0:
                value = own[plane, pl.ds(start, rows), :]
                if skip:
                    value = value.astype(jnp.float32) + 1.0
            else:
                value = (beside_a, beside_b)[slot - 1][skip + plane, pl.ds(start, rows), :]
            out[pl.ds(offset, rows), :] = value


def radius_kernel(x_size, y_size, own, early_a, early_b, band_a, band_b, inverse, beta, there):
    for x in range(x_size):
        there[x_size + x, pl.ds(REACH, y_size), :] = own[x].astype(jnp.float32) + 1.0
        for slot, ref in ((1, early_a), (2, early_b)):
            place, plane = slot_plane(x_size, slot, x)
            there[place, pl.ds(REACH, y_size), :] = ref[EDGES + plane]
    for after, ref in zip(toward_next("blk"), (band_a, band_b)):
        for slot, k, rows, offset in diamond(x_size, REACH - 1)[0]:
            place, _ = slot_plane(x_size, slot, k)
            there[place, pl.ds(jnp.where(after, REACH + y_size, REACH - rows), rows), :] = ref[pl.ds(offset, rows), :]

    def plane(k, _):
        t = there[k]
        r2 = jnp.where(t < 1.5, 0.25, jnp.where(t < 2.5, 1.0, jnp.where(t < 3.5, 4.0, 16.0)))
        share = 1.0 / (1.0 + 6.0 * r2)
        inverse[k] = share
        beta[k] = jnp.where(t > 0.5, r2 * share, 0.0)
        return 0

    lax.fori_loop(0, 3 * x_size, plane, 0, unroll=4)


def filter_kernel(x_size, y_size, own, beside_a, beside_b, band_a, band_b, inverse, beta, filtered, first, second, given):
    wide = 3 * x_size
    rows = y_size + 2 * REACH
    for x in range(x_size):
        first[x_size + x, pl.ds(PAD + REACH, y_size), :] = own[x]
        for slot, ref in ((1, beside_a), (2, beside_b)):
            place, plane = slot_plane(x_size, slot, x)
            first[place, pl.ds(PAD + REACH, y_size), :] = ref[plane]
    for after, ref in zip(toward_next("blk"), (band_a, band_b)):
        for slot, k, count, offset in diamond(x_size, REACH)[0]:
            place, _ = slot_plane(x_size, slot, k)
            at = PAD + jnp.where(after, REACH + y_size, REACH - count)
            first[place, pl.ds(at, count), :] = ref[pl.ds(offset, count), :]
    for k in range(wide):
        given[k] = first[k, pl.ds(PAD, rows), :] * inverse[k]
    source, target = first, second
    for number in range(1, SWEEPS + 1):
        final = number == SWEEPS
        margin = SWEEPS - number

        for j in range(1, 1 + y_size // 8) if final else range(rows // 8):
            at = PAD + 8 * j
            begin, end = x_size - margin, 2 * x_size + margin
            column = {x: source[x, pl.ds(at, 8), :] for x in range(begin - 1, end + 1)}
            for x in range(begin, end):
                beside = column[x + 1] + column[x - 1]
                beside = beside + source[x, pl.ds(at + 1, 8), :] + source[x, pl.ds(at - 1, 8), :]
                beside = beside + lane_pull(column[x], 1) + lane_pull(column[x], -1)
                value = given[x, pl.ds(8 * j, 8), :] + beta[x, pl.ds(8 * j, 8), :] * beside
                if final:
                    filtered[x - x_size, pl.ds(8 * j - REACH, 8), :] = value
                else:
                    target[x, pl.ds(at, 8), :] = value
        source, target = target, source


def call(kernel, outs, scratch, args, name, place=pltpu.VMEM, grant=32):
    return pl.pallas_call(
        kernel,
        out_shape=[jax.ShapeDtypeStruct(shape, jnp.float32) for shape in outs],
        in_specs=[pl.BlockSpec(memory_space=place)] * len(args),
        out_specs=[pl.BlockSpec(memory_space=pltpu.VMEM)] * len(outs),
        scratch_shapes=[pltpu.VMEM(s, jnp.float32) if isinstance(s, tuple) else s for s in scratch],
        compiler_params=pltpu.CompilerParams(vmem_limit_bytes=grant * 1024 * 1024),
        name=name,
    )(*args)


def swapped(axis, message_a, message_b):
    size = lax.axis_size(axis)
    received = []
    for begin, message in ((1, message_b), (0, message_a)):
        pairs = [(i, i + 1) for i in range(begin, size - 1, 2)]
        received.append(lax.ppermute(message, axis, pairs + [(j, i) for i, j in pairs]))
    return received[1], received[0]


def on_device(dual_populace, forward_motion_vector, forward_heat_level, objective_heat_gradient, liquid_indicator,
              filter_span_group):
    _, x_size, y_size, lanes = dual_populace.shape
    planes, pitch = x_size + 2, y_size + 2 * PAD
    sizes = (x_size, y_size)
    dual = dual_populace.reshape(POPS * x_size, y_size, lanes)
    vel = forward_motion_vector.reshape(3 * x_size, y_size, lanes)
    fields = (dual, vel, objective_heat_gradient, liquid_indicator)
    rim = (len(rim_entries()) * x_size, lanes)
    state = (POPS * planes, pitch, lanes)
    coef = (6 * x_size, pitch, lanes)
    edge_scratch = [state, coef, (len(LEVEL), pitch, lanes), (len(RIGHT), pitch, lanes)]

    rims = call(
        functools.partial(rim_kernel, *sizes),
        [rim, rim],
        [pltpu.VMEM(f.shape, f.dtype) for f in fields] + [pltpu.SemaphoreType.DMA((len(fields),))],
        fields,
        "rim_rows",
        pltpu.HBM,
        63,
    )
    rims = swapped("blk", *rims)
    early = ((EDGES + x_size) * y_size, lanes)
    earlies = call(
        functools.partial(early_kernel, *sizes),
        [early, early],
        edge_scratch,
        (*fields, filter_span_group),
        "edges_early",
    )
    earlies = swapped("grp", *earlies)
    late = (late_pieces(y_size)[1], lanes)
    lates = call(functools.partial(late_kernel, *sizes), [late, late], edge_scratch, (*fields, *rims), "edges_late")
    lates = swapped("grp", *lates)
    adjoint, sens = call(
        functools.partial(steps_kernel, *sizes),
        [(POPS * x_size, y_size, lanes), (x_size, y_size, lanes)],
        [state, state, coef, (2 * x_size, pitch, lanes), (2, pitch, lanes), (28, pitch, lanes)],
        (*fields, *rims, forward_heat_level, *earlies, *lates),
        "three_steps",
    )
    beside = swapped("grp", sens, sens)

    wide, rows = 3 * x_size, y_size + 2 * REACH
    spans = [e.reshape(EDGES + x_size, y_size, lanes) for e in earlies]
    band = (diamond(x_size, REACH - 1)[1], lanes)
    span_bands = call(
        functools.partial(band_kernel, *sizes, REACH - 1), [band, band], [], (filter_span_group, *spans), "span_bands"
    )
    span_bands = swapped("blk", *span_bands)
    beside, span_bands = lax.optimization_barrier((beside, span_bands))
    inverse, beta = call(
        functools.partial(radius_kernel, *sizes),
        [(wide, rows, lanes)] * 2,
        [(wide, rows, lanes)],
        (filter_span_group, *spans, *span_bands),
        "radius",
    )
    band = (diamond(x_size, REACH)[1], lanes)
    bands = call(functools.partial(band_kernel, *sizes, REACH), [band, band], [], (sens, *beside), "sens_bands")
    bands = swapped("blk", *bands)
    (filtered,) = call(
        functools.partial(filter_kernel, *sizes),
        [(x_size, y_size, lanes)],
        [(wide, rows + 2 * PAD, lanes)] * 2 + [(wide, rows, lanes)],
        (sens, *beside, *bands, inverse, beta),
        "eight_sweeps",
    )
    return adjoint.reshape(dual_populace.shape), filtered


def solution(mesh):
    in_specs = (
        P(None, "grp", "blk", None),
        P(None, "grp", "blk", None),
        P("grp", "blk", None),
        P("grp", "blk", None),
        P("grp", "blk", None),
        P("grp", "blk", None),
    )
    out_specs = (P(None, "grp", "blk", None), P("grp", "blk", None))
    return jax.shard_map(
        on_device, mesh=mesh, in_specs=in_specs, out_specs=out_specs, check_vma=False
    )
```

```python
import functools

import jax
import jax.numpy as jnp
from jax import lax
from jax.experimental import pallas as pl
from jax.experimental.pallas import tpu as pltpu
from jax.sharding import PartitionSpec as P

SWEEPS = 8
REACH = 8

VELOCITIES = (
    (0, 0, 0),
    (1, 0, 0),
    (-1, 0, 0),
    (0, 1, 0),
    (0, -1, 0),
    (0, 0, 1),
    (0, 0, -1),
    (1, 1, 0),
    (-1, -1, 0),
    (1, -1, 0),
    (-1, 1, 0),
    (1, 0, 1),
    (-1, 0, -1),
    (1, 0, -1),
    (-1, 0, 1),
    (0, 1, 1),
    (0, -1, -1),
    (0, 1, -1),
    (0, -1, 1),
)
POPS = 19
SHARE = 1.0 / 36.0
MULTIPLE = (12.0,) + (2.0,) * 6 + (1.0,) * 12
RIGHT = tuple(i for i in range(POPS) if VELOCITIES[i][0] == 1)
LEFT = tuple(i for i in range(POPS) if VELOCITIES[i][0] == -1)
LEVEL = tuple(i for i in range(POPS) if VELOCITIES[i][0] == 0)
PAD = 8
FIRST = 5
EDGES = 19


def rim_entries():
    entries = [(0, i, 1) for i in range(POPS)]
    entries += [(0, i, 2) for i in range(POPS) if VELOCITIES[i][1] != -1]
    entries += [(0, i, 3) for i in range(POPS) if VELOCITIES[i][1] == 1]
    for distance in (1, 2):
        entries += [(1, i, distance) for i in range(3)]
        entries += [(2, 0, distance), (3, 0, distance)]
    return entries


def mirrored(i, axis):
    velocity = list(VELOCITIES[i])
    velocity[axis] = -velocity[axis]
    return VELOCITIES.index(tuple(velocity))


def pick(condition, a, b):
    return a if a == b else jnp.where(condition, a, b)


def toward_next(axis):
    even = lax.axis_index(axis) % 2 == 0
    return even, jnp.logical_not(even)


def lane_pull(v, cz):
    if cz == 0:
        return v
    lanes = v.shape[-1]
    lane = lax.broadcasted_iota(jnp.int32, v.shape, 1)
    if cz == 1:
        return jnp.where(lane != lanes - 1, pltpu.roll(v, lanes - 1, 1), 0.0)
    return jnp.where(lane != 0, pltpu.roll(v, 1, 1), 0.0)


def total(terms):
    terms = [t for t in terms if t is not None]
    return functools.reduce(lambda a, b: a + b, terms) if terms else None


def scaled(v, factor):
    return None if v is None else factor * v


def negated(v):
    return None if v is None else -v


def moments(p):
    s, d = {}, {}
    for i in range(1, POPS, 2):
        a, b = p[i], p[i + 1]
        s[i] = total([a, b])
        d[i] = a - b if a is not None and b is not None else (a if b is None else negated(b))
    average = total(
        [scaled(p[0], 12.0), scaled(total([s[1], s[3], s[5]]), 2.0)] + [s[i] for i in (7, 9, 11, 13, 15, 17)]
    )
    along_x = total([scaled(d[1], 2.0), d[7], d[9], d[11], d[13]])
    along_y = total([scaled(d[3], 2.0), d[7], negated(d[9]), d[15], d[17]])
    along_z = total([scaled(d[5], 2.0), d[11], negated(d[13]), d[15], negated(d[17])])
    return average, (along_x, along_y, along_z)


def relaxed(p, u):
    average, along = moments(p)
    shift = total([u[k] * along[k] for k in range(3) if along[k] is not None])
    return shift, SHARE * average + shift


def pulled_from(read, pops):
    p = [None] * POPS
    for i in pops:
        p[i] = lane_pull(read(i), VELOCITIES[i][2])
    return p


def posts_of(p, keep, equilib, rate, source, pops):
    base = rate * equilib
    terms = {m: base + (source if m == 1.0 else m * source) for m in (12.0, 2.0, 1.0)}
    return {i: keep * p[i] + terms[MULTIPLE[i]] for i in pops}


def coefficients(there, ux, uy, uz, g):
    inside = there > 0.5
    wet = jnp.where(inside, there - 1.0, 0.0)
    keep = jnp.where(inside, 0.1 - 0.7 * wet, 0.0)
    rate = jnp.where(inside, 0.9 + 0.7 * wet, 0.0)
    scale = (3.0 * SHARE) * wet
    return keep, rate, scale * ux, scale * uy, scale * uz, SHARE * g


def extend_own(x_size, y_size, dual, vel, grad, fluid, state, coef):
    planes = x_size + 2

    def copy_own(i, _):
        for x in range(x_size):
            state[i * planes + x + 1, pl.ds(PAD, y_size), :] = dual[i * x_size + x]
        return 0

    lax.fori_loop(0, POPS, copy_own, 0)

    def own_coefficients(x, _):
        there = fluid[x].astype(jnp.float32) + 1.0
        values = coefficients(there, vel[x], vel[x_size + x], vel[2 * x_size + x], grad[x])
        for n, value in enumerate(values):
            coef[n * x_size + x, pl.ds(PAD, y_size), :] = value
        return 0

    lax.fori_loop(0, x_size, own_coefficients, 0)


def extend_rims(x_size, y_size, messages, state, coef):
    pitch = y_size + 2 * PAD
    planes = x_size + 2
    lanes = state.shape[-1]
    flat = state.reshape(state.shape[0] * pitch, lanes)
    coef_flat = coef.reshape(coef.shape[0] * pitch, lanes)
    for after, ref in zip(toward_next("blk"), messages):
        places = {d: jnp.where(after, PAD + y_size - 1 + d, PAD - d) for d in (1, 2, 3)}
        side = {}
        for k, (kind, i, distance) in enumerate(rim_entries()):
            value = ref[pl.ds(k * x_size, x_size), :]
            if kind == 0:
                pop = pick(after, i, mirrored(i, 1))
                at = (pop * planes + 1) * pitch + places[distance]
                flat[pl.ds(at, x_size, stride=pitch), :] = value
            else:
                side[(kind, i, distance)] = value
        for d in (1, 2):
            values = [side[key, n, d] for key, n in ((2, 0), (1, 0), (1, 1), (1, 2), (3, 0))]
            for n, value in enumerate(coefficients(*values)):
                coef_flat[pl.ds(n * x_size * pitch + places[d], x_size, stride=pitch), :] = value


def rim_kernel(x_size, y_size, *refs):
    sources, messages, held, arrived = refs[:4], (refs[5], refs[4]), refs[6:10], refs[10]
    copies = [pltpu.make_async_copy(a, b, arrived.at[n]) for n, (a, b) in enumerate(zip(sources, held))]
    for copy in copies:
        copy.start()
    for copy in copies:
        copy.wait()
    dual, vel, grad, fluid = held
    lanes = dual.shape[-1]
    flat = [ref.reshape(ref.shape[0] * y_size, lanes) for ref in (dual, vel, fluid, grad)]
    for after, out in zip(toward_next("blk"), messages):
        for k, (kind, i, distance) in enumerate(rim_entries()):
            row = jnp.where(after, y_size - distance, distance - 1)
            field = pick(after, mirrored(i, 1), i) if kind == 0 else i
            value = flat[kind][pl.ds(field * x_size * y_size + row, x_size, stride=y_size), :]
            if kind == 2:
                value = value.astype(jnp.float32) + 1.0
            out[pl.ds(k * x_size, x_size), :] = value


def edge_steps(x_size, after, state, coef, near, far, raw, first, second, put):
    known = RIGHT + LEVEL
    planes = x_size + 2
    inward = jnp.where(after, -1, 1)
    plane = jnp.where(after, x_size - 1, 0)
    turn = jnp.where(after, -1.0, 1.0)

    def coefs(x, at):
        return [coef[n * x_size + x, pl.ds(at, 8), :] for n in range(6)]

    def read_state(x, at):
        def read(i):
            cx, cy, _ = VELOCITIES[i]
            pop = pick(after, mirrored(i, 0), i)
            return state[pop * planes + x + 1 + cx * inward, pl.ds(at + cy, 8), :]

        return read

    for at in raw:
        for n, i in enumerate(RIGHT):
            pop = pick(after, mirrored(i, 0), i)
            put(0, n, at, state[pop * planes + plane + 1, pl.ds(at, 8), :])
    for at in first:
        keep, rate, *u, source = coefs(plane, at)
        for n, value in enumerate((rate, *u)):
            put(3, n, at, value)
        u[0] = turn * u[0]
        p = pulled_from(read_state(plane, at), known)
        _, equilib = relaxed(p, u)
        posts = posts_of(p, keep, equilib, rate, source, known)
        for n, i in enumerate(RIGHT):
            put(1, n, at, posts[i])
        for n, i in enumerate(LEVEL):
            near[n, pl.ds(at, 8), :] = posts[i]
        keep, rate, *u, source = coefs(plane + inward, at)
        u[0] = turn * u[0]
        p = pulled_from(read_state(plane + inward, at), range(POPS))
        _, equilib = relaxed(p, u)
        posts = posts_of(p, keep, equilib, rate, source, RIGHT)
        for n, i in enumerate(RIGHT):
            far[n, pl.ds(at, 8), :] = posts[i]
    for at in second:
        keep, rate, *u, source = coefs(plane, at)
        u[0] = turn * u[0]

        def read(i):
            ref, n = (far, RIGHT.index(i)) if i in RIGHT else (near, LEVEL.index(i))
            return ref[n, pl.ds(at + VELOCITIES[i][1], 8), :]

        p = pulled_from(read, known)
        _, equilib = relaxed(p, u)
        posts = posts_of(p, keep, equilib, rate, source, RIGHT)
        for n, i in enumerate(RIGHT):
            put(2, n, at, posts[i])


EARLY = (0, 5, 10, 15)


def early_kernel(x_size, y_size, dual, vel, grad, fluid, early_b, early_a, state, coef, near, far):
    extend_own(x_size, y_size, dual, vel, grad, fluid, state, coef)
    rows = range(PAD, PAD + y_size, 8)
    for after, out in zip(toward_next("grp"), (early_a, early_b)):

        def put(kind, n, at, value, out=out):
            out[pl.ds((EARLY[kind] + n) * y_size + at - PAD, 8), :] = value

        edge_steps(x_size, after, state, coef, near, far, rows, rows, rows, put)


def late_pieces(y_size):
    pieces, offset = {}, 0
    for end in (0, 1):
        for kind, count, reach in ((0, 5, 3), (1, 5, 2), (2, 5, 1), (3, 4, 2)):
            rows = 2 if kind == 3 else 3
            begin = PAD + y_size + reach - rows if end else PAD - reach
            pieces[kind, end] = (begin, rows, offset)
            offset += count * rows
    return pieces, -(-offset // 8) * 8


def late_kernel(x_size, y_size, dual, vel, grad, fluid, rim_b, rim_a, late_b, late_a, state, coef, near, far):
    extend_own(x_size, y_size, dual, vel, grad, fluid, state, coef)
    extend_rims(x_size, y_size, (rim_a, rim_b), state, coef)
    pieces, _ = late_pieces(y_size)
    starts = [(PAD - reach, PAD + y_size + reach - 8) for reach in (3, 2, 1)]
    for after, out in zip(toward_next("grp"), (late_a, late_b)):

        def put(kind, n, at, value, out=out):
            begin, rows, offset = pieces[kind, 1 if at > PAD else 0]
            out[pl.ds(offset + n * rows, rows), :] = value[begin - at : begin - at + rows]

        edge_steps(x_size, after, state, coef, near, far, *starts, put)


def steps_kernel(
    x_size, y_size, dual, vel, grad, fluid, rim_b, rim_a, heat, early_b, early_a, late_b, late_a,
    sens, state, coef, later, shifts, extra, halos,
):
    extend_own(x_size, y_size, dual, vel, grad, fluid, state, coef)
    extend_rims(x_size, y_size, (rim_a, rim_b), state, coef)
    planes = x_size + 2
    window = y_size + 8
    groups = window // 8
    afters = toward_next("grp")
    pieces, _ = late_pieces(y_size)

    for side, (after, early, late) in enumerate(zip(afters, (early_a, early_b), (late_a, late_b))):
        halo = jnp.where(after, x_size + 1, 0)
        for kind, count in enumerate((5, 5, 5, 4)):
            for n in range(count):
                if kind == 0:
                    ref, plane = state, pick(after, RIGHT[n], mirrored(RIGHT[n], 0)) * planes + halo
                else:
                    ref, plane = halos, side * 14 + EARLY[kind] - 5 + n
                ref[plane, pl.ds(PAD, y_size), :] = early[pl.ds((EARLY[kind] + n) * y_size, y_size), :]
                for end in (0, 1):
                    begin, rows, offset = pieces[kind, end]
                    ref[plane, pl.ds(begin, rows), :] = late[pl.ds(offset + n * rows, rows), :]

    def read_from(source, x, at):
        def read(i):
            cx, cy, _ = VELOCITIES[i]
            return source[i * planes + x + 1 + cx, pl.ds(at + cy, 8), :]

        return read

    def step(number, source, target):
        def plane(x, _):
            for j in range(groups):
                at = FIRST + 8 * j
                keep, rate, *u, drive = [coef[n * x_size + x, pl.ds(at, 8), :] for n in range(6)]
                p = pulled_from(read_from(source, x, at), range(POPS))
                shift, equilib = relaxed(p, u)
                shifts[(number - 1) * x_size + x, pl.ds(at, 8), :] = shift
                posts = posts_of(p, keep, equilib, rate, drive, range(POPS))
                for i in range(POPS):
                    target[i * planes + x + 1, pl.ds(at, 8), :] = posts[i]
            return 0

        lax.fori_loop(0, x_size, plane, 0, unroll=True)
        for side, after in enumerate(afters):
            halo = jnp.where(after, x_size + 1, 0)
            edge = jnp.where(after, x_size, 1)
            turn = jnp.where(after, 1.0, -1.0)
            for j in range(groups):
                at = FIRST + 8 * j
                rate, *u = [halos[side * 14 + 10 + n, pl.ds(at, 8), :] for n in range(4)]
                u[0] = turn * u[0]

                def read(i):
                    cy = VELOCITIES[i][1]
                    if i in LEFT:
                        return source[pick(after, i, mirrored(i, 0)) * planes + edge, pl.ds(at + cy, 8), :]
                    return extra[side, pl.ds(at + cy, 8), :]

                p = pulled_from(read, LEFT if number == 1 else LEFT + LEVEL)
                added = rate * relaxed(p, u)[1]
                if number == 1:
                    extra[side, pl.ds(at, 8), :] = added
                for n, i in enumerate(RIGHT):
                    target[pick(after, i, mirrored(i, 0)) * planes + halo, pl.ds(at, 8), :] = (
                        halos[side * 14 + 5 * number - 5 + n, pl.ds(at, 8), :] + added
                    )

    step(1, state, later)
    step(2, later, state)

    def last(x, _):
        for j in range(y_size // 8):
            at = PAD + 8 * j
            u = [coef[n * x_size + x, pl.ds(at, 8), :] for n in (2, 3, 4)]
            p = pulled_from(read_from(state, x, at), range(1, POPS))
            shift = relaxed(p, u)[0]
            shift = shifts[x, pl.ds(at, 8), :] + shifts[x_size + x, pl.ds(at, 8), :] + shift
            sens[x, pl.ds(8 * j, 8), :] = heat[x, pl.ds(8 * j, 8), :] * shift
        return 0

    lax.fori_loop(0, x_size, last, 0, unroll=True)


def adjoint_kernel(x_size, y_size, state, coef, adjoint):
    planes = x_size + 2

    def plane(x, _):
        for j in range(y_size // 8):
            at = PAD + 8 * j
            keep, rate, *u, drive = [coef[n * x_size + x, pl.ds(at, 8), :] for n in range(6)]

            def read(i):
                cx, cy, _ = VELOCITIES[i]
                return state[i * planes + x + 1 + cx, pl.ds(at + cy, 8), :]

            p = pulled_from(read, range(POPS))
            posts = posts_of(p, keep, relaxed(p, u)[1], rate, drive, range(POPS))
            for i in range(POPS):
                adjoint[i * x_size + x, pl.ds(8 * j, 8), :] = posts[i]
        return 0

    lax.fori_loop(0, x_size, plane, 0, unroll=True)


def diamond(x_size, reach):
    pieces, offset = [], 0
    for slot in range(3):
        for k in range(x_size if slot == 0 else min(x_size, reach - 1)):
            rows = reach if slot == 0 else reach - 1 - k
            pieces.append((slot, k, rows, offset))
            offset += rows
    return pieces, -(-offset // 8) * 8


def slot_plane(x_size, slot, k):
    if slot == 0:
        return x_size + k, k
    after = toward_next("grp")[slot - 1]
    return jnp.where(after, 2 * x_size + k, x_size - 1 - k), jnp.where(after, k, x_size - 1 - k)


def band_kernel(x_size, y_size, own, beside_b, beside_a, span, span_b, span_a, band_b, band_a):
    pieces, skip = diamond(x_size, REACH)
    for after, out in zip(toward_next("blk"), (band_a, band_b)):
        for refs, reach, base in (((own, beside_a, beside_b), REACH, 0), ((span, span_a, span_b), REACH - 1, skip)):
            for slot, k, rows, offset in diamond(x_size, reach)[0]:
                _, plane = slot_plane(x_size, slot, k)
                value = refs[slot][plane, pl.ds(jnp.where(after, y_size - rows, 0), rows), :]
                out[pl.ds(base + offset, rows), :] = value.astype(jnp.float32)


def shares(span, inside):
    r2 = jnp.where(span < 0.5, 0.25, jnp.where(span < 1.5, 1.0, jnp.where(span < 2.5, 4.0, 16.0)))
    share = 1.0 / (1.0 + 6.0 * r2)
    return share, jnp.where(inside, r2 * share, 0.0)


def slot_inside(slot):
    if slot == 0:
        return True
    after = toward_next("grp")[slot - 1]
    me, size = lax.axis_index("grp"), lax.axis_size("grp")
    return jnp.where(after, me < size - 1, me > 0)


def radius_kernel(x_size, y_size, span, span_b, span_a, inverse, beta):
    for slot, ref in enumerate((span, span_a, span_b)):
        inside = slot_inside(slot)

        def plane(x, _, slot=slot, ref=ref, inside=inside):
            place, k = slot_plane(x_size, slot, x)
            inverse[place], beta[place] = shares(ref[k].astype(jnp.float32), inside)
            return 0

        lax.fori_loop(0, x_size, plane, 0, unroll=4)


def filter_kernel(
    x_size, y_size, own, beside_b, beside_a, band_b, band_a, inverse, own_beta, filtered, first, second, given, beta
):
    rows = y_size + 2 * REACH
    for x in range(x_size):
        for slot, ref in enumerate((own, beside_a, beside_b)):
            place, plane = slot_plane(x_size, slot, x)
            s = ref[plane]
            first[place, pl.ds(PAD + REACH, y_size), :] = s
            given[place, pl.ds(REACH, y_size), :] = s * inverse[place]
            beta[place, pl.ds(REACH, y_size), :] = own_beta[place]
    pieces, skip = diamond(x_size, REACH)
    radii = {(slot, k): (rows, skip + offset) for slot, k, rows, offset in diamond(x_size, REACH - 1)[0]}
    me, size = lax.axis_index("blk"), lax.axis_size("blk")
    for after, ref in zip(toward_next("blk"), (band_a, band_b)):
        there = jnp.where(after, me < size - 1, me > 0)
        for slot, k, count, offset in pieces:
            place, _ = slot_plane(x_size, slot, k)
            at = jnp.where(after, REACH + y_size, REACH - count)
            s = ref[pl.ds(offset, count), :]
            first[place, pl.ds(PAD + at, count), :] = s
            if (slot, k) in radii:
                count, offset = radii[slot, k]
                at = jnp.where(after, REACH + y_size, REACH - count)
                inside = jnp.logical_and(there, slot_inside(slot))
                share, beta[place, pl.ds(at, count), :] = shares(ref[pl.ds(offset, count), :], inside)
                given[place, pl.ds(at, count), :] = first[place, pl.ds(PAD + at, count), :] * share
    source, target = first, second
    for number in range(1, SWEEPS + 1):
        final = number == SWEEPS
        margin = SWEEPS - number

        for j in range(1, 1 + y_size // 8) if final else range(rows // 8):
            at = PAD + 8 * j
            begin, end = x_size - margin, 2 * x_size + margin
            column = {x: source[x, pl.ds(at, 8), :] for x in range(begin - 1, end + 1)}
            for x in range(begin, end):
                beside = column[x + 1] + column[x - 1]
                beside = beside + source[x, pl.ds(at + 1, 8), :] + source[x, pl.ds(at - 1, 8), :]
                beside = beside + lane_pull(column[x], 1) + lane_pull(column[x], -1)
                value = given[x, pl.ds(8 * j, 8), :] + beta[x, pl.ds(8 * j, 8), :] * beside
                if final:
                    filtered[x - x_size, pl.ds(8 * j - REACH, 8), :] = value
                else:
                    target[x, pl.ds(at, 8), :] = value
        source, target = target, source


def call(kernel, outs, scratch, args, name, place=pltpu.VMEM, grant=32):
    return pl.pallas_call(
        kernel,
        out_shape=[jax.ShapeDtypeStruct(shape, jnp.float32) for shape in outs],
        in_specs=[pl.BlockSpec(memory_space=place)] * len(args),
        out_specs=[pl.BlockSpec(memory_space=pltpu.VMEM)] * len(outs),
        scratch_shapes=[pltpu.VMEM(s, jnp.float32) if isinstance(s, tuple) else s for s in scratch],
        compiler_params=pltpu.CompilerParams(vmem_limit_bytes=grant * 1024 * 1024),
        name=name,
    )(*args)


def swapped(axis, message_b, message_a):
    size = lax.axis_size(axis)
    received = []
    for begin, message in ((1, message_b), (0, message_a)):
        pairs = [(i, i + 1) for i in range(begin, size - 1, 2)]
        received.append(lax.ppermute(message, axis, pairs + [(j, i) for i, j in pairs]))
    return received


def on_device(dual_populace, forward_motion_vector, forward_heat_level, objective_heat_gradient, liquid_indicator,
              filter_span_group):
    _, x_size, y_size, lanes = dual_populace.shape
    planes, pitch = x_size + 2, y_size + 2 * PAD
    sizes = (x_size, y_size)
    dual = dual_populace.reshape(POPS * x_size, y_size, lanes)
    vel = forward_motion_vector.reshape(3 * x_size, y_size, lanes)
    fields = (dual, vel, objective_heat_gradient, liquid_indicator)
    rim = (len(rim_entries()) * x_size, lanes)
    state = (POPS * planes, pitch, lanes)
    coef = (6 * x_size, pitch, lanes)
    edge_scratch = [state, coef, (len(LEVEL), pitch, lanes), (len(RIGHT), pitch, lanes)]

    spans = swapped("grp", filter_span_group, filter_span_group)
    rims = call(
        functools.partial(rim_kernel, *sizes),
        [rim, rim],
        [pltpu.VMEM(f.shape, f.dtype) for f in fields] + [pltpu.SemaphoreType.DMA((len(fields),))],
        fields,
        "rim_rows",
        pltpu.HBM,
        63,
    )
    rims = swapped("blk", *rims)
    early = (EDGES * y_size, lanes)
    earlies = call(
        functools.partial(early_kernel, *sizes),
        [early, early],
        edge_scratch,
        fields,
        "edges_early",
    )
    earlies = swapped("grp", *earlies)
    late = (late_pieces(y_size)[1], lanes)
    lates = call(functools.partial(late_kernel, *sizes), [late, late], edge_scratch, (*fields, *rims), "edges_late")
    lates = swapped("grp", *lates)
    sens, state_2, coefs = call(
        functools.partial(steps_kernel, *sizes),
        [(x_size, y_size, lanes), state, coef],
        [state, (2 * x_size, pitch, lanes), (2, pitch, lanes), (28, pitch, lanes)],
        (*fields, *rims, forward_heat_level, *earlies, *lates),
        "two_steps_and_sens",
    )
    beside = swapped("grp", sens, sens)
    (adjoint,) = call(
        functools.partial(adjoint_kernel, *sizes), [(POPS * x_size, y_size, lanes)], [], (state_2, coefs), "third_step"
    )
    inverse, beta = call(
        functools.partial(radius_kernel, *sizes), [(3 * x_size, y_size, lanes)] * 2, [], (filter_span_group, *spans), "radius"
    )
    band = (diamond(x_size, REACH)[1] + diamond(x_size, REACH - 1)[1], lanes)
    bands = call(
        functools.partial(band_kernel, *sizes), [band, band], [], (sens, *beside, filter_span_group, *spans), "bands"
    )
    bands = swapped("blk", *bands)
    wide, rows = 3 * x_size, y_size + 2 * REACH
    (filtered,) = call(
        functools.partial(filter_kernel, *sizes),
        [(x_size, y_size, lanes)],
        [(wide, rows + 2 * PAD, lanes)] * 2 + [(wide, rows, lanes)] * 2,
        (sens, *beside, *bands, inverse, beta),
        "eight_sweeps",
    )
    return adjoint.reshape(dual_populace.shape), filtered


def solution(mesh):
    in_specs = (
        P(None, "grp", "blk", None),
        P(None, "grp", "blk", None),
        P("grp", "blk", None),
        P("grp", "blk", None),
        P("grp", "blk", None),
        P("grp", "blk", None),
    )
    out_specs = (P(None, "grp", "blk", None), P("grp", "blk", None))
    return jax.shard_map(
        on_device, mesh=mesh, in_specs=in_specs, out_specs=out_specs, check_vma=False
    )
```

```python
import functools

import jax
import jax.numpy as jnp
from jax import lax
from jax.experimental import pallas as pl
from jax.experimental.pallas import tpu as pltpu
from jax.sharding import PartitionSpec as P

SWEEPS = 8
REACH = 8

VELOCITIES = (
    (0, 0, 0),
    (1, 0, 0),
    (-1, 0, 0),
    (0, 1, 0),
    (0, -1, 0),
    (0, 0, 1),
    (0, 0, -1),
    (1, 1, 0),
    (-1, -1, 0),
    (1, -1, 0),
    (-1, 1, 0),
    (1, 0, 1),
    (-1, 0, -1),
    (1, 0, -1),
    (-1, 0, 1),
    (0, 1, 1),
    (0, -1, -1),
    (0, 1, -1),
    (0, -1, 1),
)
POPS = 19
SHARE = 1.0 / 36.0
MULTIPLE = (12.0,) + (2.0,) * 6 + (1.0,) * 12
RIGHT = tuple(i for i in range(POPS) if VELOCITIES[i][0] == 1)
LEFT = tuple(i for i in range(POPS) if VELOCITIES[i][0] == -1)
LEVEL = tuple(i for i in range(POPS) if VELOCITIES[i][0] == 0)
PAD = 8
FIRST = 5
EDGES = 19


def rim_entries():
    entries = [(0, i, 1) for i in range(POPS)]
    entries += [(0, i, 2) for i in range(POPS) if VELOCITIES[i][1] != -1]
    entries += [(0, i, 3) for i in range(POPS) if VELOCITIES[i][1] == 1]
    for distance in (1, 2):
        entries += [(1, i, distance) for i in range(3)]
        entries += [(2, 0, distance), (3, 0, distance)]
    return entries


def mirrored(i, axis):
    velocity = list(VELOCITIES[i])
    velocity[axis] = -velocity[axis]
    return VELOCITIES.index(tuple(velocity))


def pick(condition, a, b):
    return a if a == b else jnp.where(condition, a, b)


def toward_next(axis):
    even = lax.axis_index(axis) % 2 == 0
    return even, jnp.logical_not(even)


def lane_pull(v, cz):
    if cz == 0:
        return v
    lanes = v.shape[-1]
    lane = lax.broadcasted_iota(jnp.int32, v.shape, 1)
    if cz == 1:
        return jnp.where(lane != lanes - 1, pltpu.roll(v, lanes - 1, 1), 0.0)
    return jnp.where(lane != 0, pltpu.roll(v, 1, 1), 0.0)


def total(terms):
    terms = [t for t in terms if t is not None]
    return functools.reduce(lambda a, b: a + b, terms) if terms else None


def scaled(v, factor):
    return None if v is None else factor * v


def negated(v):
    return None if v is None else -v


def moments(p):
    s, d = {}, {}
    for i in range(1, POPS, 2):
        a, b = p[i], p[i + 1]
        s[i] = total([a, b])
        d[i] = a - b if a is not None and b is not None else (a if b is None else negated(b))
    average = total(
        [scaled(p[0], 12.0), scaled(total([s[1], s[3], s[5]]), 2.0)] + [s[i] for i in (7, 9, 11, 13, 15, 17)]
    )
    along_x = total([scaled(d[1], 2.0), d[7], d[9], d[11], d[13]])
    along_y = total([scaled(d[3], 2.0), d[7], negated(d[9]), d[15], d[17]])
    along_z = total([scaled(d[5], 2.0), d[11], negated(d[13]), d[15], negated(d[17])])
    return average, (along_x, along_y, along_z)


def relaxed(p, u):
    average, along = moments(p)
    shift = total([u[k] * along[k] for k in range(3) if along[k] is not None])
    return shift, SHARE * average + shift


def pulled_from(read, pops):
    p = [None] * POPS
    for i in pops:
        p[i] = lane_pull(read(i), VELOCITIES[i][2])
    return p


def posts_of(p, keep, equilib, rate, source, pops):
    base = rate * equilib
    terms = {m: base + (source if m == 1.0 else m * source) for m in (12.0, 2.0, 1.0)}
    return {i: keep * p[i] + terms[MULTIPLE[i]] for i in pops}


def coefficients(there, ux, uy, uz, g):
    inside = there > 0.5
    wet = jnp.where(inside, there - 1.0, 0.0)
    keep = jnp.where(inside, 0.1 - 0.7 * wet, 0.0)
    rate = jnp.where(inside, 0.9 + 0.7 * wet, 0.0)
    scale = (3.0 * SHARE) * wet
    return keep, rate, scale * ux, scale * uy, scale * uz, SHARE * g


def extend_own(x_size, y_size, dual, vel, grad, fluid, state, coef):
    planes = x_size + 2

    def copy_own(i, _):
        for x in range(x_size):
            state[i * planes + x + 1, pl.ds(PAD, y_size), :] = dual[i * x_size + x]
        return 0

    lax.fori_loop(0, POPS, copy_own, 0)

    def own_coefficients(x, _):
        there = fluid[x].astype(jnp.float32) + 1.0
        values = coefficients(there, vel[x], vel[x_size + x], vel[2 * x_size + x], grad[x])
        for n, value in enumerate(values):
            coef[n * x_size + x, pl.ds(PAD, y_size), :] = value
        return 0

    lax.fori_loop(0, x_size, own_coefficients, 0)


def extend_rims(x_size, y_size, messages, state, coef):
    pitch = y_size + 2 * PAD
    planes = x_size + 2
    lanes = state.shape[-1]
    flat = state.reshape(state.shape[0] * pitch, lanes)
    coef_flat = coef.reshape(coef.shape[0] * pitch, lanes)
    for after, ref in zip(toward_next("blk"), messages):
        places = {d: jnp.where(after, PAD + y_size - 1 + d, PAD - d) for d in (1, 2, 3)}
        side = {}
        for k, (kind, i, distance) in enumerate(rim_entries()):
            value = ref[pl.ds(k * x_size, x_size), :]
            if kind == 0:
                pop = pick(after, i, mirrored(i, 1))
                at = (pop * planes + 1) * pitch + places[distance]
                flat[pl.ds(at, x_size, stride=pitch), :] = value
            else:
                side[(kind, i, distance)] = value
        for d in (1, 2):
            values = [side[key, n, d] for key, n in ((2, 0), (1, 0), (1, 1), (1, 2), (3, 0))]
            for n, value in enumerate(coefficients(*values)):
                coef_flat[pl.ds(n * x_size * pitch + places[d], x_size, stride=pitch), :] = value


def rim_kernel(x_size, y_size, *refs):
    sources, messages, held, arrived = refs[:4], (refs[5], refs[4]), refs[6:10], refs[10]
    copies = [pltpu.make_async_copy(a, b, arrived.at[n]) for n, (a, b) in enumerate(zip(sources, held))]
    for copy in copies:
        copy.start()
    for copy in copies:
        copy.wait()
    dual, vel, grad, fluid = held
    lanes = dual.shape[-1]
    flat = [ref.reshape(ref.shape[0] * y_size, lanes) for ref in (dual, vel, fluid, grad)]
    for after, out in zip(toward_next("blk"), messages):
        for k, (kind, i, distance) in enumerate(rim_entries()):
            row = jnp.where(after, y_size - distance, distance - 1)
            field = pick(after, mirrored(i, 1), i) if kind == 0 else i
            value = flat[kind][pl.ds(field * x_size * y_size + row, x_size, stride=y_size), :]
            if kind == 2:
                value = value.astype(jnp.float32) + 1.0
            out[pl.ds(k * x_size, x_size), :] = value


def edge_steps(x_size, after, state, coef, near, far, raw, first, second, put):
    known = RIGHT + LEVEL
    planes = x_size + 2
    inward = jnp.where(after, -1, 1)
    plane = jnp.where(after, x_size - 1, 0)
    turn = jnp.where(after, -1.0, 1.0)

    def coefs(x, at):
        return [coef[n * x_size + x, pl.ds(at, 8), :] for n in range(6)]

    def read_state(x, at):
        def read(i):
            cx, cy, _ = VELOCITIES[i]
            pop = pick(after, mirrored(i, 0), i)
            return state[pop * planes + x + 1 + cx * inward, pl.ds(at + cy, 8), :]

        return read

    for at in raw:
        for n, i in enumerate(RIGHT):
            pop = pick(after, mirrored(i, 0), i)
            put(0, n, at, state[pop * planes + plane + 1, pl.ds(at, 8), :])
    for at in first:
        keep, rate, *u, source = coefs(plane, at)
        for n, value in enumerate((rate, *u)):
            put(3, n, at, value)
        u[0] = turn * u[0]
        p = pulled_from(read_state(plane, at), known)
        _, equilib = relaxed(p, u)
        posts = posts_of(p, keep, equilib, rate, source, known)
        for n, i in enumerate(RIGHT):
            put(1, n, at, posts[i])
        for n, i in enumerate(LEVEL):
            near[n, pl.ds(at, 8), :] = posts[i]
        keep, rate, *u, source = coefs(plane + inward, at)
        u[0] = turn * u[0]
        p = pulled_from(read_state(plane + inward, at), range(POPS))
        _, equilib = relaxed(p, u)
        posts = posts_of(p, keep, equilib, rate, source, RIGHT)
        for n, i in enumerate(RIGHT):
            far[n, pl.ds(at, 8), :] = posts[i]
    for at in second:
        keep, rate, *u, source = coefs(plane, at)
        u[0] = turn * u[0]

        def read(i):
            ref, n = (far, RIGHT.index(i)) if i in RIGHT else (near, LEVEL.index(i))
            return ref[n, pl.ds(at + VELOCITIES[i][1], 8), :]

        p = pulled_from(read, known)
        _, equilib = relaxed(p, u)
        posts = posts_of(p, keep, equilib, rate, source, RIGHT)
        for n, i in enumerate(RIGHT):
            put(2, n, at, posts[i])


EARLY = (0, 5, 10, 15)


def early_kernel(x_size, y_size, dual, vel, grad, fluid, early_b, early_a, state, coef, near, far):
    extend_own(x_size, y_size, dual, vel, grad, fluid, state, coef)
    rows = range(PAD, PAD + y_size, 8)
    for after, out in zip(toward_next("grp"), (early_a, early_b)):

        def put(kind, n, at, value, out=out):
            out[pl.ds((EARLY[kind] + n) * y_size + at - PAD, 8), :] = value

        edge_steps(x_size, after, state, coef, near, far, rows, rows, rows, put)


def late_pieces(y_size):
    pieces, offset = {}, 0
    for end in (0, 1):
        for kind, count, reach in ((0, 5, 3), (1, 5, 2), (2, 5, 1), (3, 4, 2)):
            rows = 2 if kind == 3 else 3
            begin = PAD + y_size + reach - rows if end else PAD - reach
            pieces[kind, end] = (begin, rows, offset)
            offset += count * rows
    return pieces, -(-offset // 8) * 8


def late_kernel(x_size, y_size, dual, vel, grad, fluid, rim_b, rim_a, late_b, late_a, state, coef, near, far):
    extend_own(x_size, y_size, dual, vel, grad, fluid, state, coef)
    extend_rims(x_size, y_size, (rim_a, rim_b), state, coef)
    pieces, _ = late_pieces(y_size)
    starts = [(PAD - reach, PAD + y_size + reach - 8) for reach in (3, 2, 1)]
    for after, out in zip(toward_next("grp"), (late_a, late_b)):

        def put(kind, n, at, value, out=out):
            begin, rows, offset = pieces[kind, 1 if at > PAD else 0]
            out[pl.ds(offset + n * rows, rows), :] = value[begin - at : begin - at + rows]

        edge_steps(x_size, after, state, coef, near, far, *starts, put)


def steps_kernel(
    x_size, y_size, dual, vel, grad, fluid, rim_b, rim_a, heat, early_b, early_a, late_b, late_a,
    sens, state, coef, later, shifts, extra, halos,
):
    extend_own(x_size, y_size, dual, vel, grad, fluid, state, coef)
    extend_rims(x_size, y_size, (rim_a, rim_b), state, coef)
    planes = x_size + 2
    window = y_size + 8
    groups = window // 8
    afters = toward_next("grp")
    pieces, _ = late_pieces(y_size)

    for side, (after, early, late) in enumerate(zip(afters, (early_a, early_b), (late_a, late_b))):
        halo = jnp.where(after, x_size + 1, 0)
        for kind, count in enumerate((5, 5, 5, 4)):
            for n in range(count):
                if kind == 0:
                    ref, plane = state, pick(after, RIGHT[n], mirrored(RIGHT[n], 0)) * planes + halo
                else:
                    ref, plane = halos, side * 14 + EARLY[kind] - 5 + n
                ref[plane, pl.ds(PAD, y_size), :] = early[pl.ds((EARLY[kind] + n) * y_size, y_size), :]
                for end in (0, 1):
                    begin, rows, offset = pieces[kind, end]
                    ref[plane, pl.ds(begin, rows), :] = late[pl.ds(offset + n * rows, rows), :]

    def read_from(source, x, at):
        def read(i):
            cx, cy, _ = VELOCITIES[i]
            return source[i * planes + x + 1 + cx, pl.ds(at + cy, 8), :]

        return read

    def step(number, source, target):
        def plane(x, _):
            for j in range(groups):
                at = FIRST + 8 * j
                keep, rate, *u, drive = [coef[n * x_size + x, pl.ds(at, 8), :] for n in range(6)]
                p = pulled_from(read_from(source, x, at), range(POPS))
                shift, equilib = relaxed(p, u)
                shifts[(number - 1) * x_size + x, pl.ds(at, 8), :] = shift
                posts = posts_of(p, keep, equilib, rate, drive, range(POPS))
                for i in range(POPS):
                    target[i * planes + x + 1, pl.ds(at, 8), :] = posts[i]
            return 0

        lax.fori_loop(0, x_size, plane, 0, unroll=True)
        for side, after in enumerate(afters):
            halo = jnp.where(after, x_size + 1, 0)
            edge = jnp.where(after, x_size, 1)
            turn = jnp.where(after, 1.0, -1.0)
            for j in range(groups):
                at = FIRST + 8 * j
                rate, *u = [halos[side * 14 + 10 + n, pl.ds(at, 8), :] for n in range(4)]
                u[0] = turn * u[0]

                def read(i):
                    cy = VELOCITIES[i][1]
                    if i in LEFT:
                        return source[pick(after, i, mirrored(i, 0)) * planes + edge, pl.ds(at + cy, 8), :]
                    return extra[side, pl.ds(at + cy, 8), :]

                p = pulled_from(read, LEFT if number == 1 else LEFT + LEVEL)
                added = rate * relaxed(p, u)[1]
                if number == 1:
                    extra[side, pl.ds(at, 8), :] = added
                for n, i in enumerate(RIGHT):
                    target[pick(after, i, mirrored(i, 0)) * planes + halo, pl.ds(at, 8), :] = (
                        halos[side * 14 + 5 * number - 5 + n, pl.ds(at, 8), :] + added
                    )

    step(1, state, later)
    step(2, later, state)

    def last(x, _):
        for j in range(y_size // 8):
            at = PAD + 8 * j
            u = [coef[n * x_size + x, pl.ds(at, 8), :] for n in (2, 3, 4)]
            p = pulled_from(read_from(state, x, at), range(1, POPS))
            shift = relaxed(p, u)[0]
            shift = shifts[x, pl.ds(at, 8), :] + shifts[x_size + x, pl.ds(at, 8), :] + shift
            sens[x, pl.ds(8 * j, 8), :] = heat[x, pl.ds(8 * j, 8), :] * shift
        return 0

    lax.fori_loop(0, x_size, last, 0, unroll=True)


def adjoint_kernel(x_size, y_size, state, coef, adjoint):
    planes = x_size + 2

    def plane(x, _):
        for j in range(y_size // 8):
            at = PAD + 8 * j
            keep, rate, *u, drive = [coef[n * x_size + x, pl.ds(at, 8), :] for n in range(6)]

            def read(i):
                cx, cy, _ = VELOCITIES[i]
                return state[i * planes + x + 1 + cx, pl.ds(at + cy, 8), :]

            p = pulled_from(read, range(POPS))
            posts = posts_of(p, keep, relaxed(p, u)[1], rate, drive, range(POPS))
            for i in range(POPS):
                adjoint[i * x_size + x, pl.ds(8 * j, 8), :] = posts[i]
        return 0

    lax.fori_loop(0, x_size, plane, 0, unroll=True)


def diamond(x_size, reach):
    pieces, offset = [], 0
    for slot in range(3):
        for k in range(x_size if slot == 0 else min(x_size, reach - 1)):
            rows = reach if slot == 0 else reach - 1 - k
            pieces.append((slot, k, rows, offset))
            offset += rows
    return pieces, -(-offset // 8) * 8


def slot_plane(x_size, slot, k):
    if slot == 0:
        return x_size + k, k
    after = toward_next("grp")[slot - 1]
    return jnp.where(after, 2 * x_size + k, x_size - 1 - k), jnp.where(after, k, x_size - 1 - k)


def band_kernel(x_size, y_size, own, beside_b, beside_a, span, span_b, span_a, band_b, band_a):
    pieces, skip = diamond(x_size, REACH)
    for after, out in zip(toward_next("blk"), (band_a, band_b)):
        for refs, reach, base in (((own, beside_a, beside_b), REACH, 0), ((span, span_a, span_b), REACH - 1, skip)):
            for slot, k, rows, offset in diamond(x_size, reach)[0]:
                _, plane = slot_plane(x_size, slot, k)
                value = refs[slot][plane, pl.ds(jnp.where(after, y_size - rows, 0), rows), :]
                out[pl.ds(base + offset, rows), :] = value.astype(jnp.float32)


def shares(span, inside):
    r2 = jnp.where(span < 0.5, 0.25, jnp.where(span < 1.5, 1.0, jnp.where(span < 2.5, 4.0, 16.0)))
    share = 1.0 / (1.0 + 6.0 * r2)
    return share, jnp.where(inside, r2 * share, 0.0)


def slot_inside(slot):
    if slot == 0:
        return True
    after = toward_next("grp")[slot - 1]
    me, size = lax.axis_index("grp"), lax.axis_size("grp")
    return jnp.where(after, me < size - 1, me > 0)


def radius_kernel(x_size, y_size, span, span_b, span_a, inverse, beta):
    for slot, ref in enumerate((span, span_a, span_b)):
        inside = slot_inside(slot)

        def plane(x, _, slot=slot, ref=ref, inside=inside):
            place, k = slot_plane(x_size, slot, x)
            inverse[place], beta[place] = shares(ref[k].astype(jnp.float32), inside)
            return 0

        lax.fori_loop(0, x_size, plane, 0, unroll=4)


def filter_kernel(
    x_size, y_size, own, beside_b, beside_a, band_b, band_a, inverse, own_beta, filtered, first, second, given, beta
):
    rows = y_size + 2 * REACH
    for x in range(x_size):
        for slot, ref in enumerate((own, beside_a, beside_b)):
            place, plane = slot_plane(x_size, slot, x)
            s = ref[plane]
            first[place, pl.ds(PAD + REACH, y_size), :] = s
            given[place, pl.ds(REACH, y_size), :] = s * inverse[place]
            beta[place, pl.ds(REACH, y_size), :] = own_beta[place]
    pieces, skip = diamond(x_size, REACH)
    radii = {(slot, k): (rows, skip + offset) for slot, k, rows, offset in diamond(x_size, REACH - 1)[0]}
    me, size = lax.axis_index("blk"), lax.axis_size("blk")
    for after, ref in zip(toward_next("blk"), (band_a, band_b)):
        there = jnp.where(after, me < size - 1, me > 0)
        for slot, k, count, offset in pieces:
            place, _ = slot_plane(x_size, slot, k)
            at = jnp.where(after, REACH + y_size, REACH - count)
            s = ref[pl.ds(offset, count), :]
            first[place, pl.ds(PAD + at, count), :] = s
            if (slot, k) in radii:
                count, offset = radii[slot, k]
                at = jnp.where(after, REACH + y_size, REACH - count)
                inside = jnp.logical_and(there, slot_inside(slot))
                share, beta[place, pl.ds(at, count), :] = shares(ref[pl.ds(offset, count), :], inside)
                given[place, pl.ds(at, count), :] = first[place, pl.ds(PAD + at, count), :] * share
    source, target = first, second
    for number in range(1, SWEEPS + 1):
        final = number == SWEEPS
        margin = SWEEPS - number

        for j in range(1, 1 + y_size // 8) if final else range(rows // 8):
            at = PAD + 8 * j
            begin, end = x_size - margin, 2 * x_size + margin
            column = {x: source[x, pl.ds(at, 8), :] for x in range(begin - 1, end + 1)}
            for x in range(begin, end):
                beside = column[x + 1] + column[x - 1]
                beside = beside + source[x, pl.ds(at + 1, 8), :] + source[x, pl.ds(at - 1, 8), :]
                beside = beside + lane_pull(column[x], 1) + lane_pull(column[x], -1)
                value = given[x, pl.ds(8 * j, 8), :] + beta[x, pl.ds(8 * j, 8), :] * beside
                if final:
                    filtered[x - x_size, pl.ds(8 * j - REACH, 8), :] = value
                else:
                    target[x, pl.ds(at, 8), :] = value
        source, target = target, source


def call(kernel, outs, scratch, args, name, place=pltpu.VMEM, grant=32):
    return pl.pallas_call(
        kernel,
        out_shape=[jax.ShapeDtypeStruct(shape, jnp.float32) for shape in outs],
        in_specs=[pl.BlockSpec(memory_space=place)] * len(args),
        out_specs=[pl.BlockSpec(memory_space=pltpu.VMEM)] * len(outs),
        scratch_shapes=[pltpu.VMEM(s, jnp.float32) if isinstance(s, tuple) else s for s in scratch],
        compiler_params=pltpu.CompilerParams(vmem_limit_bytes=grant * 1024 * 1024),
        name=name,
    )(*args)


def swapped(axis, message_b, message_a):
    size = lax.axis_size(axis)
    received = []
    for begin, message in ((1, message_b), (0, message_a)):
        pairs = [(i, i + 1) for i in range(begin, size - 1, 2)]
        received.append(lax.ppermute(message, axis, pairs + [(j, i) for i, j in pairs]))
    return received


def on_device(dual_populace, forward_motion_vector, forward_heat_level, objective_heat_gradient, liquid_indicator,
              filter_span_group):
    _, x_size, y_size, lanes = dual_populace.shape
    planes, pitch = x_size + 2, y_size + 2 * PAD
    sizes = (x_size, y_size)
    dual = dual_populace.reshape(POPS * x_size, y_size, lanes)
    vel = forward_motion_vector.reshape(3 * x_size, y_size, lanes)
    fields = (dual, vel, objective_heat_gradient, liquid_indicator)
    rim = (len(rim_entries()) * x_size, lanes)
    state = (POPS * planes, pitch, lanes)
    coef = (6 * x_size, pitch, lanes)
    edge_scratch = [state, coef, (len(LEVEL), pitch, lanes), (len(RIGHT), pitch, lanes)]

    spans = swapped("grp", filter_span_group, filter_span_group)
    rims = call(
        functools.partial(rim_kernel, *sizes),
        [rim, rim],
        [pltpu.VMEM(f.shape, f.dtype) for f in fields] + [pltpu.SemaphoreType.DMA((len(fields),))],
        fields,
        "rim_rows",
        pltpu.HBM,
        62,
    )
    rims = swapped("blk", *rims)
    early = (EDGES * y_size, lanes)
    earlies = call(
        functools.partial(early_kernel, *sizes),
        [early, early],
        edge_scratch,
        fields,
        "edges_early",
    )
    earlies = swapped("grp", *earlies)
    rims, spans = lax.optimization_barrier((rims, spans))
    late = (late_pieces(y_size)[1], lanes)
    lates = call(functools.partial(late_kernel, *sizes), [late, late], edge_scratch, (*fields, *rims), "edges_late")
    lates = swapped("grp", *lates)
    sens, state_2, coefs = call(
        functools.partial(steps_kernel, *sizes),
        [(x_size, y_size, lanes), state, coef],
        [state, (2 * x_size, pitch, lanes), (2, pitch, lanes), (28, pitch, lanes)],
        (*fields, *rims, forward_heat_level, *earlies, *lates),
        "two_steps_and_sens",
    )
    beside = swapped("grp", sens, sens)
    (adjoint,) = call(
        functools.partial(adjoint_kernel, *sizes), [(POPS * x_size, y_size, lanes)], [], (state_2, coefs), "third_step"
    )
    inverse, beta = call(
        functools.partial(radius_kernel, *sizes), [(3 * x_size, y_size, lanes)] * 2, [], (filter_span_group, *spans), "radius"
    )
    band = (diamond(x_size, REACH)[1] + diamond(x_size, REACH - 1)[1], lanes)
    bands = call(
        functools.partial(band_kernel, *sizes), [band, band], [], (sens, *beside, filter_span_group, *spans), "bands"
    )
    bands = swapped("blk", *bands)
    wide, rows = 3 * x_size, y_size + 2 * REACH
    (filtered,) = call(
        functools.partial(filter_kernel, *sizes),
        [(x_size, y_size, lanes)],
        [(wide, rows + 2 * PAD, lanes)] * 2 + [(wide, rows, lanes)] * 2,
        (sens, *beside, *bands, inverse, beta),
        "eight_sweeps",
    )
    return adjoint.reshape(dual_populace.shape), filtered


def solution(mesh):
    in_specs = (
        P(None, "grp", "blk", None),
        P(None, "grp", "blk", None),
        P("grp", "blk", None),
        P("grp", "blk", None),
        P("grp", "blk", None),
        P("grp", "blk", None),
    )
    out_specs = (P(None, "grp", "blk", None), P("grp", "blk", None))
    return jax.shard_map(
        on_device, mesh=mesh, in_specs=in_specs, out_specs=out_specs, check_vma=False
    )
```

```python
import functools

import jax
import jax.numpy as jnp
from jax import lax
from jax.experimental import pallas as pl
from jax.experimental.pallas import tpu as pltpu
from jax.sharding import PartitionSpec as P

SWEEPS = 8
REACH = 8

VELOCITIES = (
    (0, 0, 0),
    (1, 0, 0),
    (-1, 0, 0),
    (0, 1, 0),
    (0, -1, 0),
    (0, 0, 1),
    (0, 0, -1),
    (1, 1, 0),
    (-1, -1, 0),
    (1, -1, 0),
    (-1, 1, 0),
    (1, 0, 1),
    (-1, 0, -1),
    (1, 0, -1),
    (-1, 0, 1),
    (0, 1, 1),
    (0, -1, -1),
    (0, 1, -1),
    (0, -1, 1),
)
POPS = 19
SHARE = 1.0 / 36.0
MULTIPLE = (12.0,) + (2.0,) * 6 + (1.0,) * 12
RIGHT = tuple(i for i in range(POPS) if VELOCITIES[i][0] == 1)
LEFT = tuple(i for i in range(POPS) if VELOCITIES[i][0] == -1)
LEVEL = tuple(i for i in range(POPS) if VELOCITIES[i][0] == 0)
PAD = 8
FIRST = 5
EDGES = 19


def rim_entries():
    entries = [(0, i, 1) for i in range(POPS)]
    entries += [(0, i, 2) for i in range(POPS) if VELOCITIES[i][1] != -1]
    entries += [(0, i, 3) for i in range(POPS) if VELOCITIES[i][1] == 1]
    for distance in (1, 2):
        entries += [(1, i, distance) for i in range(3)]
        entries += [(2, 0, distance), (3, 0, distance)]
    return entries


def mirrored(i, axis):
    velocity = list(VELOCITIES[i])
    velocity[axis] = -velocity[axis]
    return VELOCITIES.index(tuple(velocity))


def pick(condition, a, b):
    return a if a == b else jnp.where(condition, a, b)


def toward_next(axis):
    even = lax.axis_index(axis) % 2 == 0
    return even, jnp.logical_not(even)


def lane_pull(v, cz):
    if cz == 0:
        return v
    lanes = v.shape[-1]
    lane = lax.broadcasted_iota(jnp.int32, v.shape, 1)
    if cz == 1:
        return jnp.where(lane != lanes - 1, pltpu.roll(v, lanes - 1, 1), 0.0)
    return jnp.where(lane != 0, pltpu.roll(v, 1, 1), 0.0)


def total(terms):
    terms = [t for t in terms if t is not None]
    return functools.reduce(lambda a, b: a + b, terms) if terms else None


def scaled(v, factor):
    return None if v is None else factor * v


def negated(v):
    return None if v is None else -v


def moments(p):
    s, d = {}, {}
    for i in range(1, POPS, 2):
        a, b = p[i], p[i + 1]
        s[i] = total([a, b])
        d[i] = a - b if a is not None and b is not None else (a if b is None else negated(b))
    average = total(
        [scaled(p[0], 12.0), scaled(total([s[1], s[3], s[5]]), 2.0)] + [s[i] for i in (7, 9, 11, 13, 15, 17)]
    )
    along_x = total([scaled(d[1], 2.0), d[7], d[9], d[11], d[13]])
    along_y = total([scaled(d[3], 2.0), d[7], negated(d[9]), d[15], d[17]])
    along_z = total([scaled(d[5], 2.0), d[11], negated(d[13]), d[15], negated(d[17])])
    return average, (along_x, along_y, along_z)


def relaxed(p, u):
    average, along = moments(p)
    shift = total([u[k] * along[k] for k in range(3) if along[k] is not None])
    return shift, SHARE * average + shift


def pulled_from(read, pops):
    p = [None] * POPS
    for i in pops:
        p[i] = lane_pull(read(i), VELOCITIES[i][2])
    return p


def posts_of(p, keep, equilib, rate, source, pops):
    base = rate * equilib
    terms = {m: base + (source if m == 1.0 else m * source) for m in (12.0, 2.0, 1.0)}
    return {i: keep * p[i] + terms[MULTIPLE[i]] for i in pops}


def coefficients(there, ux, uy, uz, g):
    inside = there > 0.5
    wet = jnp.where(inside, there - 1.0, 0.0)
    keep = jnp.where(inside, 0.1 - 0.7 * wet, 0.0)
    rate = jnp.where(inside, 0.9 + 0.7 * wet, 0.0)
    scale = (3.0 * SHARE) * wet
    return keep, rate, scale * ux, scale * uy, scale * uz, SHARE * g


def extend_own(x_size, y_size, dual, vel, grad, fluid, state, coef):
    planes = x_size + 2

    def copy_own(i, _):
        for x in range(x_size):
            state[i * planes + x + 1, pl.ds(PAD, y_size), :] = dual[i * x_size + x]
        return 0

    lax.fori_loop(0, POPS, copy_own, 0)

    def own_coefficients(x, _):
        there = fluid[x].astype(jnp.float32) + 1.0
        values = coefficients(there, vel[x], vel[x_size + x], vel[2 * x_size + x], grad[x])
        for n, value in enumerate(values):
            coef[n * x_size + x, pl.ds(PAD, y_size), :] = value
        return 0

    lax.fori_loop(0, x_size, own_coefficients, 0)


def extend_rims(x_size, y_size, messages, state, coef):
    pitch = y_size + 2 * PAD
    planes = x_size + 2
    lanes = state.shape[-1]
    flat = state.reshape(state.shape[0] * pitch, lanes)
    coef_flat = coef.reshape(coef.shape[0] * pitch, lanes)
    for after, ref in zip(toward_next("blk"), messages):
        places = {d: jnp.where(after, PAD + y_size - 1 + d, PAD - d) for d in (1, 2, 3)}
        side = {}
        for k, (kind, i, distance) in enumerate(rim_entries()):
            value = ref[pl.ds(k * x_size, x_size), :]
            if kind == 0:
                pop = pick(after, i, mirrored(i, 1))
                at = (pop * planes + 1) * pitch + places[distance]
                flat[pl.ds(at, x_size, stride=pitch), :] = value
            else:
                side[(kind, i, distance)] = value
        for d in (1, 2):
            values = [side[key, n, d] for key, n in ((2, 0), (1, 0), (1, 1), (1, 2), (3, 0))]
            for n, value in enumerate(coefficients(*values)):
                coef_flat[pl.ds(n * x_size * pitch + places[d], x_size, stride=pitch), :] = value


def rim_kernel(x_size, y_size, *refs):
    sources, (b, a, state, coef, heat, radii), held, arrived = refs[:6], refs[6:12], refs[12:17], refs[17]
    messages = (a, b)
    copies = [pltpu.make_async_copy(a, b, arrived.at[n]) for n, (a, b) in enumerate(zip(sources, (*held, heat)))]
    for copy in copies:
        copy.start()
    for copy in copies:
        copy.wait()
    dual, vel, grad, fluid, span = held
    lanes = dual.shape[-1]
    flat = [ref.reshape(ref.shape[0] * y_size, lanes) for ref in (dual, vel, fluid, grad)]
    for after, out in zip(toward_next("blk"), messages):
        for k, (kind, i, distance) in enumerate(rim_entries()):
            row = jnp.where(after, y_size - distance, distance - 1)
            field = pick(after, mirrored(i, 1), i) if kind == 0 else i
            value = flat[kind][pl.ds(field * x_size * y_size + row, x_size, stride=y_size), :]
            if kind == 2:
                value = value.astype(jnp.float32) + 1.0
            out[pl.ds(k * x_size, x_size), :] = value
    extend_own(x_size, y_size, dual, vel, grad, fluid, state, coef)
    for x in range(x_size):
        radii[x] = span[x].astype(jnp.float32)


def edge_steps(x_size, after, state, coef, near, far, raw, first, second, put):
    known = RIGHT + LEVEL
    planes = x_size + 2
    inward = jnp.where(after, -1, 1)
    plane = jnp.where(after, x_size - 1, 0)
    turn = jnp.where(after, -1.0, 1.0)

    def coefs(x, at):
        return [coef[n * x_size + x, pl.ds(at, 8), :] for n in range(6)]

    def read_state(x, at):
        def read(i):
            cx, cy, _ = VELOCITIES[i]
            pop = pick(after, mirrored(i, 0), i)
            return state[pop * planes + x + 1 + cx * inward, pl.ds(at + cy, 8), :]

        return read

    for at in raw:
        for n, i in enumerate(RIGHT):
            pop = pick(after, mirrored(i, 0), i)
            put(0, n, at, state[pop * planes + plane + 1, pl.ds(at, 8), :])
    for at in first:
        keep, rate, *u, source = coefs(plane, at)
        for n, value in enumerate((rate, *u)):
            put(3, n, at, value)
        u[0] = turn * u[0]
        p = pulled_from(read_state(plane, at), known)
        _, equilib = relaxed(p, u)
        posts = posts_of(p, keep, equilib, rate, source, known)
        for n, i in enumerate(RIGHT):
            put(1, n, at, posts[i])
        for n, i in enumerate(LEVEL):
            near[n, pl.ds(at, 8), :] = posts[i]
        keep, rate, *u, source = coefs(plane + inward, at)
        u[0] = turn * u[0]
        p = pulled_from(read_state(plane + inward, at), range(POPS))
        _, equilib = relaxed(p, u)
        posts = posts_of(p, keep, equilib, rate, source, RIGHT)
        for n, i in enumerate(RIGHT):
            far[n, pl.ds(at, 8), :] = posts[i]
    for at in second:
        keep, rate, *u, source = coefs(plane, at)
        u[0] = turn * u[0]

        def read(i):
            ref, n = (far, RIGHT.index(i)) if i in RIGHT else (near, LEVEL.index(i))
            return ref[n, pl.ds(at + VELOCITIES[i][1], 8), :]

        p = pulled_from(read, known)
        _, equilib = relaxed(p, u)
        posts = posts_of(p, keep, equilib, rate, source, RIGHT)
        for n, i in enumerate(RIGHT):
            put(2, n, at, posts[i])


EARLY = (0, 5, 10, 15)


def early_kernel(x_size, y_size, state, coef, span, early_b, early_a, near, far):
    rows = range(PAD, PAD + y_size, 8)
    for after, out in zip(toward_next("grp"), (early_a, early_b)):

        def put(kind, n, at, value, out=out):
            out[pl.ds((EARLY[kind] + n) * y_size + at - PAD, 8), :] = value

        edge_steps(x_size, after, state, coef, near, far, rows, rows, rows, put)
        for x in range(x_size):
            out[pl.ds((EDGES + x) * y_size, y_size), :] = span[x]


def late_pieces(y_size):
    pieces, offset = {}, 0
    for end in (0, 1):
        for kind, count, reach in ((0, 5, 3), (1, 5, 2), (2, 5, 1), (3, 4, 2)):
            rows = 2 if kind == 3 else 3
            begin = PAD + y_size + reach - rows if end else PAD - reach
            pieces[kind, end] = (begin, rows, offset)
            offset += count * rows
    return pieces, -(-offset // 8) * 8


def late_kernel(x_size, y_size, _state, _coef, rim_b, rim_a, late_b, late_a, state, coef, near, far):
    extend_rims(x_size, y_size, (rim_a, rim_b), state, coef)
    pieces, _ = late_pieces(y_size)
    starts = [(PAD - reach, PAD + y_size + reach - 8) for reach in (3, 2, 1)]
    for after, out in zip(toward_next("grp"), (late_a, late_b)):

        def put(kind, n, at, value, out=out):
            begin, rows, offset = pieces[kind, 1 if at > PAD else 0]
            out[pl.ds(offset + n * rows, rows), :] = value[begin - at : begin - at + rows]

        edge_steps(x_size, after, state, coef, near, far, *starts, put)


def step_plane(x_size, y_size, number, x, source, target, coef, shifts):
    planes = x_size + 2
    for j in range((y_size + 8) // 8):
        at = FIRST + 8 * j
        keep, rate, *u, drive = [coef[n * x_size + x, pl.ds(at, 8), :] for n in range(6)]
        p = pulled_from(reader(planes, source, x, at), range(POPS))
        shift, equilib = relaxed(p, u)
        shifts[(number - 1) * x_size + x, pl.ds(at, 8), :] = shift
        posts = posts_of(p, keep, equilib, rate, drive, range(POPS))
        for i in range(POPS):
            target[i * planes + x + 1, pl.ds(at, 8), :] = posts[i]


def reader(planes, source, x, at):
    def read(i):
        cx, cy, _ = VELOCITIES[i]
        return source[i * planes + x + 1 + cx, pl.ds(at + cy, 8), :]

    return read


def sens_plane(x_size, y_size, x, state, coef, shifts, heat, sens):
    for j in range(y_size // 8):
        at = PAD + 8 * j
        u = [coef[n * x_size + x, pl.ds(at, 8), :] for n in (2, 3, 4)]
        p = pulled_from(reader(x_size + 2, state, x, at), range(1, POPS))
        shift = shifts[x, pl.ds(at, 8), :] + shifts[x_size + x, pl.ds(at, 8), :] + relaxed(p, u)[0]
        sens[x, pl.ds(8 * j, 8), :] = heat[x, pl.ds(8 * j, 8), :] * shift


def inner_kernel(x_size, y_size, state, coef, heat, state_1, state_2, shifts, sens):
    for x in range(1, x_size - 1):
        step_plane(x_size, y_size, 1, x, state, state_1, coef, shifts)
    for x in range(2, x_size - 2):
        step_plane(x_size, y_size, 2, x, state_1, state_2, coef, shifts)
    for x in range(3, x_size - 3):
        sens_plane(x_size, y_size, x, state_2, coef, shifts, heat, sens)


def outer_kernel(
    x_size, y_size, coef, heat, early_b, early_a, late_b, late_a, _state, _state_1, _state_2, _shifts, _sens,
    state, state_1, state_2, shifts, sens, extra, halos,
):
    planes = x_size + 2
    window = y_size + 8
    groups = window // 8
    afters = toward_next("grp")
    pieces, _ = late_pieces(y_size)

    for side, (after, early, late) in enumerate(zip(afters, (early_a, early_b), (late_a, late_b))):
        halo = jnp.where(after, x_size + 1, 0)
        for kind, count in enumerate((5, 5, 5, 4)):
            for n in range(count):
                if kind == 0:
                    ref, plane = state, pick(after, RIGHT[n], mirrored(RIGHT[n], 0)) * planes + halo
                else:
                    ref, plane = halos, side * 14 + EARLY[kind] - 5 + n
                ref[plane, pl.ds(PAD, y_size), :] = early[pl.ds((EARLY[kind] + n) * y_size, y_size), :]
                for end in (0, 1):
                    begin, rows, offset = pieces[kind, end]
                    ref[plane, pl.ds(begin, rows), :] = late[pl.ds(offset + n * rows, rows), :]

    for number, source, target in ((1, state, state_1), (2, state_1, state_2)):
        for x in (*range(number), *range(x_size - number, x_size)):
            step_plane(x_size, y_size, number, x, source, target, coef, shifts)
        for side, after in enumerate(afters):
            halo = jnp.where(after, x_size + 1, 0)
            edge = jnp.where(after, x_size, 1)
            turn = jnp.where(after, 1.0, -1.0)
            for j in range(groups):
                at = FIRST + 8 * j
                rate, *u = [halos[side * 14 + 10 + n, pl.ds(at, 8), :] for n in range(4)]
                u[0] = turn * u[0]

                def read(i):
                    cy = VELOCITIES[i][1]
                    if i in LEFT:
                        return source[pick(after, i, mirrored(i, 0)) * planes + edge, pl.ds(at + cy, 8), :]
                    return extra[side, pl.ds(at + cy, 8), :]

                p = pulled_from(read, LEFT if number == 1 else LEFT + LEVEL)
                added = rate * relaxed(p, u)[1]
                if number == 1:
                    extra[side, pl.ds(at, 8), :] = added
                for n, i in enumerate(RIGHT):
                    target[pick(after, i, mirrored(i, 0)) * planes + halo, pl.ds(at, 8), :] = (
                        halos[side * 14 + 5 * number - 5 + n, pl.ds(at, 8), :] + added
                    )
    for x in (*range(3), *range(x_size - 3, x_size)):
        sens_plane(x_size, y_size, x, state_2, coef, shifts, heat, sens)


def adjoint_kernel(x_size, y_size, state, coef, adjoint):
    planes = x_size + 2

    def plane(x, _):
        for j in range(y_size // 8):
            at = PAD + 8 * j
            keep, rate, *u, drive = [coef[n * x_size + x, pl.ds(at, 8), :] for n in range(6)]

            def read(i):
                cx, cy, _ = VELOCITIES[i]
                return state[i * planes + x + 1 + cx, pl.ds(at + cy, 8), :]

            p = pulled_from(read, range(POPS))
            posts = posts_of(p, keep, relaxed(p, u)[1], rate, drive, range(POPS))
            for i in range(POPS):
                adjoint[i * x_size + x, pl.ds(8 * j, 8), :] = posts[i]
        return 0

    lax.fori_loop(0, x_size, plane, 0, unroll=True)


def diamond(x_size, reach):
    pieces, offset = [], 0
    for slot in range(3):
        for k in range(x_size if slot == 0 else min(x_size, reach - 1)):
            rows = reach if slot == 0 else reach - 1 - k
            pieces.append((slot, k, rows, offset))
            offset += rows
    return pieces, -(-offset // 8) * 8


def slot_plane(x_size, slot, k):
    if slot == 0:
        return x_size + k, k
    after = toward_next("grp")[slot - 1]
    return jnp.where(after, 2 * x_size + k, x_size - 1 - k), jnp.where(after, k, x_size - 1 - k)


def band_kernel(x_size, y_size, own, beside_b, beside_a, span, span_b, span_a, band_b, band_a):
    pieces, skip = diamond(x_size, REACH)
    for after, out in zip(toward_next("blk"), (band_a, band_b)):
        for refs, reach, base in (((own, beside_a, beside_b), REACH, 0), ((span, span_a, span_b), REACH - 1, skip)):
            for slot, k, rows, offset in diamond(x_size, reach)[0]:
                _, plane = slot_plane(x_size, slot, k)
                plane = plane + EDGES if slot > 0 and base > 0 else plane
                value = refs[slot][plane, pl.ds(jnp.where(after, y_size - rows, 0), rows), :]
                out[pl.ds(base + offset, rows), :] = value.astype(jnp.float32)


def shares(span, inside):
    r2 = jnp.where(span < 0.5, 0.25, jnp.where(span < 1.5, 1.0, jnp.where(span < 2.5, 4.0, 16.0)))
    share = 1.0 / (1.0 + 6.0 * r2)
    return share, jnp.where(inside, r2 * share, 0.0)


def slot_inside(slot):
    if slot == 0:
        return True
    after = toward_next("grp")[slot - 1]
    me, size = lax.axis_index("grp"), lax.axis_size("grp")
    return jnp.where(after, me < size - 1, me > 0)


def radius_kernel(x_size, y_size, span, span_b, span_a, inverse, beta):
    for slot, ref in enumerate((span, span_a, span_b)):
        inside = slot_inside(slot)

        def plane(x, _, slot=slot, ref=ref, inside=inside):
            place, k = slot_plane(x_size, slot, x)
            inverse[place], beta[place] = shares(ref[k if slot == 0 else EDGES + k].astype(jnp.float32), inside)
            return 0

        lax.fori_loop(0, x_size, plane, 0, unroll=4)


def filter_kernel(
    x_size, y_size, own, beside_b, beside_a, band_b, band_a, inverse, own_beta, filtered, first, second, given, beta
):
    rows = y_size + 2 * REACH
    for x in range(x_size):
        for slot, ref in enumerate((own, beside_a, beside_b)):
            place, plane = slot_plane(x_size, slot, x)
            s = ref[plane]
            first[place, pl.ds(PAD + REACH, y_size), :] = s
            given[place, pl.ds(REACH, y_size), :] = s * inverse[place]
            beta[place, pl.ds(REACH, y_size), :] = own_beta[place]
    pieces, skip = diamond(x_size, REACH)
    radii = {(slot, k): (rows, skip + offset) for slot, k, rows, offset in diamond(x_size, REACH - 1)[0]}
    me, size = lax.axis_index("blk"), lax.axis_size("blk")
    for after, ref in zip(toward_next("blk"), (band_a, band_b)):
        there = jnp.where(after, me < size - 1, me > 0)
        for slot, k, count, offset in pieces:
            place, _ = slot_plane(x_size, slot, k)
            at = jnp.where(after, REACH + y_size, REACH - count)
            s = ref[pl.ds(offset, count), :]
            first[place, pl.ds(PAD + at, count), :] = s
            if (slot, k) in radii:
                count, offset = radii[slot, k]
                at = jnp.where(after, REACH + y_size, REACH - count)
                inside = jnp.logical_and(there, slot_inside(slot))
                share, beta[place, pl.ds(at, count), :] = shares(ref[pl.ds(offset, count), :], inside)
                given[place, pl.ds(at, count), :] = first[place, pl.ds(PAD + at, count), :] * share
    source, target = first, second
    for number in range(1, SWEEPS + 1):
        final = number == SWEEPS
        margin = SWEEPS - number

        for j in range(1, 1 + y_size // 8) if final else range(rows // 8):
            at = PAD + 8 * j
            begin, end = x_size - margin, 2 * x_size + margin
            column = {x: source[x, pl.ds(at, 8), :] for x in range(begin - 1, end + 1)}
            for x in range(begin, end):
                beside = column[x + 1] + column[x - 1]
                beside = beside + source[x, pl.ds(at + 1, 8), :] + source[x, pl.ds(at - 1, 8), :]
                beside = beside + lane_pull(column[x], 1) + lane_pull(column[x], -1)
                value = given[x, pl.ds(8 * j, 8), :] + beta[x, pl.ds(8 * j, 8), :] * beside
                if final:
                    filtered[x - x_size, pl.ds(8 * j - REACH, 8), :] = value
                else:
                    target[x, pl.ds(at, 8), :] = value
        source, target = target, source


def call(kernel, outs, scratch, args, name, place=pltpu.VMEM, in_place=()):
    return pl.pallas_call(
        kernel,
        out_shape=[jax.ShapeDtypeStruct(shape, jnp.float32) for shape in outs],
        in_specs=[pl.BlockSpec(memory_space=place)] * len(args),
        out_specs=[pl.BlockSpec(memory_space=pltpu.VMEM)] * len(outs),
        scratch_shapes=[pltpu.VMEM(s, jnp.float32) if isinstance(s, tuple) else s for s in scratch],
        compiler_params=pltpu.CompilerParams(vmem_limit_bytes=32 * 1024 * 1024),
        input_output_aliases=dict(in_place),
        name=name,
    )(*args)


def swapped(axis, message_b, message_a):
    size = lax.axis_size(axis)
    received = []
    for begin, message in ((1, message_b), (0, message_a)):
        pairs = [(i, i + 1) for i in range(begin, size - 1, 2)]
        received.append(lax.ppermute(message, axis, pairs + [(j, i) for i, j in pairs]))
    return received


def on_device(dual_populace, forward_motion_vector, forward_heat_level, objective_heat_gradient, liquid_indicator,
              filter_span_group):
    _, x_size, y_size, lanes = dual_populace.shape
    planes, pitch = x_size + 2, y_size + 2 * PAD
    sizes = (x_size, y_size)
    dual = dual_populace.reshape(POPS * x_size, y_size, lanes)
    vel = forward_motion_vector.reshape(3 * x_size, y_size, lanes)
    fields = (dual, vel, objective_heat_gradient, liquid_indicator)
    rim = (len(rim_entries()) * x_size, lanes)
    state = (POPS * planes, pitch, lanes)
    coef = (6 * x_size, pitch, lanes)
    edge_scratch = [state, coef, (len(LEVEL), pitch, lanes), (len(RIGHT), pitch, lanes)]

    own = (x_size, y_size, lanes)
    fields = (*fields, filter_span_group, forward_heat_level)
    *rims, state_0, coefs, heat, span = call(
        functools.partial(rim_kernel, *sizes),
        [rim, rim, state, coef, own, own],
        [pltpu.VMEM(f.shape, f.dtype) for f in fields[:-1]] + [pltpu.SemaphoreType.DMA((len(fields),))],
        [pltpu.with_memory_space_constraint(f, pltpu.HBM) for f in fields],
        "rim_rows",
        pltpu.HBM,
    )
    rims = swapped("blk", *rims)
    early = ((EDGES + x_size) * y_size, lanes)
    near_far = [(len(LEVEL), pitch, lanes), (len(RIGHT), pitch, lanes)]
    earlies = call(
        functools.partial(early_kernel, *sizes),
        [early, early],
        near_far,
        (state_0, coefs, span),
        "edges_early",
    )
    earlies = swapped("grp", *earlies)
    late = (late_pieces(y_size)[1], lanes)
    *lates, state_0, coefs = call(
        functools.partial(late_kernel, *sizes),
        [late, late, state, coef],
        near_far,
        (state_0, coefs, *rims),
        "edges_late",
        in_place=((0, 2), (1, 3)),
    )
    lates = swapped("grp", *lates)
    shifts = (2 * x_size, pitch, lanes)
    inner = call(
        functools.partial(inner_kernel, *sizes),
        [state, state, shifts, own],
        [],
        (state_0, coefs, heat),
        "steps_inside",
    )
    _, _, state_2, _, sens = call(
        functools.partial(outer_kernel, *sizes),
        [state, state, state, shifts, own],
        [(2, pitch, lanes), (28, pitch, lanes)],
        (coefs, heat, *earlies, *lates, state_0, *inner),
        "steps_at_edges",
        in_place=((6, 0), (7, 1), (8, 2), (9, 3), (10, 4)),
    )
    spans = [e.reshape(EDGES + x_size, y_size, lanes) for e in earlies]
    beside = swapped("grp", sens, sens)
    (adjoint,) = call(
        functools.partial(adjoint_kernel, *sizes), [(POPS * x_size, y_size, lanes)], [], (state_2, coefs), "third_step"
    )
    inverse, beta = call(
        functools.partial(radius_kernel, *sizes), [(3 * x_size, y_size, lanes)] * 2, [], (span, *spans), "radius"
    )
    band = (diamond(x_size, REACH)[1] + diamond(x_size, REACH - 1)[1], lanes)
    bands = call(
        functools.partial(band_kernel, *sizes), [band, band], [], (sens, *beside, span, *spans), "bands"
    )
    bands = swapped("blk", *bands)
    wide, rows = 3 * x_size, y_size + 2 * REACH
    (filtered,) = call(
        functools.partial(filter_kernel, *sizes),
        [(x_size, y_size, lanes)],
        [(wide, rows + 2 * PAD, lanes)] * 2 + [(wide, rows, lanes)] * 2,
        (sens, *beside, *bands, inverse, beta),
        "eight_sweeps",
    )
    return adjoint.reshape(dual_populace.shape), filtered


def solution(mesh):
    in_specs = (
        P(None, "grp", "blk", None),
        P(None, "grp", "blk", None),
        P("grp", "blk", None),
        P("grp", "blk", None),
        P("grp", "blk", None),
        P("grp", "blk", None),
    )
    out_specs = (P(None, "grp", "blk", None), P("grp", "blk", None))
    return jax.shard_map(
        on_device, mesh=mesh, in_specs=in_specs, out_specs=out_specs, check_vma=False
    )
```

```python
import functools

import jax
import jax.numpy as jnp
from jax import lax
from jax.experimental import pallas as pl
from jax.experimental.pallas import tpu as pltpu
from jax.sharding import PartitionSpec as P

SWEEPS = 8
REACH = 8

VELOCITIES = (
    (0, 0, 0),
    (1, 0, 0),
    (-1, 0, 0),
    (0, 1, 0),
    (0, -1, 0),
    (0, 0, 1),
    (0, 0, -1),
    (1, 1, 0),
    (-1, -1, 0),
    (1, -1, 0),
    (-1, 1, 0),
    (1, 0, 1),
    (-1, 0, -1),
    (1, 0, -1),
    (-1, 0, 1),
    (0, 1, 1),
    (0, -1, -1),
    (0, 1, -1),
    (0, -1, 1),
)
POPS = 19
SHARE = 1.0 / 36.0
MULTIPLE = (12.0,) + (2.0,) * 6 + (1.0,) * 12
RIGHT = tuple(i for i in range(POPS) if VELOCITIES[i][0] == 1)
LEFT = tuple(i for i in range(POPS) if VELOCITIES[i][0] == -1)
LEVEL = tuple(i for i in range(POPS) if VELOCITIES[i][0] == 0)
PAD = 8
FIRST = 5


def rim_entries():
    entries = [(0, i, 1) for i in range(POPS)]
    entries += [(0, i, 2) for i in range(POPS) if VELOCITIES[i][1] != -1]
    entries += [(0, i, 3) for i in range(POPS) if VELOCITIES[i][1] == 1]
    for distance in (1, 2):
        entries += [(1, i, distance) for i in range(3)]
        entries += [(2, 0, distance), (3, 0, distance)]
    return entries


def mirrored(i, axis):
    velocity = list(VELOCITIES[i])
    velocity[axis] = -velocity[axis]
    return VELOCITIES.index(tuple(velocity))


def pick(condition, a, b):
    return a if a == b else jnp.where(condition, a, b)


def toward_next(axis):
    even = lax.axis_index(axis) % 2 == 0
    return even, jnp.logical_not(even)


def lane_pull(v, cz):
    if cz == 0:
        return v
    lanes = v.shape[-1]
    lane = lax.broadcasted_iota(jnp.int32, v.shape, 1)
    if cz == 1:
        return jnp.where(lane != lanes - 1, pltpu.roll(v, lanes - 1, 1), 0.0)
    return jnp.where(lane != 0, pltpu.roll(v, 1, 1), 0.0)


def total(terms):
    terms = [t for t in terms if t is not None]
    return functools.reduce(lambda a, b: a + b, terms) if terms else None


def scaled(v, factor):
    return None if v is None else factor * v


def negated(v):
    return None if v is None else -v


def moments(p):
    s, d = {}, {}
    for i in range(1, POPS, 2):
        a, b = p[i], p[i + 1]
        s[i] = total([a, b])
        d[i] = a - b if a is not None and b is not None else (a if b is None else negated(b))
    average = total(
        [scaled(p[0], 12.0), scaled(total([s[1], s[3], s[5]]), 2.0)] + [s[i] for i in (7, 9, 11, 13, 15, 17)]
    )
    along_x = total([scaled(d[1], 2.0), d[7], d[9], d[11], d[13]])
    along_y = total([scaled(d[3], 2.0), d[7], negated(d[9]), d[15], d[17]])
    along_z = total([scaled(d[5], 2.0), d[11], negated(d[13]), d[15], negated(d[17])])
    return average, (along_x, along_y, along_z)


def relaxed(p, u):
    average, along = moments(p)
    shift = total([u[k] * along[k] for k in range(3) if along[k] is not None])
    return shift, SHARE * average + shift


def pulled_from(read, pops):
    p = [None] * POPS
    for i in pops:
        p[i] = lane_pull(read(i), VELOCITIES[i][2])
    return p


def posts_of(p, keep, equilib, rate, source, pops):
    base = rate * equilib
    terms = {m: base + (source if m == 1.0 else m * source) for m in (12.0, 2.0, 1.0)}
    return {i: keep * p[i] + terms[MULTIPLE[i]] for i in pops}


def coefficients(there, ux, uy, uz, g):
    inside = there > 0.5
    wet = jnp.where(inside, there - 1.0, 0.0)
    keep = jnp.where(inside, 0.1 - 0.7 * wet, 0.0)
    rate = jnp.where(inside, 0.9 + 0.7 * wet, 0.0)
    scale = (3.0 * SHARE) * wet
    return keep, rate, scale * ux, scale * uy, scale * uz, SHARE * g


def extend_own(x_size, y_size, dual, vel, grad, fluid, state, coef):
    planes = x_size + 2

    def copy_own(i, _):
        for x in range(x_size):
            state[i * planes + x + 1, pl.ds(PAD, y_size), :] = dual[i * x_size + x]
        return 0

    lax.fori_loop(0, POPS, copy_own, 0)

    def own_coefficients(x, _):
        there = fluid[x].astype(jnp.float32) + 1.0
        values = coefficients(there, vel[x], vel[x_size + x], vel[2 * x_size + x], grad[x])
        for n, value in enumerate(values):
            coef[n * x_size + x, pl.ds(PAD, y_size), :] = value
        return 0

    lax.fori_loop(0, x_size, own_coefficients, 0)


def extend_rims(x_size, y_size, messages, state, coef):
    pitch = y_size + 2 * PAD
    planes = x_size + 2
    lanes = state.shape[-1]
    flat = state.reshape(state.shape[0] * pitch, lanes)
    coef_flat = coef.reshape(coef.shape[0] * pitch, lanes)
    for after, ref in zip(toward_next("blk"), messages):
        places = {d: jnp.where(after, PAD + y_size - 1 + d, PAD - d) for d in (1, 2, 3)}
        side = {}
        for k, (kind, i, distance) in enumerate(rim_entries()):
            value = ref[pl.ds(k * x_size, x_size), :]
            if kind == 0:
                pop = pick(after, i, mirrored(i, 1))
                at = (pop * planes + 1) * pitch + places[distance]
                flat[pl.ds(at, x_size, stride=pitch), :] = value
            else:
                side[(kind, i, distance)] = value
        for d in (1, 2):
            values = [side[key, n, d] for key, n in ((2, 0), (1, 0), (1, 1), (1, 2), (3, 0))]
            for n, value in enumerate(coefficients(*values)):
                coef_flat[pl.ds(n * x_size * pitch + places[d], x_size, stride=pitch), :] = value


def rim_kernel(x_size, y_size, *refs):
    sources, (b, a, state, coef, heat, radii), held, arrived = refs[:6], refs[6:12], refs[12:17], refs[17]
    messages = (a, b)
    copies = [pltpu.make_async_copy(a, b, arrived.at[n]) for n, (a, b) in enumerate(zip(sources, (*held, heat)))]
    for copy in copies:
        copy.start()
    for copy in copies:
        copy.wait()
    dual, vel, grad, fluid, span = held
    lanes = dual.shape[-1]
    flat = [ref.reshape(ref.shape[0] * y_size, lanes) for ref in (dual, vel, fluid, grad)]
    for after, out in zip(toward_next("blk"), messages):
        for k, (kind, i, distance) in enumerate(rim_entries()):
            row = jnp.where(after, y_size - distance, distance - 1)
            field = pick(after, mirrored(i, 1), i) if kind == 0 else i
            value = flat[kind][pl.ds(field * x_size * y_size + row, x_size, stride=y_size), :]
            if kind == 2:
                value = value.astype(jnp.float32) + 1.0
            out[pl.ds(k * x_size, x_size), :] = value
    extend_own(x_size, y_size, dual, vel, grad, fluid, state, coef)
    for x in range(x_size):
        radii[x] = span[x].astype(jnp.float32)


def edge_steps(x_size, after, state, coef, near, far, raw, first, second, put):
    known = RIGHT + LEVEL
    planes = x_size + 2
    inward = jnp.where(after, -1, 1)
    plane = jnp.where(after, x_size - 1, 0)
    turn = jnp.where(after, -1.0, 1.0)

    def coefs(x, at):
        return [coef[n * x_size + x, pl.ds(at, 8), :] for n in range(6)]

    def read_state(x, at):
        def read(i):
            cx, cy, _ = VELOCITIES[i]
            pop = pick(after, mirrored(i, 0), i)
            return state[pop * planes + x + 1 + cx * inward, pl.ds(at + cy, 8), :]

        return read

    for at in raw:
        for n, i in enumerate(RIGHT):
            pop = pick(after, mirrored(i, 0), i)
            put(0, n, at, state[pop * planes + plane + 1, pl.ds(at, 8), :])
    for at in first:
        keep, rate, *u, source = coefs(plane, at)
        for n, value in enumerate((rate, *u)):
            put(3, n, at, value)
        u[0] = turn * u[0]
        p = pulled_from(read_state(plane, at), known)
        _, equilib = relaxed(p, u)
        posts = posts_of(p, keep, equilib, rate, source, known)
        for n, i in enumerate(RIGHT):
            put(1, n, at, posts[i])
        for n, i in enumerate(LEVEL):
            near[n, pl.ds(at, 8), :] = posts[i]
        keep, rate, *u, source = coefs(plane + inward, at)
        u[0] = turn * u[0]
        p = pulled_from(read_state(plane + inward, at), range(POPS))
        _, equilib = relaxed(p, u)
        posts = posts_of(p, keep, equilib, rate, source, RIGHT)
        for n, i in enumerate(RIGHT):
            far[n, pl.ds(at, 8), :] = posts[i]
    for at in second:
        keep, rate, *u, source = coefs(plane, at)
        u[0] = turn * u[0]

        def read(i):
            ref, n = (far, RIGHT.index(i)) if i in RIGHT else (near, LEVEL.index(i))
            return ref[n, pl.ds(at + VELOCITIES[i][1], 8), :]

        p = pulled_from(read, known)
        _, equilib = relaxed(p, u)
        posts = posts_of(p, keep, equilib, rate, source, RIGHT)
        for n, i in enumerate(RIGHT):
            put(2, n, at, posts[i])


def early_pieces(y_size):
    pieces, offset = [], 0
    for count, margin in ((5, 0), (5, 1), (5, 2), (4, 0)):
        pieces.append((offset, margin))
        offset += count * (y_size - 2 * margin)
    return pieces, offset


def early_kernel(x_size, y_size, state, coef, span, early_b, early_a, near, far):
    rows = range(PAD, PAD + y_size, 8)
    pieces, radii = early_pieces(y_size)
    for after, out in zip(toward_next("grp"), (early_a, early_b)):

        def put(kind, n, at, value, out=out):
            offset, margin = pieces[kind]
            begin = max(at, PAD + margin)
            end = min(at + 8, PAD + y_size - margin)
            place = offset + n * (y_size - 2 * margin) + begin - PAD - margin
            out[pl.ds(place, end - begin), :] = value[begin - at : end - at]

        edge_steps(x_size, after, state, coef, near, far, rows, rows, rows, put)
        for k in range(REACH - 1):
            plane = jnp.where(after, x_size - 1 - k, k)
            out[pl.ds(radii + k * y_size, y_size), :] = span[plane]


def late_pieces(y_size):
    pieces, offset = {}, 0
    for end in (0, 1):
        for kind, count, reach in ((0, 5, 3), (1, 5, 2), (2, 5, 1), (3, 4, 2)):
            rows = 2 if kind == 3 else 3
            begin = PAD + y_size + reach - rows if end else PAD - reach
            pieces[kind, end] = (begin, rows, offset)
            offset += count * rows
    return pieces, -(-offset // 8) * 8


def late_kernel(x_size, y_size, _state, _coef, rim_b, rim_a, late_b, late_a, state, coef, near, far):
    extend_rims(x_size, y_size, (rim_a, rim_b), state, coef)
    pieces, _ = late_pieces(y_size)
    starts = [(PAD - reach, PAD + y_size + reach - 8) for reach in (3, 2, 1)]
    for after, out in zip(toward_next("grp"), (late_a, late_b)):

        def put(kind, n, at, value, out=out):
            begin, rows, offset = pieces[kind, 1 if at > PAD else 0]
            out[pl.ds(offset + n * rows, rows), :] = value[begin - at : begin - at + rows]

        edge_steps(x_size, after, state, coef, near, far, *starts, put)


def step_plane(x_size, y_size, number, x, source, target, coef, shifts):
    planes = x_size + 2
    for j in range((y_size + 8) // 8):
        at = FIRST + 8 * j
        keep, rate, *u, drive = [coef[n * x_size + x, pl.ds(at, 8), :] for n in range(6)]
        p = pulled_from(reader(planes, source, x, at), range(POPS))
        shift, equilib = relaxed(p, u)
        shifts[(number - 1) * x_size + x, pl.ds(at, 8), :] = shift
        posts = posts_of(p, keep, equilib, rate, drive, range(POPS))
        for i in range(POPS):
            target[i * planes + x + 1, pl.ds(at, 8), :] = posts[i]


def reader(planes, source, x, at):
    def read(i):
        cx, cy, _ = VELOCITIES[i]
        return source[i * planes + x + 1 + cx, pl.ds(at + cy, 8), :]

    return read


def sens_plane(x_size, y_size, x, state, coef, shifts, heat, sens):
    for j in range(y_size // 8):
        at = PAD + 8 * j
        u = [coef[n * x_size + x, pl.ds(at, 8), :] for n in (2, 3, 4)]
        p = pulled_from(reader(x_size + 2, state, x, at), range(1, POPS))
        shift = shifts[x, pl.ds(at, 8), :] + shifts[x_size + x, pl.ds(at, 8), :] + relaxed(p, u)[0]
        sens[x, pl.ds(8 * j, 8), :] = heat[x, pl.ds(8 * j, 8), :] * shift


def inner_kernel(x_size, y_size, state, coef, heat, state_1, state_2, shifts, sens):
    for x in range(1, x_size - 1):
        step_plane(x_size, y_size, 1, x, state, state_1, coef, shifts)
    for x in range(2, x_size - 2):
        step_plane(x_size, y_size, 2, x, state_1, state_2, coef, shifts)
    for x in range(3, x_size - 3):
        sens_plane(x_size, y_size, x, state_2, coef, shifts, heat, sens)


def outer_kernel(
    x_size, y_size, coef, heat, early_b, early_a, late_b, late_a, _state, _state_1, _state_2, _shifts, _sens,
    state, state_1, state_2, shifts, sens, extra, halos,
):
    planes = x_size + 2
    window = y_size + 8
    groups = window // 8
    afters = toward_next("grp")
    pieces, _ = late_pieces(y_size)

    for side, (after, early, late) in enumerate(zip(afters, (early_a, early_b), (late_a, late_b))):
        halo = jnp.where(after, x_size + 1, 0)
        for kind, count in enumerate((5, 5, 5, 4)):
            for n in range(count):
                if kind == 0:
                    ref, plane = state, pick(after, RIGHT[n], mirrored(RIGHT[n], 0)) * planes + halo
                else:
                    ref, plane = halos, side * 14 + 5 * kind - 5 + n
                offset, margin = early_pieces(y_size)[0][kind]
                rows = y_size - 2 * margin
                ref[plane, pl.ds(PAD + margin, rows), :] = early[pl.ds(offset + n * rows, rows), :]
                for end in (0, 1):
                    begin, rows, offset = pieces[kind, end]
                    ref[plane, pl.ds(begin, rows), :] = late[pl.ds(offset + n * rows, rows), :]

    for number, source, target in ((1, state, state_1), (2, state_1, state_2)):
        for x in (*range(number), *range(x_size - number, x_size)):
            step_plane(x_size, y_size, number, x, source, target, coef, shifts)
        for side, after in enumerate(afters):
            halo = jnp.where(after, x_size + 1, 0)
            edge = jnp.where(after, x_size, 1)
            turn = jnp.where(after, 1.0, -1.0)
            for j in range(groups):
                at = FIRST + 8 * j
                rate, *u = [halos[side * 14 + 10 + n, pl.ds(at, 8), :] for n in range(4)]
                u[0] = turn * u[0]

                def read(i):
                    cy = VELOCITIES[i][1]
                    if i in LEFT:
                        return source[pick(after, i, mirrored(i, 0)) * planes + edge, pl.ds(at + cy, 8), :]
                    return extra[side, pl.ds(at + cy, 8), :]

                p = pulled_from(read, LEFT if number == 1 else LEFT + LEVEL)
                added = rate * relaxed(p, u)[1]
                if number == 1:
                    extra[side, pl.ds(at, 8), :] = added
                for n, i in enumerate(RIGHT):
                    target[pick(after, i, mirrored(i, 0)) * planes + halo, pl.ds(at, 8), :] = (
                        halos[side * 14 + 5 * number - 5 + n, pl.ds(at, 8), :] + added
                    )
    for x in (*range(3), *range(x_size - 3, x_size)):
        sens_plane(x_size, y_size, x, state_2, coef, shifts, heat, sens)


def adjoint_kernel(x_size, y_size, state, coef, adjoint):
    planes = x_size + 2

    def plane(x, _):
        for j in range(y_size // 8):
            at = PAD + 8 * j
            keep, rate, *u, drive = [coef[n * x_size + x, pl.ds(at, 8), :] for n in range(6)]

            def read(i):
                cx, cy, _ = VELOCITIES[i]
                return state[i * planes + x + 1 + cx, pl.ds(at + cy, 8), :]

            p = pulled_from(read, range(POPS))
            posts = posts_of(p, keep, relaxed(p, u)[1], rate, drive, range(POPS))
            for i in range(POPS):
                adjoint[i * x_size + x, pl.ds(8 * j, 8), :] = posts[i]
        return 0

    lax.fori_loop(0, x_size, plane, 0, unroll=True)


def diamond(x_size, reach, slots, base=0):
    pieces, offset = [], base
    for slot in slots:
        for k in range(x_size if slot == 0 else min(x_size, reach - 1)):
            rows = reach if slot == 0 else reach - 1 - k
            pieces.append((slot, k, rows, offset))
            offset += rows
    return pieces, offset


def bands_of(x_size, slots):
    sens, offset = diamond(x_size, REACH, slots)
    radii, offset = diamond(x_size, REACH - 1, slots, offset)
    return sens, radii, -(-offset // 8) * 8


def slot_plane(x_size, slot, k):
    if slot == 0:
        return x_size + k, k
    after = toward_next("grp")[slot - 1]
    return jnp.where(after, 2 * x_size + k, x_size - 1 - k), jnp.where(after, k, x_size - 1 - k)


def own_band_kernel(x_size, y_size, own, span, band_b, band_a):
    sens, radii, _ = bands_of(x_size, (0,))
    for after, out in zip(toward_next("blk"), (band_a, band_b)):
        for ref, pieces in ((own, sens), (span, radii)):
            for _, k, rows, offset in pieces:
                out[pl.ds(offset, rows), :] = ref[k, pl.ds(jnp.where(after, y_size - rows, 0), rows), :]


def band_kernel(x_size, y_size, beside_b, beside_a, early_b, early_a, band_b, band_a):
    sens, radii, _ = bands_of(x_size, (1, 2))
    for after, out in zip(toward_next("blk"), (band_a, band_b)):
        for slot, k, rows, offset in sens:
            _, plane = slot_plane(x_size, slot, k)
            start = jnp.where(after, y_size - rows, 0)
            out[pl.ds(offset, rows), :] = (beside_a, beside_b)[slot - 1][plane, pl.ds(start, rows), :]
        for slot, k, rows, offset in radii:
            start = early_pieces(y_size)[1] + k * y_size + jnp.where(after, y_size - rows, 0)
            out[pl.ds(offset, rows), :] = (early_a, early_b)[slot - 1][pl.ds(start, rows), :]


def shares(span, inside):
    r2 = jnp.where(span < 0.5, 0.25, jnp.where(span < 1.5, 1.0, jnp.where(span < 2.5, 4.0, 16.0)))
    share = 1.0 / (1.0 + 6.0 * r2)
    return share, jnp.where(inside, r2 * share, 0.0)


def slot_inside(slot):
    if slot == 0:
        return True
    after = toward_next("grp")[slot - 1]
    me, size = lax.axis_index("grp"), lax.axis_size("grp")
    return jnp.where(after, me < size - 1, me > 0)


def radius_kernel(x_size, y_size, span, span_b, span_a, inverse, beta):
    for slot, ref in enumerate((span, span_a, span_b)):
        inside = slot_inside(slot)

        for x in range(x_size if slot == 0 else min(x_size, REACH - 1)):
            place, _ = slot_plane(x_size, slot, x)
            classes = ref[x] if slot == 0 else ref[pl.ds(early_pieces(y_size)[1] + x * y_size, y_size), :]
            inverse[place], beta[place] = shares(classes, inside)


def filter_kernel(
    x_size, y_size, own, beside_b, beside_a, own_b, own_a, band_b, band_a, inverse, own_beta, filtered, first, second, given, beta
):
    rows = y_size + 2 * REACH
    for x in range(x_size):
        for slot, ref in enumerate((own, beside_a, beside_b)):
            place, plane = slot_plane(x_size, slot, x)
            s = ref[plane]
            first[place, pl.ds(PAD + REACH, y_size), :] = s
            given[place, pl.ds(REACH, y_size), :] = s * inverse[place]
            beta[place, pl.ds(REACH, y_size), :] = own_beta[place]
    me, size = lax.axis_index("blk"), lax.axis_size("blk")
    for after, refs in zip(toward_next("blk"), ((own_a, band_a), (own_b, band_b))):
        there = jnp.where(after, me < size - 1, me > 0)
        for ref, slots in zip(refs, ((0,), (1, 2))):
            pieces, radii, _ = bands_of(x_size, slots)
            radii = {(slot, k): (count, offset) for slot, k, count, offset in radii}
            for slot, k, count, offset in pieces:
                place, _ = slot_plane(x_size, slot, k)
                at = jnp.where(after, REACH + y_size, REACH - count)
                first[place, pl.ds(PAD + at, count), :] = ref[pl.ds(offset, count), :]
                if (slot, k) in radii:
                    count, offset = radii[slot, k]
                    at = jnp.where(after, REACH + y_size, REACH - count)
                    inside = jnp.logical_and(there, slot_inside(slot))
                    share, beta[place, pl.ds(at, count), :] = shares(ref[pl.ds(offset, count), :], inside)
                    given[place, pl.ds(at, count), :] = first[place, pl.ds(PAD + at, count), :] * share
    source, target = first, second
    for number in range(1, SWEEPS + 1):
        final = number == SWEEPS
        margin = SWEEPS - number

        groups = -(-(y_size + 2 * margin) // 8)
        start = min(REACH - margin, rows - 8 * groups)
        for row in range(start, start + 8 * groups, 8):
            at = PAD + row
            begin, end = x_size - margin, 2 * x_size + margin
            column = {x: source[x, pl.ds(at, 8), :] for x in range(begin - 1, end + 1)}
            for x in range(begin, end):
                beside = column[x + 1] + column[x - 1]
                beside = beside + source[x, pl.ds(at + 1, 8), :] + source[x, pl.ds(at - 1, 8), :]
                beside = beside + lane_pull(column[x], 1) + lane_pull(column[x], -1)
                value = given[x, pl.ds(row, 8), :] + beta[x, pl.ds(row, 8), :] * beside
                if final:
                    filtered[x - x_size, pl.ds(row - REACH, 8), :] = value
                else:
                    target[x, pl.ds(at, 8), :] = value
        source, target = target, source


def call(kernel, outs, scratch, args, name, place=pltpu.VMEM, in_place=()):
    return pl.pallas_call(
        kernel,
        out_shape=[jax.ShapeDtypeStruct(shape, jnp.float32) for shape in outs],
        in_specs=[pl.BlockSpec(memory_space=place)] * len(args),
        out_specs=[pl.BlockSpec(memory_space=pltpu.VMEM)] * len(outs),
        scratch_shapes=[pltpu.VMEM(s, jnp.float32) if isinstance(s, tuple) else s for s in scratch],
        compiler_params=pltpu.CompilerParams(vmem_limit_bytes=32 * 1024 * 1024),
        input_output_aliases=dict(in_place),
        name=name,
    )(*args)


def swapped(axis, message_b, message_a):
    size = lax.axis_size(axis)
    received = []
    for begin, message in ((1, message_b), (0, message_a)):
        pairs = [(i, i + 1) for i in range(begin, size - 1, 2)]
        received.append(lax.ppermute(message, axis, pairs + [(j, i) for i, j in pairs]))
    return received


def on_device(dual_populace, forward_motion_vector, forward_heat_level, objective_heat_gradient, liquid_indicator,
              filter_span_group):
    _, x_size, y_size, lanes = dual_populace.shape
    planes, pitch = x_size + 2, y_size + 2 * PAD
    sizes = (x_size, y_size)
    dual = dual_populace.reshape(POPS * x_size, y_size, lanes)
    vel = forward_motion_vector.reshape(3 * x_size, y_size, lanes)
    fields = (dual, vel, objective_heat_gradient, liquid_indicator)
    rim = (len(rim_entries()) * x_size, lanes)
    state = (POPS * planes, pitch, lanes)
    coef = (6 * x_size, pitch, lanes)
    edge_scratch = [state, coef, (len(LEVEL), pitch, lanes), (len(RIGHT), pitch, lanes)]

    own = (x_size, y_size, lanes)
    fields = (*fields, filter_span_group, forward_heat_level)
    *rims, state_0, coefs, heat, span = call(
        functools.partial(rim_kernel, *sizes),
        [rim, rim, state, coef, own, own],
        [pltpu.VMEM(f.shape, f.dtype) for f in fields[:-1]] + [pltpu.SemaphoreType.DMA((len(fields),))],
        [pltpu.with_memory_space_constraint(f, pltpu.HBM) for f in fields],
        "rim_rows",
        pltpu.HBM,
    )
    rims = swapped("blk", *rims)
    early = (early_pieces(y_size)[1] + (REACH - 1) * y_size, lanes)
    near_far = [(len(LEVEL), pitch, lanes), (len(RIGHT), pitch, lanes)]
    earlies = call(
        functools.partial(early_kernel, *sizes),
        [early, early],
        near_far,
        (state_0, coefs, span),
        "edges_early",
    )
    earlies = swapped("grp", *earlies)
    late = (late_pieces(y_size)[1], lanes)
    *lates, state_0, coefs = call(
        functools.partial(late_kernel, *sizes),
        [late, late, state, coef],
        near_far,
        (state_0, coefs, *rims),
        "edges_late",
        in_place=((0, 2), (1, 3)),
    )
    lates = swapped("grp", *lates)
    shifts = (2 * x_size, pitch, lanes)
    inner = call(
        functools.partial(inner_kernel, *sizes),
        [state, state, shifts, own],
        [],
        (state_0, coefs, heat),
        "steps_inside",
    )
    _, _, state_2, _, sens = call(
        functools.partial(outer_kernel, *sizes),
        [state, state, state, shifts, own],
        [(2, pitch, lanes), (28, pitch, lanes)],
        (coefs, heat, *earlies, *lates, state_0, *inner),
        "steps_at_edges",
        in_place=((6, 0), (7, 1), (8, 2), (9, 3), (10, 4)),
    )
    spans = earlies
    beside = swapped("grp", sens, sens)
    band = (bands_of(x_size, (0,))[2], lanes)
    own_bands = call(functools.partial(own_band_kernel, *sizes), [band, band], [], (sens, span), "own_bands")
    own_bands = swapped("blk", *own_bands)
    band = (bands_of(x_size, (1, 2))[2], lanes)
    bands = call(functools.partial(band_kernel, *sizes), [band, band], [], (*beside, *spans), "bands")
    bands = swapped("blk", *bands)
    own_bands, state_2 = lax.optimization_barrier((own_bands, state_2))
    (adjoint,) = call(
        functools.partial(adjoint_kernel, *sizes), [(POPS * x_size, y_size, lanes)], [], (state_2, coefs), "third_step"
    )
    inverse, beta = call(
        functools.partial(radius_kernel, *sizes), [(3 * x_size, y_size, lanes)] * 2, [], (span, *spans), "radius"
    )
    wide, rows = 3 * x_size, y_size + 2 * REACH
    (filtered,) = call(
        functools.partial(filter_kernel, *sizes),
        [(x_size, y_size, lanes)],
        [(wide, rows + 2 * PAD, lanes)] * 2 + [(wide, rows, lanes)] * 2,
        (sens, *beside, *own_bands, *bands, inverse, beta),
        "eight_sweeps",
    )
    return adjoint.reshape(dual_populace.shape), filtered


def solution(mesh):
    in_specs = (
        P(None, "grp", "blk", None),
        P(None, "grp", "blk", None),
        P("grp", "blk", None),
        P("grp", "blk", None),
        P("grp", "blk", None),
        P("grp", "blk", None),
    )
    out_specs = (P(None, "grp", "blk", None), P("grp", "blk", None))
    return jax.shard_map(
        on_device, mesh=mesh, in_specs=in_specs, out_specs=out_specs, check_vma=False
    )
```

```python
import functools

import jax
import jax.numpy as jnp
from jax import lax
from jax.experimental import pallas as pl
from jax.experimental.pallas import tpu as pltpu
from jax.sharding import PartitionSpec as P

SWEEPS = 8
REACH = 8

VELOCITIES = (
    (0, 0, 0),
    (1, 0, 0),
    (-1, 0, 0),
    (0, 1, 0),
    (0, -1, 0),
    (0, 0, 1),
    (0, 0, -1),
    (1, 1, 0),
    (-1, -1, 0),
    (1, -1, 0),
    (-1, 1, 0),
    (1, 0, 1),
    (-1, 0, -1),
    (1, 0, -1),
    (-1, 0, 1),
    (0, 1, 1),
    (0, -1, -1),
    (0, 1, -1),
    (0, -1, 1),
)
POPS = 19
SHARE = 1.0 / 36.0
MULTIPLE = (12.0,) + (2.0,) * 6 + (1.0,) * 12
RIGHT = tuple(i for i in range(POPS) if VELOCITIES[i][0] == 1)
LEFT = tuple(i for i in range(POPS) if VELOCITIES[i][0] == -1)
LEVEL = tuple(i for i in range(POPS) if VELOCITIES[i][0] == 0)
PAD = 8
FIRST = 5


def rim_entries():
    entries = [(0, i, 1) for i in range(POPS)]
    entries += [(0, i, 2) for i in range(POPS) if VELOCITIES[i][1] != -1]
    entries += [(0, i, 3) for i in range(POPS) if VELOCITIES[i][1] == 1]
    for distance in (1, 2):
        entries += [(1, i, distance) for i in range(3)]
        entries += [(2, 0, distance), (3, 0, distance)]
    return entries


def mirrored(i, axis):
    velocity = list(VELOCITIES[i])
    velocity[axis] = -velocity[axis]
    return VELOCITIES.index(tuple(velocity))


def pick(condition, a, b):
    return a if a == b else jnp.where(condition, a, b)


def toward_next(axis):
    even = lax.axis_index(axis) % 2 == 0
    return even, jnp.logical_not(even)


def lane_pull(v, cz):
    if cz == 0:
        return v
    lanes = v.shape[-1]
    lane = lax.broadcasted_iota(jnp.int32, v.shape, 1)
    if cz == 1:
        return jnp.where(lane != lanes - 1, pltpu.roll(v, lanes - 1, 1), 0.0)
    return jnp.where(lane != 0, pltpu.roll(v, 1, 1), 0.0)


def total(terms):
    terms = [t for t in terms if t is not None]
    return functools.reduce(lambda a, b: a + b, terms) if terms else None


def scaled(v, factor):
    return None if v is None else factor * v


def negated(v):
    return None if v is None else -v


def moments(p):
    s, d = {}, {}
    for i in range(1, POPS, 2):
        a, b = p[i], p[i + 1]
        s[i] = total([a, b])
        d[i] = a - b if a is not None and b is not None else (a if b is None else negated(b))
    average = total(
        [scaled(p[0], 12.0), scaled(total([s[1], s[3], s[5]]), 2.0)] + [s[i] for i in (7, 9, 11, 13, 15, 17)]
    )
    along_x = total([scaled(d[1], 2.0), d[7], d[9], d[11], d[13]])
    along_y = total([scaled(d[3], 2.0), d[7], negated(d[9]), d[15], d[17]])
    along_z = total([scaled(d[5], 2.0), d[11], negated(d[13]), d[15], negated(d[17])])
    return average, (along_x, along_y, along_z)


def relaxed(p, u):
    average, along = moments(p)
    shift = total([u[k] * along[k] for k in range(3) if along[k] is not None])
    return shift, SHARE * average + shift


def pulled_from(read, pops):
    p = [None] * POPS
    for i in pops:
        p[i] = lane_pull(read(i), VELOCITIES[i][2])
    return p


def posts_of(p, keep, equilib, rate, source, pops):
    base = rate * equilib
    terms = {m: base + (source if m == 1.0 else m * source) for m in (12.0, 2.0, 1.0)}
    return {i: keep * p[i] + terms[MULTIPLE[i]] for i in pops}


def coefficients(there, ux, uy, uz, g):
    inside = there > 0.5
    wet = jnp.where(inside, there - 1.0, 0.0)
    keep = jnp.where(inside, 0.1 - 0.7 * wet, 0.0)
    rate = jnp.where(inside, 0.9 + 0.7 * wet, 0.0)
    scale = (3.0 * SHARE) * wet
    return keep, rate, scale * ux, scale * uy, scale * uz, SHARE * g


def extend_own(x_size, y_size, dual, vel, grad, fluid, state, coef):
    planes = x_size + 2

    def copy_own(i, _):
        for x in range(x_size):
            state[i * planes + x + 1, pl.ds(PAD, y_size), :] = dual[i * x_size + x]
        return 0

    lax.fori_loop(0, POPS, copy_own, 0)

    def own_coefficients(x, _):
        there = fluid[x].astype(jnp.float32) + 1.0
        values = coefficients(there, vel[x], vel[x_size + x], vel[2 * x_size + x], grad[x])
        for n, value in enumerate(values):
            coef[n * x_size + x, pl.ds(PAD, y_size), :] = value
        return 0

    lax.fori_loop(0, x_size, own_coefficients, 0)


def extend_rims(x_size, y_size, messages, state, coef):
    pitch = y_size + 2 * PAD
    planes = x_size + 2
    lanes = state.shape[-1]
    flat = state.reshape(state.shape[0] * pitch, lanes)
    coef_flat = coef.reshape(coef.shape[0] * pitch, lanes)
    for after, ref in zip(toward_next("blk"), messages):
        places = {d: jnp.where(after, PAD + y_size - 1 + d, PAD - d) for d in (1, 2, 3)}
        side = {}
        for k, (kind, i, distance) in enumerate(rim_entries()):
            value = ref[pl.ds(k * x_size, x_size), :]
            if kind == 0:
                pop = pick(after, i, mirrored(i, 1))
                at = (pop * planes + 1) * pitch + places[distance]
                flat[pl.ds(at, x_size, stride=pitch), :] = value
            else:
                side[(kind, i, distance)] = value
        for d in (1, 2):
            values = [side[key, n, d] for key, n in ((2, 0), (1, 0), (1, 1), (1, 2), (3, 0))]
            for n, value in enumerate(coefficients(*values)):
                coef_flat[pl.ds(n * x_size * pitch + places[d], x_size, stride=pitch), :] = value


def rim_kernel(x_size, y_size, *refs):
    sources, (b, a, state, coef, heat, radii), held, arrived = refs[:6], refs[6:12], refs[12:17], refs[17]
    messages = (a, b)
    copies = [pltpu.make_async_copy(a, b, arrived.at[n]) for n, (a, b) in enumerate(zip(sources, (*held, heat)))]
    for copy in copies:
        copy.start()
    for copy in copies:
        copy.wait()
    dual, vel, grad, fluid, span = held
    lanes = dual.shape[-1]
    flat = [ref.reshape(ref.shape[0] * y_size, lanes) for ref in (dual, vel, fluid, grad)]
    for after, out in zip(toward_next("blk"), messages):
        for k, (kind, i, distance) in enumerate(rim_entries()):
            row = jnp.where(after, y_size - distance, distance - 1)
            field = pick(after, mirrored(i, 1), i) if kind == 0 else i
            value = flat[kind][pl.ds(field * x_size * y_size + row, x_size, stride=y_size), :]
            if kind == 2:
                value = value.astype(jnp.float32) + 1.0
            out[pl.ds(k * x_size, x_size), :] = value
    extend_own(x_size, y_size, dual, vel, grad, fluid, state, coef)
    for x in range(x_size):
        radii[x] = span[x].astype(jnp.float32)


def edge_steps(x_size, after, state, coef, near, far, raw, first, second, put):
    known = RIGHT + LEVEL
    planes = x_size + 2
    inward = jnp.where(after, -1, 1)
    plane = jnp.where(after, x_size - 1, 0)
    turn = jnp.where(after, -1.0, 1.0)

    def coefs(x, at):
        return [coef[n * x_size + x, pl.ds(at, 8), :] for n in range(6)]

    def read_state(x, at):
        def read(i):
            cx, cy, _ = VELOCITIES[i]
            pop = pick(after, mirrored(i, 0), i)
            return state[pop * planes + x + 1 + cx * inward, pl.ds(at + cy, 8), :]

        return read

    for at in raw:
        for n, i in enumerate(RIGHT):
            pop = pick(after, mirrored(i, 0), i)
            put(0, n, at, state[pop * planes + plane + 1, pl.ds(at, 8), :])
    for at in first:
        keep, rate, *u, source = coefs(plane, at)
        for n, value in enumerate((rate, *u)):
            put(3, n, at, value)
        u[0] = turn * u[0]
        p = pulled_from(read_state(plane, at), known)
        _, equilib = relaxed(p, u)
        posts = posts_of(p, keep, equilib, rate, source, known)
        for n, i in enumerate(RIGHT):
            put(1, n, at, posts[i])
        for n, i in enumerate(LEVEL):
            near[n, pl.ds(at, 8), :] = posts[i]
        keep, rate, *u, source = coefs(plane + inward, at)
        u[0] = turn * u[0]
        p = pulled_from(read_state(plane + inward, at), range(POPS))
        _, equilib = relaxed(p, u)
        posts = posts_of(p, keep, equilib, rate, source, RIGHT)
        for n, i in enumerate(RIGHT):
            far[n, pl.ds(at, 8), :] = posts[i]
    for at in second:
        keep, rate, *u, source = coefs(plane, at)
        u[0] = turn * u[0]

        def read(i):
            ref, n = (far, RIGHT.index(i)) if i in RIGHT else (near, LEVEL.index(i))
            return ref[n, pl.ds(at + VELOCITIES[i][1], 8), :]

        p = pulled_from(read, known)
        _, equilib = relaxed(p, u)
        posts = posts_of(p, keep, equilib, rate, source, RIGHT)
        for n, i in enumerate(RIGHT):
            put(2, n, at, posts[i])


def early_pieces(y_size):
    pieces, offset = [], 0
    for count, margin in ((5, 0), (5, 1), (5, 2), (4, 0)):
        pieces.append((offset, margin))
        offset += count * (y_size - 2 * margin)
    return pieces, offset


def early_kernel(x_size, y_size, state, coef, span, early_b, early_a, near, far):
    rows = range(PAD, PAD + y_size, 8)
    pieces, radii = early_pieces(y_size)
    for after, out in zip(toward_next("grp"), (early_a, early_b)):

        def put(kind, n, at, value, out=out):
            offset, margin = pieces[kind]
            begin = max(at, PAD + margin)
            end = min(at + 8, PAD + y_size - margin)
            place = offset + n * (y_size - 2 * margin) + begin - PAD - margin
            out[pl.ds(place, end - begin), :] = value[begin - at : end - at]

        edge_steps(x_size, after, state, coef, near, far, rows, rows, rows, put)
        for k in range(REACH - 1):
            plane = jnp.where(after, x_size - 1 - k, k)
            out[pl.ds(radii + k * y_size, y_size), :] = span[plane]


def late_pieces(y_size):
    pieces, offset = {}, 0
    for end in (0, 1):
        for kind, count, reach in ((0, 5, 3), (1, 5, 2), (2, 5, 1), (3, 4, 2)):
            rows = 2 if kind == 3 else 3
            begin = PAD + y_size + reach - rows if end else PAD - reach
            pieces[kind, end] = (begin, rows, offset)
            offset += count * rows
    return pieces, -(-offset // 8) * 8


def late_kernel(x_size, y_size, _state, _coef, rim_b, rim_a, late_b, late_a, state, coef, near, far):
    extend_rims(x_size, y_size, (rim_a, rim_b), state, coef)
    pieces, _ = late_pieces(y_size)
    starts = [(PAD - reach, PAD + y_size + reach - 8) for reach in (3, 2, 1)]
    for after, out in zip(toward_next("grp"), (late_a, late_b)):

        def put(kind, n, at, value, out=out):
            begin, rows, offset = pieces[kind, 1 if at > PAD else 0]
            out[pl.ds(offset + n * rows, rows), :] = value[begin - at : begin - at + rows]

        edge_steps(x_size, after, state, coef, near, far, *starts, put)


def step_plane(x_size, y_size, number, x, source, target, coef, shifts):
    planes = x_size + 2
    for j in range((y_size + 8) // 8):
        at = FIRST + 8 * j
        keep, rate, *u, drive = [coef[n * x_size + x, pl.ds(at, 8), :] for n in range(6)]
        p = pulled_from(reader(planes, source, x, at), range(POPS))
        shift, equilib = relaxed(p, u)
        shifts[(number - 1) * x_size + x, pl.ds(at, 8), :] = shift
        posts = posts_of(p, keep, equilib, rate, drive, range(POPS))
        for i in range(POPS):
            target[i * planes + x + 1, pl.ds(at, 8), :] = posts[i]


def reader(planes, source, x, at):
    def read(i):
        cx, cy, _ = VELOCITIES[i]
        return source[i * planes + x + 1 + cx, pl.ds(at + cy, 8), :]

    return read


def sens_plane(x_size, y_size, x, state, coef, shifts, heat, sens):
    for j in range(y_size // 8):
        at = PAD + 8 * j
        u = [coef[n * x_size + x, pl.ds(at, 8), :] for n in (2, 3, 4)]
        p = pulled_from(reader(x_size + 2, state, x, at), range(1, POPS))
        shift = shifts[x, pl.ds(at, 8), :] + shifts[x_size + x, pl.ds(at, 8), :] + relaxed(p, u)[0]
        sens[x, pl.ds(8 * j, 8), :] = heat[x, pl.ds(8 * j, 8), :] * shift


def inner_kernel(x_size, y_size, state, coef, heat, state_1, state_2, shifts, sens):
    for x in range(1, x_size - 1):
        step_plane(x_size, y_size, 1, x, state, state_1, coef, shifts)
    for x in range(2, x_size - 2):
        step_plane(x_size, y_size, 2, x, state_1, state_2, coef, shifts)
    for x in range(3, x_size - 3):
        sens_plane(x_size, y_size, x, state_2, coef, shifts, heat, sens)


def outer_kernel(
    x_size, y_size, coef, heat, early_b, early_a, late_b, late_a, _state, _state_1, _state_2, _shifts, _sens,
    state, state_1, state_2, shifts, sens, extra, halos,
):
    planes = x_size + 2
    window = y_size + 8
    groups = window // 8
    afters = toward_next("grp")
    pieces, _ = late_pieces(y_size)

    for side, (after, early, late) in enumerate(zip(afters, (early_a, early_b), (late_a, late_b))):
        halo = jnp.where(after, x_size + 1, 0)
        for kind, count in enumerate((5, 5, 5, 4)):
            for n in range(count):
                if kind == 0:
                    ref, plane = state, pick(after, RIGHT[n], mirrored(RIGHT[n], 0)) * planes + halo
                else:
                    ref, plane = halos, side * 14 + 5 * kind - 5 + n
                offset, margin = early_pieces(y_size)[0][kind]
                rows = y_size - 2 * margin
                ref[plane, pl.ds(PAD + margin, rows), :] = early[pl.ds(offset + n * rows, rows), :]
                for end in (0, 1):
                    begin, rows, offset = pieces[kind, end]
                    ref[plane, pl.ds(begin, rows), :] = late[pl.ds(offset + n * rows, rows), :]

    for number, source, target in ((1, state, state_1), (2, state_1, state_2)):
        for x in (*range(number), *range(x_size - number, x_size)):
            step_plane(x_size, y_size, number, x, source, target, coef, shifts)
        for side, after in enumerate(afters):
            halo = jnp.where(after, x_size + 1, 0)
            edge = jnp.where(after, x_size, 1)
            turn = jnp.where(after, 1.0, -1.0)
            for j in range(groups):
                at = FIRST + 8 * j
                rate, *u = [halos[side * 14 + 10 + n, pl.ds(at, 8), :] for n in range(4)]
                u[0] = turn * u[0]

                def read(i):
                    cy = VELOCITIES[i][1]
                    if i in LEFT:
                        return source[pick(after, i, mirrored(i, 0)) * planes + edge, pl.ds(at + cy, 8), :]
                    return extra[side, pl.ds(at + cy, 8), :]

                p = pulled_from(read, LEFT if number == 1 else LEFT + LEVEL)
                added = rate * relaxed(p, u)[1]
                if number == 1:
                    extra[side, pl.ds(at, 8), :] = added
                for n, i in enumerate(RIGHT):
                    target[pick(after, i, mirrored(i, 0)) * planes + halo, pl.ds(at, 8), :] = (
                        halos[side * 14 + 5 * number - 5 + n, pl.ds(at, 8), :] + added
                    )
    for x in (*range(3), *range(x_size - 3, x_size)):
        sens_plane(x_size, y_size, x, state_2, coef, shifts, heat, sens)


def adjoint_kernel(x_size, y_size, state, coef, adjoint):
    planes = x_size + 2

    def plane(x, _):
        for j in range(y_size // 8):
            at = PAD + 8 * j
            keep, rate, *u, drive = [coef[n * x_size + x, pl.ds(at, 8), :] for n in range(6)]

            def read(i):
                cx, cy, _ = VELOCITIES[i]
                return state[i * planes + x + 1 + cx, pl.ds(at + cy, 8), :]

            p = pulled_from(read, range(POPS))
            posts = posts_of(p, keep, relaxed(p, u)[1], rate, drive, range(POPS))
            for i in range(POPS):
                adjoint[i * x_size + x, pl.ds(8 * j, 8), :] = posts[i]
        return 0

    lax.fori_loop(0, x_size, plane, 0, unroll=True)


def diamond(x_size, reach):
    pieces, offset = [], 0
    for slot in range(3):
        for k in range(x_size if slot == 0 else min(x_size, reach - 1)):
            rows = reach if slot == 0 else reach - 1 - k
            pieces.append((slot, k, rows, offset))
            offset += rows
    return pieces, -(-offset // 8) * 8


def slot_plane(x_size, slot, k):
    if slot == 0:
        return x_size + k, k
    after = toward_next("grp")[slot - 1]
    return jnp.where(after, 2 * x_size + k, x_size - 1 - k), jnp.where(after, k, x_size - 1 - k)


def band_kernel(x_size, y_size, own, beside_a, beside_b, span, span_b, span_a, band_b, band_a):
    pieces, skip = diamond(x_size, REACH)
    for after, out in zip(toward_next("blk"), (band_a, band_b)):
        for refs, reach, base in (((own, beside_a, beside_b), REACH, 0), ((span, span_a, span_b), REACH - 1, skip)):
            for slot, k, rows, offset in diamond(x_size, reach)[0]:
                _, plane = slot_plane(x_size, slot, k)
                start = jnp.where(after, y_size - rows, 0)
                if slot > 0 and base > 0:
                    value = refs[slot][pl.ds(early_pieces(y_size)[1] + k * y_size + start, rows), :]
                else:
                    value = refs[slot][plane, pl.ds(start, rows), :]
                out[pl.ds(base + offset, rows), :] = value


def shares(span, inside):
    r2 = jnp.where(span < 0.5, 0.25, jnp.where(span < 1.5, 1.0, jnp.where(span < 2.5, 4.0, 16.0)))
    share = 1.0 / (1.0 + 6.0 * r2)
    return share, jnp.where(inside, r2 * share, 0.0)


def slot_inside(slot):
    if slot == 0:
        return True
    after = toward_next("grp")[slot - 1]
    me, size = lax.axis_index("grp"), lax.axis_size("grp")
    return jnp.where(after, me < size - 1, me > 0)


def sweep(x_size, number, row, source, given, beta, put):
    margin = SWEEPS - number
    begin, end = x_size - margin, 2 * x_size + margin
    column = {x: source(x, row) for x in range(begin - 1, end + 1)}
    for x in range(begin, end):
        beside = column[x + 1] + column[x - 1]
        beside = beside + source(x, row + 1) + source(x, row - 1)
        beside = beside + lane_pull(column[x], 1) + lane_pull(column[x], -1)
        place = pl.ds(REACH + row, 8)
        put(x, row, given[x, place, :] + beta[x, place, :] * beside)


def level_access(x_size, levels, number):
    def read(x, row):
        return levels[number * 3 * x_size + x, pl.ds(PAD + REACH + row, 8), :]

    def write(x, row, value):
        levels[number * 3 * x_size + x, pl.ds(PAD + REACH + row, 8), :] = value

    return read, write


def inner_sweeps_kernel(
    x_size, y_size, beside_b, beside_a, own, span, span_b, span_a, levels, given, beta
):
    for slot, (classes, sens) in enumerate(((span, own), (span_a, beside_a), (span_b, beside_b))):
        inside = slot_inside(slot)
        for k in range(x_size):
            place, plane = slot_plane(x_size, slot, k)
            s = sens[plane]
            levels[place, pl.ds(PAD + REACH, y_size), :] = s
            if slot == 0 or k < REACH - 1:
                c = classes[k] if slot == 0 else classes[pl.ds(early_pieces(y_size)[1] + k * y_size, y_size), :]
                share, beta[place, pl.ds(REACH, y_size), :] = shares(c, inside)
                given[place, pl.ds(REACH, y_size), :] = s * share
    for number in range(1, SWEEPS):
        source, _ = level_access(x_size, levels, number - 1)
        _, put = level_access(x_size, levels, number)
        for row in range(number, y_size - number, 8):
            sweep(x_size, number, row, source, given, beta, put)


def outer_sweeps_kernel(
    x_size, y_size, band_b, band_a, _levels, _given, _beta, filtered, levels, given, beta
):
    pieces, skip = diamond(x_size, REACH)
    radii = {(slot, k): (rows, skip + offset) for slot, k, rows, offset in diamond(x_size, REACH - 1)[0]}
    me, size = lax.axis_index("blk"), lax.axis_size("blk")
    for after, ref in zip(toward_next("blk"), (band_a, band_b)):
        there = jnp.where(after, me < size - 1, me > 0)
        for slot, k, count, offset in pieces:
            place, _ = slot_plane(x_size, slot, k)
            at = jnp.where(after, REACH + y_size, REACH - count)
            levels[place, pl.ds(PAD + at, count), :] = ref[pl.ds(offset, count), :]
            if (slot, k) in radii:
                rows, base = radii[slot, k]
                at = jnp.where(after, REACH + y_size, REACH - rows)
                inside = jnp.logical_and(there, slot_inside(slot))
                first = offset + jnp.where(after, 0, count - rows)
                share, beta[place, pl.ds(at, rows), :] = shares(ref[pl.ds(base, rows), :], inside)
                given[place, pl.ds(at, rows), :] = ref[pl.ds(first, rows), :] * share

    def put_out(x, row, value):
        filtered[x - x_size, pl.ds(row, 8), :] = value

    for number in range(1, SWEEPS + 1):
        source, _ = level_access(x_size, levels, number - 1)
        put = level_access(x_size, levels, number)[1] if number < SWEEPS else put_out
        for row in (number - SWEEPS, y_size - number):
            sweep(x_size, number, row, source, given, beta, put)


def call(kernel, outs, scratch, args, name, place=pltpu.VMEM, in_place=()):
    return pl.pallas_call(
        kernel,
        out_shape=[jax.ShapeDtypeStruct(shape, jnp.float32) for shape in outs],
        in_specs=[pl.BlockSpec(memory_space=place)] * len(args),
        out_specs=[pl.BlockSpec(memory_space=pltpu.VMEM)] * len(outs),
        scratch_shapes=[pltpu.VMEM(s, jnp.float32) if isinstance(s, tuple) else s for s in scratch],
        compiler_params=pltpu.CompilerParams(vmem_limit_bytes=32 * 1024 * 1024),
        input_output_aliases=dict(in_place),
        name=name,
    )(*args)


def swapped(axis, message_b, message_a):
    size = lax.axis_size(axis)
    received = []
    for begin, message in ((1, message_b), (0, message_a)):
        pairs = [(i, i + 1) for i in range(begin, size - 1, 2)]
        received.append(lax.ppermute(message, axis, pairs + [(j, i) for i, j in pairs]))
    return received


def on_device(dual_populace, forward_motion_vector, forward_heat_level, objective_heat_gradient, liquid_indicator,
              filter_span_group):
    _, x_size, y_size, lanes = dual_populace.shape
    assert x_size >= REACH and y_size == 2 * REACH
    planes, pitch = x_size + 2, y_size + 2 * PAD
    sizes = (x_size, y_size)
    dual = dual_populace.reshape(POPS * x_size, y_size, lanes)
    vel = forward_motion_vector.reshape(3 * x_size, y_size, lanes)
    fields = (dual, vel, objective_heat_gradient, liquid_indicator)
    rim = (len(rim_entries()) * x_size, lanes)
    state = (POPS * planes, pitch, lanes)
    coef = (6 * x_size, pitch, lanes)
    edge_scratch = [state, coef, (len(LEVEL), pitch, lanes), (len(RIGHT), pitch, lanes)]

    own = (x_size, y_size, lanes)
    fields = (*fields, filter_span_group, forward_heat_level)
    *rims, state_0, coefs, heat, span = call(
        functools.partial(rim_kernel, *sizes),
        [rim, rim, state, coef, own, own],
        [pltpu.VMEM(f.shape, f.dtype) for f in fields[:-1]] + [pltpu.SemaphoreType.DMA((len(fields),))],
        [pltpu.with_memory_space_constraint(f, pltpu.HBM) for f in fields],
        "rim_rows",
        pltpu.HBM,
    )
    rims = swapped("blk", *rims)
    early = (early_pieces(y_size)[1] + (REACH - 1) * y_size, lanes)
    near_far = [(len(LEVEL), pitch, lanes), (len(RIGHT), pitch, lanes)]
    earlies = call(
        functools.partial(early_kernel, *sizes),
        [early, early],
        near_far,
        (state_0, coefs, span),
        "edges_early",
    )
    earlies = swapped("grp", *earlies)
    late = (late_pieces(y_size)[1], lanes)
    *lates, state_0, coefs = call(
        functools.partial(late_kernel, *sizes),
        [late, late, state, coef],
        near_far,
        (state_0, coefs, *rims),
        "edges_late",
        in_place=((0, 2), (1, 3)),
    )
    lates = swapped("grp", *lates)
    shifts = (2 * x_size, pitch, lanes)
    inner = call(
        functools.partial(inner_kernel, *sizes),
        [state, state, shifts, own],
        [],
        (state_0, coefs, heat),
        "steps_inside",
    )
    _, _, state_2, _, sens = call(
        functools.partial(outer_kernel, *sizes),
        [state, state, state, shifts, own],
        [(2, pitch, lanes), (28, pitch, lanes)],
        (coefs, heat, *earlies, *lates, state_0, *inner),
        "steps_at_edges",
        in_place=((6, 0), (7, 1), (8, 2), (9, 3), (10, 4)),
    )
    spans = earlies
    beside = swapped("grp", sens, sens)
    (adjoint,) = call(
        functools.partial(adjoint_kernel, *sizes), [(POPS * x_size, y_size, lanes)], [], (state_2, coefs), "third_step"
    )
    band = (diamond(x_size, REACH)[1] + diamond(x_size, REACH - 1)[1], lanes)
    bands = call(
        functools.partial(band_kernel, *sizes), [band, band], [], (sens, *beside[::-1], span, *spans), "bands"
    )
    bands = swapped("blk", *bands)
    wide, rows = 3 * x_size, y_size + 2 * REACH
    smooth = [(SWEEPS * wide, rows + 2 * PAD, lanes), (wide, rows, lanes), (wide, rows, lanes)]
    inner = call(
        functools.partial(inner_sweeps_kernel, *sizes), smooth, [], (*beside, sens, span, *spans), "sweeps_inside"
    )
    filtered, *_ = call(
        functools.partial(outer_sweeps_kernel, *sizes),
        [own, *smooth],
        [],
        (*bands, *inner),
        "sweeps_at_ends",
        in_place=((2, 1), (3, 2), (4, 3)),
    )
    return adjoint.reshape(dual_populace.shape), filtered


def solution(mesh):
    in_specs = (
        P(None, "grp", "blk", None),
        P(None, "grp", "blk", None),
        P("grp", "blk", None),
        P("grp", "blk", None),
        P("grp", "blk", None),
        P("grp", "blk", None),
    )
    out_specs = (P(None, "grp", "blk", None), P("grp", "blk", None))
    return jax.shard_map(
        on_device, mesh=mesh, in_specs=in_specs, out_specs=out_specs, check_vma=False
    )
```
